32 devices in a mesh: section: 2 (over core), dp: 4 (over z), seq: 4 (over y, x).
Axes of the slice: x: 2, y: 2, z: 4, core: 2. Of those that a mesh axis runs over, the one named last changes fastest.
Arguments:
- inputs: bfloat16 [2, 4, 1024, 1024], P('section', 'dp', 'seq'), may hold values from -6 to 6
- cotangent: bfloat16 [2, 4, 1024, 1024], P('section', 'dp', 'seq'), may hold values from -6 to 6
- norm_gain: float32 [1024], replicated, may hold values from 0.5 to 1.5
- first_pack: bfloat16 [2, 1024, 4096], P('section'), as said below
- second_pack: bfloat16 [2, 1024, 4096], P('section'), as said below
- w_z: bfloat16 [1024, 128], replicated, may hold values from -0.1875 to 0.1875
- qk_affine: float32 [4, 128], replicated, may hold values from -9 to 9
- ema_params: float32 [4, 1024, 16], replicated, may hold values from -16 to 8, as said below
- omega: float32 [1024], replicated, may hold values from -6 to 6
- ffn_gain: float32 [1024], replicated, may hold values from 0.5 to 1.5
Outputs:
- block_output: float32 [2, 4, 1024, 1024], P('section', 'dp', 'seq')
- input_grad: float32 [2, 4, 1024, 1024], P('section', 'dp', 'seq')
- norm_gain_grad: float32 [1024], replicated
- first_pack_grad: float32 [2, 1024, 4096], P('section', 'seq')
- second_pack_grad: float32 [2, 1024, 4096], P('section', 'seq')
- w_z_grad: float32 [1024, 128], replicated
- qk_affine_grad: float32 [4, 128], replicated
- ema_params_grad: float32 [4, 1024, 16], replicated
- omega_grad: float32 [1024], replicated
- ffn_gain_grad: float32 [1024], replicated
The draws below stay inside these ranges and needn't reach their ends.
Inputs may be any that keep to these rules, and one draw needn't show every extreme that they name: ema_params[0] and [1] are raw values whose sigmoids give the rate and damping; rows 2 and 3 are finite. `first_pack`: finite projection entries. `second_pack`: finite projection entries.
All inputs are finite; a program needn't handle non-finite values.
Results may differ from the reference program's by a relative error of at most 0.015.
Values may be sent and summed in bfloat16 or wider, within the bound.
A program may use at most 384 MiB of HBM per device.

```python
import jax
import jax.numpy as jnp
from jax import lax

D = 1024
QUERY_KEY_WIDTH = 128
VALUE_WIDTH = 2048
NDIM = 16
FF = 4096
BLOCK_POSITIONS = 128
MB = 2
LEN = 1024
BATCH = 4
TOKENS = 8192


def draw_ema_params(key, part):
    key = jax.random.fold_in(key, 7)
    subkeys = jax.random.split(key, 6)
    grid_shape = (D, NDIM)
    slow_share = 0.5
    slow_mask = jax.random.uniform(subkeys[0], grid_shape) < slow_share
    slow_rate = jnp.exp(jax.random.uniform(subkeys[1], grid_shape, minval=jnp.log(0.2 / LEN), maxval=jnp.log(2.0 / LEN)))
    fast_rate = jnp.exp(jax.random.uniform(subkeys[2], grid_shape, minval=jnp.log(0.02), maxval=jnp.log(0.04)))
    rate_all = jnp.where(slow_mask, slow_rate, fast_rate)
    alpha_rate = jax.random.uniform(subkeys[3], grid_shape, minval=0.3, maxval=0.9)
    damping = rate_all / alpha_rate
    expand = jax.random.normal(subkeys[4], grid_shape) * jnp.sqrt(2.0 * rate_all) / alpha_rate
    project = jax.random.normal(subkeys[5], grid_shape) * 0.25
    alpha_raw = jnp.log(alpha_rate / (1.0 - alpha_rate))
    damp_raw = jnp.log(damping / (1.0 - damping))
    return jnp.stack([alpha_raw, damp_raw, expand, project]).astype(jnp.float32)


def draw_first_pack(key, part):
    key = jax.random.fold_in(key, 11)
    raw = jnp.clip(jax.random.normal(key, (2, D, FF)), -6.0, 6.0)
    columns = jnp.arange(FF)[None, :]
    mega_scale = jnp.where(columns < VALUE_WIDTH, D ** (-0.5), (VALUE_WIDTH // 8) ** (-0.5))
    ffn_scale = jnp.full((1, FF), D ** (-0.5))
    scales = jnp.stack([mega_scale, ffn_scale])
    return (raw * scales).astype(jnp.bfloat16)


def draw_second_pack(key, part):
    key = jax.random.fold_in(key, 13)
    raw = jnp.clip(jax.random.normal(key, (2, D, FF)), -6.0, 6.0)
    scales = jnp.array([D ** (-0.5), FF ** (-0.5)], jnp.float32)[:, None, None]
    return (raw * scales).astype(jnp.bfloat16)


def block_scale(key, dims, shards, smallest, top_value):
    level, own = 1.0, jax.random.fold_in(key, 6)
    for dim, blocks in shards:
        heights = jnp.exp(jax.random.uniform(jax.random.fold_in(own, dim), (blocks,), jnp.float32, smallest / len(shards), top_value / len(shards)))
        level = level * jnp.repeat(heights, dims[dim] // blocks).reshape([-1 if axis == dim else 1 for axis in range(len(dims))])
    return level


def bell_draw(key, shape, scale, most, cuts=(), held_as=jnp.bfloat16):
    level = block_scale(key, shape, cuts, -0.22, 0.18) if cuts else 1.0
    values = jax.random.normal(key, shape, jnp.float32) * scale * level
    return jnp.minimum(jnp.maximum(values, -most), most).astype(held_as)


def setup_inputs(seed: int = 0) -> dict:
    key_list = jax.random.split(jax.random.key(seed), 11)
    inputs = bell_draw(key_list[0], (MB, BATCH, LEN, D), 1.0, 6.0, ((0, 2), (1, 4), (2, 4)))
    cotangent = bell_draw(key_list[1], (MB, BATCH, LEN, D), 1.0, 6.0, ((0, 2), (1, 4), (2, 4)))
    norm_gain = jnp.clip(1.0 + 0.1 * jax.random.normal(key_list[2], (D,), jnp.float32), 0.5, 1.5)
    first_pack = draw_first_pack(jax.random.fold_in(key_list[10], 71), 0)
    second_pack = draw_second_pack(jax.random.fold_in(key_list[10], 71), 0)
    w_z = bell_draw(key_list[5], (D, QUERY_KEY_WIDTH), D ** -0.5, 0.1875)
    qk_affine = bell_draw(key_list[6], (4, QUERY_KEY_WIDTH), 1.5, 9.0, (), jnp.float32)
    ema_params = draw_ema_params(jax.random.fold_in(key_list[10], 71), 0)
    omega = bell_draw(key_list[8], (D,), 1.0, 6.0, (), jnp.float32)
    ffn_gain = jnp.clip(1.0 + 0.1 * jax.random.normal(key_list[9], (D,), jnp.float32), 0.5, 1.5)
    return dict(inputs=inputs, cotangent=cotangent, norm_gain=norm_gain, first_pack=first_pack, second_pack=second_pack, w_z=w_z, qk_affine=qk_affine, ema_params=ema_params, omega=omega, ffn_gain=ffn_gain)


@jax.custom_vjp
def low(v):
    return lax.optimization_barrier(v.astype(jnp.bfloat16)).astype(jnp.float32)

@jax.custom_vjp
def low_back(v):
    return v

def low_keep(v):
    return (low(v), None)

def low_pass(kept, grad):
    return (grad,)

def back_keep(v):
    return (v, None)

def back_low(kept, grad):
    return (low(grad),)
low.defvjp(low_keep, low_pass)
low_back.defvjp(back_keep, back_low)
EPSILON = 1e-05
DECAY = 0.01
HIGH_PRECISION = lax.Precision.HIGHEST

def product(left, right):
    return jnp.dot(left, right, precision=HIGH_PRECISION, preferred_element_type=jnp.float32)

def layer_norm(values, gain):
    center = values - lax.optimization_barrier(jnp.mean(values, axis=-1, keepdims=True))
    spread = lax.optimization_barrier(jnp.mean(center * center, axis=-1, keepdims=True))
    return center * lax.rsqrt(spread + EPSILON) * gain

def ema_smooth(normed, ema_params):
    alpha_rate = jax.nn.sigmoid(ema_params[0])
    damping = jax.nn.sigmoid(ema_params[1])
    decay_rate = 1.0 - alpha_rate * damping
    log_decay = jnp.log(decay_rate)
    inject = alpha_rate * ema_params[2]
    steps = jnp.arange(BLOCK_POSITIONS, dtype=jnp.float32)[:, None, None]
    grow = jnp.exp(-steps * log_decay)
    shrink = jnp.exp(steps * log_decay)

    def block_step(carried, block_rows):
        weighted = block_rows[:, :, None] * inject * grow
        states = shrink * jnp.cumsum(weighted, axis=0) + shrink * decay_rate * carried
        return (states[-1], lax.optimization_barrier(jnp.sum(states * ema_params[3], axis=-1)))
    start_state = jnp.zeros(ema_params.shape[1:], jnp.float32)
    blocks = normed.reshape(-1, BLOCK_POSITIONS, normed.shape[1])
    last_state, smooth = lax.scan(jax.checkpoint(block_step), start_state, blocks)
    return smooth.reshape(normed.shape)

def mega_block(values, norm_gain, w_value, w_mix, w_merge, qk_affine, ema_params, omega):
    normed = layer_norm(values, norm_gain)
    reduced_value = low(jax.nn.silu(low_back(product(low(normed), w_value))))
    mixed_low = low(jax.nn.silu(ema_smooth(normed, ema_params) + omega * normed))
    mix = low_back(product(mixed_low, w_mix))
    zpart = jax.nn.silu(mix[:, :QUERY_KEY_WIDTH])
    reset = jax.nn.silu(mix[:, QUERY_KEY_WIDTH:QUERY_KEY_WIDTH + VALUE_WIDTH])
    update = jax.nn.sigmoid(mix[:, QUERY_KEY_WIDTH + VALUE_WIDTH:QUERY_KEY_WIDTH + VALUE_WIDTH + D])
    query_rows = low(zpart * qk_affine[0] + qk_affine[1]).reshape(-1, BLOCK_POSITIONS, QUERY_KEY_WIDTH)
    key_rows = low(zpart * qk_affine[2] + qk_affine[3]).reshape(-1, BLOCK_POSITIONS, QUERY_KEY_WIDTH)
    attention_scores = low_back(jnp.einsum('scm,shm->sch', query_rows, key_rows, precision=HIGH_PRECISION) * QUERY_KEY_WIDTH ** (-0.5))
    causal = jnp.arange(BLOCK_POSITIONS)[:, None] >= jnp.arange(BLOCK_POSITIONS)[None, :]
    attention_weights = low(jax.nn.softmax(jnp.where(causal, attention_scores, -1e+30), axis=-1))
    attended_values = low_back(jnp.einsum('xyi,xit->xyt', attention_weights, reduced_value.reshape(-1, BLOCK_POSITIONS, VALUE_WIDTH), precision=HIGH_PRECISION))
    gated = low(reset * attended_values.reshape(-1, VALUE_WIDTH))
    hidden = jax.nn.silu(low_back(mix[:, QUERY_KEY_WIDTH + VALUE_WIDTH + D:] + product(gated, w_merge)))
    return update * hidden + (1.0 - update) * values

def feed_forward(values, ffn_gain, w_up, w_down):
    normed = low(layer_norm(values, ffn_gain))
    active = low(jax.nn.silu(low_back(product(normed, w_up))))
    return values + low_back(product(active, w_down))

def whole_layer(values, params):
    norm_gain, first_pack, second_pack, w_z, qk_affine, ema_params, omega, ffn_gain = params
    w_value = first_pack[0][:, :VALUE_WIDTH]
    w_merge = first_pack[0][:, VALUE_WIDTH:].T
    w_mix = jnp.concatenate([w_z, second_pack[0]], axis=1)
    passed = low(low_back(mega_block(values, norm_gain, w_value, w_mix, w_merge, qk_affine, ema_params, omega)))
    return feed_forward(passed, ffn_gain, first_pack[1], second_pack[1].T)

def reference(inputs, cotangent, norm_gain, first_pack, second_pack, w_z, qk_affine, ema_params, omega, ffn_gain):
    initials = (norm_gain, first_pack, second_pack, w_z, qk_affine, ema_params, omega, ffn_gain)
    params = tuple((item.astype(jnp.float32) for item in initials))
    seq_inputs = inputs.astype(jnp.float32).reshape(-1, LEN, D)
    seq_cot = cotangent.astype(jnp.float32).reshape(-1, LEN, D)

    def one_sequence(totals, pair):
        values, grad_out = pair
        result, pull = jax.vjp(whole_layer, values, params)
        grad_values, grad_params = pull(grad_out)
        summed = tuple((total_now + grad_now for total_now, grad_now in zip(totals, grad_params)))
        return (summed, (result, grad_values))
    zeros = tuple((jnp.zeros_like(item) for item in params))
    totals, outputs = lax.scan(one_sequence, zeros, (seq_inputs, seq_cot))
    results, grad_inputs = outputs
    decayed = tuple((total_now if position in (5, 6) else total_now + DECAY * TOKENS * param_now for position, (total_now, param_now) in enumerate(zip(totals, params))))
    return (results.reshape(inputs.shape), grad_inputs.reshape(inputs.shape)) + decayed
```

```python
import functools

import jax
import jax.numpy as jnp
from jax import lax
from jax.experimental import pallas as pl
from jax.experimental.pallas import tpu as pltpu
from jax.sharding import PartitionSpec as P

MESH = pl.DeviceIdType.MESH
F32 = jnp.float32
BF16 = jnp.bfloat16
VALUE_WIDTH = 2048
BLOCK = 128
EPSILON = 1e-05
DECAY = 0.01
CH = 512
TILE = 32
LANES = 128
VMEM_LIMIT = 60 * 1024 * 1024


def dot(a, b):
    return lax.dot_general(a, b, (((1,), (0,)), ((), ())), preferred_element_type=F32)


def dot_nt(a, b):
    return lax.dot_general(a, b, (((1,), (1,)), ((), ())), preferred_element_type=F32)


def normed_rows(v):
    center = v - jnp.mean(v, axis=-1, keepdims=True)
    factor = lax.rsqrt(jnp.mean(center * center, axis=-1, keepdims=True) + EPSILON)
    return center * factor, factor


def norm_back(grad, gain, unit, factor):
    s = grad * gain
    return factor * (
        s
        - jnp.mean(s, axis=-1, keepdims=True)
        - unit * jnp.mean(s * unit, axis=-1, keepdims=True)
    )


def loop(count, body):
    lax.fori_loop(0, count, lambda i, c: (body(i), c)[1], 0)


def aligned(i, size):
    return pl.ds(pl.multiple_of(i * size, size), size)


def to_channel_rows(ref, row, tile):
    groups = tile.shape[1] // LANES
    for sub in range(tile.shape[0] // 8):
        for j in range(groups):
            ref[pl.ds((row + 8 * sub) * groups + j, 8, stride=groups), :] = tile[
                8 * sub : 8 * sub + 8, j * LANES : (j + 1) * LANES
            ]


def from_channel_rows(ref, row, rows, groups):
    tiles = []
    for sub in range(rows // 8):
        tiles.append(
            jnp.concatenate(
                [
                    ref[pl.ds((row + 8 * sub) * groups + j, 8, stride=groups), :]
                    for j in range(groups)
                ],
                axis=1,
            )
        )
    return jnp.concatenate(tiles, axis=0)


def bit_of(value, bit):
    return lax.rem(lax.div(value, 1 << bit), 2)


def flip(value, bit):
    return value + (1 - 2 * bit_of(value, bit)) * (1 << bit)


def rows_of(values):
    return [values[:, j * LANES : (j + 1) * LANES] for j in range(values.shape[1] // LANES)]


def add_all(terms):
    terms = list(terms)
    while len(terms) > 1:
        terms = [a + b for a, b in zip(terms[::2], terms[1::2])] + (
            [terms[-1]] if len(terms) % 2 else []
        )
    return terms[0]


def relay_kernel(
    n,
    x_own, c_own, gain, omega, fgain, q_r, w_r, qt_r, qk, wz, w1h, w2h,
    l_h, r_h, xs_h, gs_h, gxn_h, xx_h, cd_h, gp_h, h0_h, out_h, zg_o, misc_o,
    w1, w2, xc, xn, xs, rv, lv, vl, vsl, rs, ra, mlow, msl, cu, cc, cd, ps, gp,
    gm, zp, zs, zq, zk, pr, prl, tl, tr, h0, fg, fgr, gz, qks, tmp,
    w_sem, in_sem, o_sem, d2d_s, d2d_r, t_s, t_r,
):
    sec = lax.axis_index("section")
    seq = lax.axis_index("seq")
    rows, width = xc.shape
    tok = rows // 2
    groups = width // LANES
    ndim = q_r.shape[0]
    ff = w1.shape[1]
    vw = VALUE_WIDTH
    nblk = rows // BLOCK

    loads = []
    for k, (src, dst) in enumerate(((w1h, w1), (w2h, w2))):
        cp = pltpu.make_async_copy(src, dst, w_sem.at[k])
        cp.start()
        loads.append(cp)

    barrier = pltpu.get_barrier_semaphore()
    pl.semaphore_signal(barrier, inc=1, device_id={"section": 1 - sec}, device_id_type=MESH)
    for k in range(1, n):
        pl.semaphore_signal(
            barrier, inc=1, device_id={"seq": lax.rem(seq + k, n)}, device_id_type=MESH
        )
    pl.semaphore_wait(barrier, n)

    def to_sibling(src, dst, k):
        return pltpu.make_async_remote_copy(
            src_ref=src, dst_ref=dst, send_sem=d2d_s.at[k], recv_sem=d2d_r.at[k],
            device_id={"section": 1 - sec}, device_id_type=MESH,
        )

    def out_copy(src, dst, k):
        cp = pltpu.make_async_copy(src, dst, o_sem.at[k])
        cp.start()
        return cp

    def tail_copy(k):
        return pltpu.make_async_remote_copy(
            src_ref=tl, dst_ref=tr.at[k], send_sem=t_s.at[k], recv_sem=t_r.at[k],
            device_id={"seq": seq + k}, device_id_type=MESH,
        )

    first_half, second_half = xc.at[pl.ds(0, tok)], xc.at[pl.ds(tok, tok)]

    def transpose_into(slot, src):
        def one(j):
            lv[slot, aligned(j, LANES), :] = src[:, aligned(j, LANES)].T

        loop(width // LANES, one)

    @pl.when(sec == 0)
    def _():
        give = to_sibling(c_own, first_half, 0)
        give.start()
        own = pltpu.make_async_copy(x_own, first_half, in_sem)
        own.start()
        own.wait()
        give.wait()
        outs = [out_copy(xc, xx_h, 0)]

        g = gain[...]

        def norm_tile(i):
            unit, _ = normed_rows(xc[aligned(i, TILE), :].astype(F32))
            tile = unit * g
            xn[aligned(i, TILE), :] = tile
            mlow[aligned(i, TILE), :] = tile.astype(BF16)
            to_channel_rows(xs, i * TILE, tile)

        loop(rows // TILE, norm_tile)
        xs_out = out_copy(xs, xs_h, 1)

        q = [q_r[j] for j in range(ndim)]
        for m in range(2):

            def tail_step(i, h):
                for u in range(8):
                    x = xs[pl.ds(pl.multiple_of((m * tok + i * 8 + u) * groups, groups), groups), :]
                    h = tuple(q[j] * h[j] + x for j in range(ndim))
                return h

            h = lax.fori_loop(
                0, tok // 8, tail_step, tuple(jnp.zeros((groups, LANES), F32) for _ in range(ndim))
            )
            for j in range(ndim):
                tl[m, j] = h[j]
        for k in range(1, n):

            @pl.when(seq + k < n)
            def _():
                tail_copy(k).start()

            @pl.when(seq - k < 0)
            def _():
                tr[k] = jnp.zeros(tr.shape[1:], F32)

        for cp in loads:
            cp.wait()
        transpose_into(0, mlow)

        def value_chunk(c):
            pre = dot(mlow[...], w1[:, aligned(c, CH)])
            sig = jax.nn.sigmoid(pre)
            vl[:, aligned(c, CH)] = (pre * sig).astype(BF16)
            vsl[:, aligned(c, CH)] = (sig * (1.0 + pre * (1.0 - sig))).astype(BF16)

        loop(vw // CH, value_chunk)

        for k in range(1, n):

            @pl.when(seq - k >= 0)
            def _():
                tail_copy(k).wait_recv()

        for m in range(2):
            for j in range(ndim):
                state = jnp.zeros((groups, LANES), F32)
                for k in range(n - 1, 0, -1):
                    state = state * qt_r[j] + tr[k, m, j]
                h0[m, j] = state
        outs.append(out_copy(h0, h0_h, 2))
        xs_out.wait()

        w = [w_r[j] for j in range(ndim)]
        for m in range(2):

            def scan_step(i, h):
                for u in range(8):
                    at = pl.ds(pl.multiple_of((m * tok + i * 8 + u) * groups, groups), groups)
                    x = xs[at, :]
                    h = tuple(q[j] * h[j] + x for j in range(ndim))
                    xs[at, :] = add_all(w[j] * h[j] for j in range(ndim))
                return h

            lax.fori_loop(0, tok // 8, scan_step, tuple(h0[m, j] for j in range(ndim)))

        om = omega[...]

        def mixed_tile(i):
            smooth = from_channel_rows(xs, i * TILE, TILE, groups)
            pre = smooth + om * xn[aligned(i, TILE), :]
            sig = jax.nn.sigmoid(pre)
            mlow[aligned(i, TILE), :] = (pre * sig).astype(BF16)
            msl[aligned(i, TILE), :] = (sig * (1.0 + pre * (1.0 - sig))).astype(BF16)

        loop(rows // TILE, mixed_tile)

        z_pre = dot(mlow[...], wz[...])
        sig = jax.nn.sigmoid(z_pre)
        zpart = z_pre * sig
        zp[...] = zpart
        zs[...] = sig * (1.0 + z_pre * (1.0 - sig))
        zq[...] = (zpart * qk[0:1, :] + qk[1:2, :]).astype(BF16)
        zk[...] = (zpart * qk[2:3, :] + qk[3:4, :]).astype(BF16)
        scale = qk.shape[1] ** -0.5
        row_ids = lax.broadcasted_iota(jnp.int32, (BLOCK, BLOCK), 0)
        col_ids = lax.broadcasted_iota(jnp.int32, (BLOCK, BLOCK), 1)
        for b in range(nblk):
            at = pl.ds(b * BLOCK, BLOCK)
            scores = jnp.where(row_ids >= col_ids, dot_nt(zq[at, :], zk[at, :]) * scale, -1e30)
            expo = jnp.exp(scores - jnp.max(scores, axis=-1, keepdims=True))
            probs = expo / jnp.sum(expo, axis=-1, keepdims=True)
            pr[at, :] = probs
            prl[at, :] = probs.astype(BF16)

        def reset_chunk(c):
            at = aligned(c, CH)
            pre = dot(mlow[...], w2[:, at])
            for b in range(nblk):
                part = pl.ds(b * BLOCK, BLOCK)
                att = dot(prl[part, :], vl[part, at])
                p = pre[b * BLOCK : (b + 1) * BLOCK]
                sig = jax.nn.sigmoid(p)
                reset = p * sig
                rs[part, at] = reset.astype(BF16)
                ra[part, at] = (att * (sig * (1.0 + p * (1.0 - sig)))).astype(BF16)
                rv[part, aligned(c + vw // CH, CH)] = (reset * att).astype(BF16)

        loop(vw // CH, reset_chunk)

        def cand_chunk(c):
            at = aligned(c, CH)
            update = jax.nn.sigmoid(dot(mlow[...], w2[:, aligned(c + vw // CH, CH)]))
            gm[:, at] = dot(mlow[...], w2[:, aligned(c + (vw + width) // CH, CH)])
            cand = gm[:, at] + dot_nt(rv[:, vw : 2 * vw], w1[at, vw : 2 * vw])
            x = xc[:, at].astype(F32)
            sig = jax.nn.sigmoid(cand)
            hidden = cand * sig
            keep = 1.0 - update
            ps[:, at] = (update * hidden + keep * x).astype(BF16)
            cu[:, at] = ((hidden - x) * update * keep).astype(BF16)
            cc[:, at] = (update * (sig * (1.0 + cand * (1.0 - sig)))).astype(BF16)
            cd[:, at] = keep.astype(BF16)

        loop(width // CH, cand_chunk)
        forth = to_sibling(ps, ps, 1)
        forth.start()
        outs.append(out_copy(cd, cd_h, 3))
        transpose_into(2, mlow)
        to_sibling(gp, gp, 2).wait_recv()
        outs.append(out_copy(gp, gp_h, 4))

        def direct_tile(i):
            at = aligned(i, TILE)
            grad = gp[at, :].astype(F32)
            rv[at, 3 * vw : 3 * vw + width] = (grad * cu[at, :].astype(F32)).astype(BF16)
            rv[at, 3 * vw + width :] = (grad * cc[at, :].astype(F32)).astype(BF16)

        loop(rows // TILE, direct_tile)

        def gated_chunk(c):
            at = aligned(c, CH)
            grad = dot(rv[:, 3 * vw + width :], w1[:, aligned(c + vw // CH, CH)])
            rv[:, aligned(c + 2 * vw // CH, CH)] = (grad * ra[:, at].astype(F32)).astype(BF16)
            rs[:, at] = (grad * rs[:, at].astype(F32)).astype(BF16)

        loop(vw // CH, gated_chunk)

        qks[...] = jnp.zeros_like(qks)

        def attention_back(b):
            at = aligned(b, BLOCK)
            probs = pr[at, :]
            tmp[0] = dot_nt(rs[at, :], vl[at, :])
            grad_probs = tmp[0]
            grad_scores = probs * (
                grad_probs - jnp.sum(grad_probs * probs, axis=-1, keepdims=True)
            )
            tmp[1] = dot(grad_scores.astype(BF16), zk[at, :])
            tmp[2] = dot(grad_scores.T.astype(BF16), zq[at, :])
            grad_query, grad_keys = tmp[1] * scale, tmp[2] * scale
            zpart = zp[at, :]
            for k, term in enumerate((grad_query * zpart, grad_query, grad_keys * zpart, grad_keys)):
                qks[k : k + 1, :] += jnp.sum(term, axis=0, keepdims=True)
            gz[at, :] = (
                (grad_query * qk[0:1, :] + grad_keys * qk[2:3, :]) * zs[at, :]
            ).astype(BF16)
            prl[at, :] = probs.T.astype(BF16)

        loop(nblk, attention_back)

        def grad_value_chunk(c):
            at = aligned(c, CH)
            for b in range(nblk):
                part = pl.ds(b * BLOCK, BLOCK)
                rv[part, at] = (
                    dot(prl[part, :], rs[part, at]) * vsl[part, at].astype(F32)
                ).astype(BF16)

        loop(vw // CH, grad_value_chunk)
        outs.append(out_copy(rv, r_h, 5))
        transpose_into(1, rv.at[:, pl.ds(3 * vw + width, width)])
        outs.append(out_copy(lv, l_h, 6))

        def mixed_chunk(c):
            at = aligned(c, CH)
            gm[:, at] = dot_nt(gz[...], wz[at, :])
            grad = (gm[:, at] + dot_nt(rv[:, 2 * vw :], w2[at, :])) * msl[:, at].astype(F32)
            fgr[0:1, at] = jnp.sum(grad * xn[:, at], axis=0, keepdims=True)
            xn[:, at] = grad * omega[:, at] + dot_nt(rv[:, 0:vw], w1[at, 0:vw])
            gm[:, at] = grad

        loop(width // CH, mixed_chunk)
        outs.append(out_copy(xn, gxn_h, 7))

        def spread_tile(i):
            to_channel_rows(xs, i * TILE, gm[aligned(i, TILE), :])

        loop(rows // TILE, spread_tile)
        outs.append(out_copy(xs, gs_h, 8))
        zg_o[...] = dot(lv[2], gz[...])
        for j, part in enumerate(rows_of(fgr[0:1, :])):
            misc_o[j : j + 1, :] = part
        to_sibling(fg, fg, 3).wait_recv()
        for j, part in enumerate(rows_of(fg[0:1, :])):
            misc_o[groups + j : groups + j + 1, :] = part
        misc_o[2 * groups : 3 * groups, :] = qks[...]
        misc_o[3 * groups :, :] = jnp.zeros((groups, LANES), F32)
        to_sibling(out_h, out_h, 4).wait_recv()
        forth.wait_send()
        for k in range(1, n):

            @pl.when(seq + k < n)
            def _():
                tail_copy(k).wait_send()

        for cp in outs:
            cp.wait()

    @pl.when(sec == 1)
    def _():
        give = to_sibling(x_own, second_half, 0)
        give.start()
        own = pltpu.make_async_copy(c_own, second_half, in_sem)
        own.start()
        own.wait()
        give.wait()
        for cp in loads:
            cp.wait()

        def active_chunk(c):
            rv[:, aligned(c, CH)] = dot(xc[...], w2[:, aligned(c, CH)]).astype(BF16)

        loop(ff // CH, active_chunk)
        transpose_into(2, xc)
        to_sibling(ps, ps, 1).wait_recv()
        g = fgain[...]

        def norm_tile(i):
            at = aligned(i, TILE)
            unit, _ = normed_rows(ps[at, :].astype(F32))
            mlow[at, :] = (unit * g).astype(BF16)

        loop(rows // TILE, norm_tile)
        xn[...] = jnp.zeros_like(xn)

        def hidden_chunk(c):
            at = aligned(c, CH)
            pre = dot(mlow[...], w1[:, at])
            sig = jax.nn.sigmoid(pre)
            rv[:, aligned(c + ff // CH, CH)] = (pre * sig).astype(BF16)
            grad = (rv[:, at].astype(F32) * (sig * (1.0 + pre * (1.0 - sig)))).astype(BF16)
            rv[:, at] = grad
            xn[...] += dot_nt(grad, w1[:, at])

        loop(ff // CH, hidden_chunk)
        outs = [out_copy(rv, r_h, 5)]
        fg[...] = jnp.zeros_like(fg)

        def back_tile(i):
            at = aligned(i, TILE)
            unit, factor = normed_rows(ps[at, :].astype(F32))
            grad = xn[at, :]
            fg[0:1, :] += jnp.sum(grad * unit, axis=0, keepdims=True)
            gp[at, :] = (
                xc[at, :].astype(F32) + norm_back(grad, g, unit, factor)
            ).astype(BF16)

        loop(rows // TILE, back_tile)
        back = to_sibling(gp, gp, 2)
        back.start()
        gains = to_sibling(fg, fg, 3)
        gains.start()
        transpose_into(0, mlow)
        transpose_into(1, mlow)
        outs.append(out_copy(lv, l_h, 6))

        def out_chunk(c):
            at = aligned(c, CH)
            xn[:, at] = ps[:, at].astype(F32) + dot_nt(rv[:, ff : 2 * ff], w2[at, :])

        loop(width // CH, out_chunk)
        result = to_sibling(xn.at[pl.ds(0, tok)], out_h, 4)
        result.start()
        outs.append(out_copy(xn.at[pl.ds(tok, tok)], out_h, 7))
        for cp in (back, gains, result):
            cp.wait_send()
        for cp in outs:
            cp.wait()


def relay(n, x, c, gain, omega, fgain, q, w, qt, qk, wz, w1, w2):
    rows, width = 2 * x.shape[0], x.shape[1]
    ff, vw, zw = w1.shape[1], VALUE_WIDTH, wz.shape[1]
    groups = width // LANES
    ndim = q.shape[0]
    any_spec = pl.BlockSpec(memory_space=pl.ANY)
    vmem = pl.BlockSpec(memory_space=pltpu.VMEM)

    def shape(dims, kind):
        return jax.ShapeDtypeStruct(dims, kind)

    outs = [
        (shape((3, width, rows), BF16), any_spec),
        (shape((rows, 2 * ff), BF16), any_spec),
        (shape((rows * groups, LANES), F32), any_spec),
        (shape((rows * groups, LANES), F32), any_spec),
        (shape((rows, width), F32), any_spec),
        (shape((rows, width), BF16), any_spec),
        (shape((rows, width), BF16), any_spec),
        (shape((rows, width), BF16), any_spec),
        (shape((2, ndim, groups, LANES), F32), any_spec),
        (shape((rows // 2, width), F32), any_spec),
        (shape((width, zw), F32), vmem),
        (shape((4 * groups, LANES), F32), vmem),
    ]
    return pl.pallas_call(
        functools.partial(relay_kernel, n),
        out_shape=[o[0] for o in outs],
        in_specs=[any_spec, any_spec] + [vmem] * 8 + [any_spec, any_spec],
        out_specs=[o[1] for o in outs],
        scratch_shapes=[
            pltpu.VMEM((width, ff), BF16),
            pltpu.VMEM((width, ff), BF16),
            pltpu.VMEM((rows, width), BF16),
            pltpu.VMEM((rows, width), F32),
            pltpu.VMEM((rows * groups, LANES), F32),
            pltpu.VMEM((rows, 2 * ff), BF16),
            pltpu.VMEM((3, width, rows), BF16),
            pltpu.VMEM((rows, vw), BF16),
            pltpu.VMEM((rows, vw), BF16),
            pltpu.VMEM((rows, vw), BF16),
            pltpu.VMEM((rows, vw), BF16),
            pltpu.VMEM((rows, width), BF16),
            pltpu.VMEM((rows, width), BF16),
            pltpu.VMEM((rows, width), BF16),
            pltpu.VMEM((rows, width), BF16),
            pltpu.VMEM((rows, width), BF16),
            pltpu.VMEM((rows, width), BF16),
            pltpu.VMEM((rows, width), BF16),
            pltpu.VMEM((rows, width), F32),
            pltpu.VMEM((rows, zw), F32),
            pltpu.VMEM((rows, zw), F32),
            pltpu.VMEM((rows, zw), BF16),
            pltpu.VMEM((rows, zw), BF16),
            pltpu.VMEM((rows, BLOCK), F32),
            pltpu.VMEM((rows, BLOCK), BF16),
            pltpu.VMEM((2, ndim, groups, LANES), F32),
            pltpu.VMEM((n, 2, ndim, groups, LANES), F32),
            pltpu.VMEM((2, ndim, groups, LANES), F32),
            pltpu.VMEM((8, width), F32),
            pltpu.VMEM((8, width), F32),
            pltpu.VMEM((rows, zw), BF16),
            pltpu.VMEM((8, zw), F32),
            pltpu.VMEM((3, BLOCK, BLOCK), F32),
            pltpu.SemaphoreType.DMA((2,)),
            pltpu.SemaphoreType.DMA,
            pltpu.SemaphoreType.DMA((9,)),
            pltpu.SemaphoreType.DMA((5,)),
            pltpu.SemaphoreType.DMA((5,)),
            pltpu.SemaphoreType.DMA((n,)),
            pltpu.SemaphoreType.DMA((n,)),
        ],
        compiler_params=pltpu.CompilerParams(
            collective_id=0, has_side_effects=True, vmem_limit_bytes=VMEM_LIMIT
        ),
        name="relay",
    )(x, c, gain, omega, fgain, q, w, qt, qk, wz, w1, w2)


LAG_STEP = 2
LAG_Z = 1


def reduce_kernel(
    n, nd, schedule,
    l_h, r_h, xs_h, gs_h, gxn_h, xx_h, cd_h, gp_h, h0, zg, misc, q_r, w_r, qt_r, gain,
    red_h, ig_h, sm_h,
    lv, rv, part, recvs, zr1, zr2, xs, gs, gxn, xx, cd, gp, tl, tr, carry, sm, smr, smz,
    l_sem, r_sem, e_sem, x_s, x_r, z_s, z_r, o_sem, t_s, t_r, m_s, m_r, mo_sem,
):
    sec = lax.axis_index("section")
    seq = lax.axis_index("seq")
    dp = lax.axis_index("dp")
    steps = n.bit_length() - 1
    pairs = part.shape[0]
    block_rows = part.shape[3]
    rows, width = gxn.shape
    tok = rows // 2
    groups = width // LANES
    ndim = q_r.shape[0]
    bit_orders = [
        [(s + color * (steps // 2)) % max(steps, 1) for s in range(steps)] for color in range(2)
    ]
    inner = (dp > 0) & (dp < nd - 1)
    outer_peer = jnp.where(dp < nd // 2, dp - 1, dp + 1)
    middle_peer = jnp.where(dp < nd // 2, dp + 1, dp - 1)

    load_l = pltpu.make_async_copy(l_h, lv, l_sem)
    load_l.start()

    def load_r(t, color):
        at = pl.ds(pl.multiple_of((t + color * pairs) * CH, CH), CH)
        return pltpu.make_async_copy(
            r_h.at[:, at], rv.at[lax.rem(t, 2), color], r_sem.at[lax.rem(t, 2), color]
        )

    for color in range(2):
        load_r(0, color).start()

    barrier = pltpu.get_barrier_semaphore()
    for k in range(1, n):
        pl.semaphore_signal(
            barrier, inc=1, device_id={"seq": lax.rem(seq + k, n)}, device_id_type=MESH
        )

    @pl.when(dp > 0)
    def _():
        pl.semaphore_signal(barrier, inc=1, device_id={"dp": dp - 1}, device_id_type=MESH)

    @pl.when(dp < nd - 1)
    def _():
        pl.semaphore_signal(barrier, inc=1, device_id={"dp": dp + 1}, device_id_type=MESH)

    pl.semaphore_wait(barrier, n - 1 + jnp.where(inner, 2, 1))
    load_l.wait()

    def block_at(color, p):
        blk = seq
        for s in range(steps):
            if (p >> (steps - 1 - s)) & 1:
                blk = flip(blk, bit_orders[color][s])
        return blk

    def xy_copy(t, color, s):
        half = n >> (s + 1)
        return pltpu.make_async_remote_copy(
            src_ref=part.at[t, color, pl.ds(half, half)],
            dst_ref=recvs[s].at[t, color],
            send_sem=x_s.at[s, t, color],
            recv_sem=x_r.at[s, t, color],
            device_id={"seq": flip(seq, bit_orders[color][s])},
            device_id_type=MESH,
        )

    def z_copy(k, t, color):
        src, dst, peer = (
            (part.at[t, color, 0], zr1, middle_peer),
            (part.at[t, color, 0], zr2, middle_peer),
            (zr1.at[t, color], zr2, outer_peer),
        )[k]
        return pltpu.make_async_remote_copy(
            src_ref=src, dst_ref=dst.at[t, color],
            send_sem=z_s.at[0 if k < 2 else 1, t, color], recv_sem=z_r.at[min(k, 1), t, color],
            device_id={"dp": peer}, device_id_type=MESH,
        )

    def store(src, t, color):
        at = pl.ds(pl.multiple_of(t * CH, CH), CH)
        return pltpu.make_async_copy(src, red_h.at[color, :, at], o_sem.at[t, color])

    def produce(t):
        @pl.when(t + 1 < pairs)
        def _():
            for color in range(2):
                load_r(t + 1, color).start()

        for color in range(2):
            load_r(t, color).wait()
            slot = 2 if color else lax.div(t, pairs // 2)
            right = rv[lax.rem(t, 2), color]
            for p in range(n - 1, -1, -1):
                left = lv[slot, aligned(block_at(color, p), block_rows), :]
                part[t, color, p] = dot(left, right).astype(BF16)
                if steps and p == n // 2:
                    xy_copy(t, color, 0).start()

    def absorb(t, s):
        half = n >> (s + 1)
        for color in range(2):
            xy_copy(t, color, s).wait_recv()
            for p in range(half - 1, -1, -1):
                part[t, color, p] = (
                    part[t, color, p].astype(F32) + recvs[s][t, color, p].astype(F32)
                ).astype(BF16)
                if s + 1 < steps and p == half // 2:
                    xy_copy(t, color, s + 1).start()

    def z_first(t):
        @pl.when(jnp.logical_not(inner))
        def _():
            for color in range(2):
                z_copy(0, t, color).start()

    def z_second(t):
        @pl.when(inner)
        def _():
            for color in range(2):
                z_copy(0, t, color).wait_recv()
                part[t, color, 0] = (
                    part[t, color, 0].astype(F32) + zr1[t, color].astype(F32)
                ).astype(BF16)
                z_copy(1, t, color).start()

    def z_third(t):
        @pl.when(inner)
        def _():
            for color in range(2):
                z_copy(1, t, color).wait_recv()
                zr1[t, color] = (
                    part[t, color, 0].astype(F32) + zr2[t, color].astype(F32)
                ).astype(BF16)
                z_copy(2, t, color).start()
                store(zr1.at[t, color], t, color).start()

    def z_last(t):
        @pl.when(jnp.logical_not(inner))
        def _():
            for color in range(2):
                z_copy(2, t, color).wait_recv()
                store(zr2.at[t, color], t, color).start()

    def state_copy(k, way):
        return pltpu.make_async_remote_copy(
            src_ref=tl.at[way], dst_ref=tr.at[way, k],
            send_sem=t_s.at[way, k], recv_sem=t_r.at[way, k],
            device_id={"seq": seq + k if way == 0 else seq - k}, device_id_type=MESH,
        )

    def loads():
        return [
            pltpu.make_async_copy(src, dst, e_sem.at[k])
            for k, (src, dst) in enumerate(
                ((xs_h, xs), (gs_h, gs), (gxn_h, gxn), (xx_h, xx), (cd_h, cd), (gp_h, gp))
            )
        ]

    def channel_rows(t):
        return pl.ds(pl.multiple_of(t * groups, groups), groups)

    zeros = jnp.zeros((groups, LANES), F32)

    def ema_ends():
        for cp in loads()[:2]:
            cp.wait()
        q = [q_r[j] for j in range(ndim)]
        half = ndim // 2
        for m in range(2):
            for part_of in range(2):
                js = range(part_of * half, (part_of + 1) * half)

                def forth(i, state):
                    h, d = state
                    for u in range(8):
                        x = xs[channel_rows(m * tok + i * 8 + u), :]
                        d = tuple(q[j] * d[k] + h[k] for k, j in enumerate(js))
                        h = tuple(q[j] * h[k] + x for k, j in enumerate(js))
                    return h, d

                _, d = lax.fori_loop(
                    0, tok // 8, forth,
                    (tuple(h0[m, j] for j in js), tuple(zeros for _ in js)),
                )
                for k, j in enumerate(js):
                    tl[0, m, j] = d[k]

            def back(i, a):
                for u in range(8):
                    g = gs[channel_rows(m * tok + tok - 1 - (i * 8 + u)), :]
                    a = tuple(q[j] * a[j] + g for j in range(ndim))
                return a

            a = lax.fori_loop(0, tok // 8, back, tuple(zeros for _ in range(ndim)))
            for j in range(ndim):
                tl[1, m, j] = a[j]
        for way in range(2):
            for k in range(1, n):
                has = (seq + k < n) if way == 0 else (seq - k >= 0)
                gets = (seq - k >= 0) if way == 0 else (seq + k < n)

                @pl.when(has)
                def _():
                    state_copy(k, way).start()

                @pl.when(jnp.logical_not(gets))
                def _():
                    tr[way, k] = jnp.zeros(tr.shape[2:], F32)

    def ema_carries():
        for way in range(2):
            for k in range(1, n):
                gets = (seq - k >= 0) if way == 0 else (seq + k < n)

                @pl.when(gets)
                def _():
                    state_copy(k, way).wait_recv()

            for m in range(2):
                for j in range(ndim):
                    state = zeros
                    for k in range(n - 1, 0, -1):
                        state = state * qt_r[j] + tr[way, k, m, j]
                    carry[way, m, j] = state

    def ema_sums():
        half = ndim // 2
        for part_of in range(2):
            js = range(part_of * half, (part_of + 1) * half)
            q = [q_r[j] for j in js]
            total = tuple(zeros for _ in range(2 * half))
            for m in range(2):

                def forth(i, state):
                    h, d, s0, s1 = state
                    for u in range(4):
                        at = channel_rows(m * tok + i * 4 + u)
                        x, g = xs[at, :], gs[at, :]
                        d = tuple(q[k] * d[k] + h[k] for k in range(half))
                        h = tuple(q[k] * h[k] + x for k in range(half))
                        s0 = tuple(s0[k] + g * h[k] for k in range(half))
                        s1 = tuple(s1[k] + g * d[k] for k in range(half))
                    return h, d, s0, s1

                _, _, s0, s1 = lax.fori_loop(
                    0, tok // 4, forth,
                    (
                        tuple(h0[m, j] for j in js),
                        tuple(carry[0, m, j] for j in js),
                        total[:half],
                        total[half:],
                    ),
                )
                total = s0 + s1
            for k, j in enumerate(js):
                sm[pl.ds(width + j * groups, groups), :] = total[k]
                sm[pl.ds(width + (ndim + j) * groups, groups), :] = total[half + k]

    def ema_adjoint():
        q = [q_r[j] for j in range(ndim)]
        w = [w_r[j] for j in range(ndim)]
        for m in range(2):

            def back(i, a):
                for u in range(8):
                    at = channel_rows(m * tok + tok - 1 - (i * 8 + u))
                    g = gs[at, :]
                    a = tuple(q[j] * a[j] + g for j in range(ndim))
                    xs[at, :] = add_all(w[j] * a[j] for j in range(ndim))
                return a

            lax.fori_loop(0, tok // 8, back, tuple(carry[1, m, j] for j in range(ndim)))

    base = width + 2 * ndim * groups

    def input_grads():
        for cp in loads()[2:]:
            cp.wait()
        sm[0:width, :] = zg[...]
        sm[pl.ds(base, 3 * groups), :] = misc[0 : 3 * groups, :]
        g = gain[...]

        def tile(i, total):
            at = aligned(i, TILE)
            unit, factor = normed_rows(xx[at, :].astype(F32))
            grad = gxn[at, :] + from_channel_rows(xs, i * TILE, TILE, groups)
            gxn[at, :] = norm_back(grad, g, unit, factor) + gp[at, :].astype(F32) * cd[
                at, :
            ].astype(F32)
            return total + jnp.sum(grad * unit, axis=0, keepdims=True)

        total = lax.fori_loop(0, rows // TILE, tile, jnp.zeros((1, width), F32))
        for j, piece in enumerate(rows_of(total)):
            sm[base + 3 * groups + j : base + 3 * groups + j + 1, :] = piece
        pltpu.make_async_copy(gxn, ig_h, mo_sem.at[0]).start()

    def small_copy(k):
        return pltpu.make_async_remote_copy(
            src_ref=sm, dst_ref=smr.at[k], send_sem=m_s.at[k], recv_sem=m_r.at[k],
            device_id={"seq": flip(seq, k)}, device_id_type=MESH,
        )

    def small_z(k):
        src, dst, peer = (
            (sm, smz.at[0], middle_peer),
            (sm, smz.at[1], middle_peer),
            (sm, smz.at[1], outer_peer),
        )[k]
        return pltpu.make_async_remote_copy(
            src_ref=src, dst_ref=dst,
            send_sem=m_s.at[steps + (0 if k < 2 else 1)],
            recv_sem=m_r.at[steps + min(k, 1)],
            device_id={"dp": peer}, device_id_type=MESH,
        )

    def small_add(k):
        small_copy(k).wait()
        sm[...] += smr[k]

    def small_z_first():
        @pl.when(jnp.logical_not(inner))
        def _():
            small_z(0).start()

    def small_z_second():
        @pl.when(inner)
        def _():
            small_z(0).wait_recv()
            sm[...] += smz[0]
            small_z(1).start()

    def small_z_third():
        @pl.when(inner)
        def _():
            small_z(1).wait()
            sm[...] += smz[1]
            small_z(2).start()
            pltpu.make_async_copy(sm, sm_h, mo_sem.at[1]).start()

    def small_z_last():
        @pl.when(jnp.logical_not(inner))
        def _():
            small_z(2).wait_recv()
            pltpu.make_async_copy(smz.at[1], sm_h, mo_sem.at[1]).start()

    first_lag, z_lag, mega_at, ticks = schedule
    mega_work = [
        lambda: [cp.start() for cp in loads()], ema_ends, ema_carries, ema_sums, ema_adjoint, input_grads
    ]
    mega_ticks = list(mega_at)
    for k in range(steps):
        mega_work.append(lambda k=k: small_copy(k).start())
        mega_work.append(lambda k=k: small_add(k))
        mega_ticks += [mega_ticks[-1], mega_ticks[-1] + 2]
    for stage in (small_z_first, small_z_second, small_z_third, small_z_last):
        mega_work.append(stage)
        mega_ticks.append(mega_ticks[-1] + 1)

    def tick(t):
        def at_lag(lag, stage):
            @pl.when((t >= lag) & (t - lag < pairs))
            def _():
                stage(t - lag)

        at_lag(0, produce)
        lag = 0
        for s in range(steps):
            lag += first_lag
            at_lag(lag, lambda u, s=s: absorb(u, s))
        at_lag(lag, z_first)
        for stage in (z_second, z_third, z_last):
            lag += z_lag
            at_lag(lag, stage)

        for when in sorted(set(mega_ticks)):
            work = [f for f, m in zip(mega_work, mega_ticks) if m == when]

            @pl.when((t == when) & (sec == 0))
            def _():
                for f in work:
                    f()

    total_ticks = max(pairs + steps * first_lag + 3 * z_lag, mega_ticks[-1] + 1)
    loop(total_ticks, tick)

    def drain(t):
        for color in range(2):
            for s in range(steps):
                xy_copy(t, color, s).wait_send()

            @pl.when(inner)
            def _():
                z_copy(1, t, color).wait_send()
                z_copy(2, t, color).wait_send()
                store(zr1.at[t, color], t, color).wait()

            @pl.when(jnp.logical_not(inner))
            def _():
                z_copy(0, t, color).wait_send()
                store(zr2.at[t, color], t, color).wait()

    loop(pairs, drain)

    @pl.when(sec == 0)
    def _():
        for way in range(2):
            for k in range(1, n):
                has = (seq + k < n) if way == 0 else (seq - k >= 0)

                @pl.when(has)
                def _():
                    state_copy(k, way).wait_send()

        @pl.when(inner)
        def _():
            small_z(2).wait_send()
            pltpu.make_async_copy(sm, sm_h, mo_sem.at[1]).wait()

        @pl.when(jnp.logical_not(inner))
        def _():
            small_z(0).wait_send()
            pltpu.make_async_copy(smz.at[1], sm_h, mo_sem.at[1]).wait()

        pltpu.make_async_copy(gxn, ig_h, mo_sem.at[0]).wait()


SCHEDULE = (2, 1, (1, 2, 3, 4, 5, 6), 0)


def reduce_grads(n, nd, l, r, xs, gs, gxn, xx, cd, gp, h0, zg, misc, q, w, qt, gain):
    rows, width = gxn.shape
    groups = width // LANES
    ndim = q.shape[0]
    ff = r.shape[1] // 2
    pairs = ff // CH
    block_rows = width // n
    steps = n.bit_length() - 1
    small_rows = width + 2 * ndim * groups + 4 * groups
    any_spec = pl.BlockSpec(memory_space=pl.ANY)
    vmem = pl.BlockSpec(memory_space=pltpu.VMEM)

    def kernel(*refs):
        fixed = refs[: 18 + 3]
        rest = list(refs[18 + 3 :])
        recvs = rest[:steps]
        reduce_kernel(n, nd, SCHEDULE, *fixed, recvs, *rest[steps:])

    return pl.pallas_call(
        kernel,
        out_shape=[
            jax.ShapeDtypeStruct((2, block_rows, ff), BF16),
            jax.ShapeDtypeStruct((rows, width), F32),
            jax.ShapeDtypeStruct((small_rows, LANES), F32),
        ],
        in_specs=[any_spec] * 8 + [vmem] * 7,
        out_specs=[any_spec] * 3,
        scratch_shapes=[
            pltpu.VMEM((3, width, rows), BF16),
            pltpu.VMEM((2, 2, rows, CH), BF16),
            pltpu.VMEM((pairs, 2, n, block_rows, CH), BF16),
        ]
        + [pltpu.VMEM((pairs, 2, n >> (s + 1), block_rows, CH), BF16) for s in range(steps)]
        + [
            pltpu.VMEM((pairs, 2, block_rows, CH), BF16),
            pltpu.VMEM((pairs, 2, block_rows, CH), BF16),
            pltpu.VMEM((rows * groups, LANES), F32),
            pltpu.VMEM((rows * groups, LANES), F32),
            pltpu.VMEM((rows, width), F32),
            pltpu.VMEM((rows, width), BF16),
            pltpu.VMEM((rows, width), BF16),
            pltpu.VMEM((rows, width), BF16),
            pltpu.VMEM((2, 2, ndim, groups, LANES), F32),
            pltpu.VMEM((2, n, 2, ndim, groups, LANES), F32),
            pltpu.VMEM((2, 2, ndim, groups, LANES), F32),
            pltpu.VMEM((small_rows, LANES), F32),
            pltpu.VMEM((max(steps, 1), small_rows, LANES), F32),
            pltpu.VMEM((2, small_rows, LANES), F32),
            pltpu.SemaphoreType.DMA,
            pltpu.SemaphoreType.DMA((2, 2)),
            pltpu.SemaphoreType.DMA((6,)),
            pltpu.SemaphoreType.DMA((max(steps, 1), pairs, 2)),
            pltpu.SemaphoreType.DMA((max(steps, 1), pairs, 2)),
            pltpu.SemaphoreType.DMA((2, pairs, 2)),
            pltpu.SemaphoreType.DMA((2, pairs, 2)),
            pltpu.SemaphoreType.DMA((pairs, 2)),
            pltpu.SemaphoreType.DMA((2, n)),
            pltpu.SemaphoreType.DMA((2, n)),
            pltpu.SemaphoreType.DMA((steps + 2,)),
            pltpu.SemaphoreType.DMA((steps + 2,)),
            pltpu.SemaphoreType.DMA((2,)),
        ],
        compiler_params=pltpu.CompilerParams(
            collective_id=1, has_side_effects=True, vmem_limit_bytes=VMEM_LIMIT
        ),
        name="reduce_grads",
    )(l, r, xs, gs, gxn, xx, cd, gp, h0, zg, misc, q, w, qt, gain)


def body(
    inputs, cotangent, norm_gain, first_pack, second_pack, w_z, qk_affine, ema_params, omega, ffn_gain
):
    n = lax.axis_size("seq")
    nd = lax.axis_size("dp")
    is_first = lax.axis_index("section") == 0
    tok, width = inputs.shape[2:]
    groups = width // LANES
    ndim = ema_params.shape[2]

    alpha = jax.nn.sigmoid(ema_params[0])
    damp = jax.nn.sigmoid(ema_params[1])
    inject = alpha * ema_params[2]
    eta = ema_params[3]
    weight = eta * inject

    def by_dim(a):
        return a.T.reshape(ndim, groups, LANES)

    q = by_dim(1.0 - alpha * damp)
    w = by_dim(weight)
    qt = lax.integer_pow(q, tok)

    def line(v):
        return v.reshape(1, width)

    l, r, xs, gs, gxn, xx, cd, gp, h0, block_output, zg, misc = relay(
        n, inputs[0, 0], cotangent[0, 0], line(norm_gain), line(omega), line(ffn_gain),
        q, w, qt, qk_affine, w_z, first_pack[0], second_pack[0],
    )
    red, grads, small = reduce_grads(
        n, nd, l, r, xs, gs, gxn, xx, cd, gp, h0, zg, misc, q, w, qt, line(norm_gain)
    )
    there = lax.ppermute(grads[tok:], "section", [(0, 1)])
    small_there = lax.ppermute(small, "section", [(0, 1)])
    input_grad = jnp.where(is_first, grads[:tok], there)
    small = jnp.where(is_first, small, small_there)

    coeff = DECAY * 2 * nd * n * tok
    block_rows = width // n
    seq = lax.axis_index("seq")

    def decayed(share, pack):
        own = lax.dynamic_slice_in_dim(pack, seq * block_rows, block_rows, 0)
        return (share.astype(F32) + coeff * own.astype(F32))[None]

    def from_dims(rows):
        return rows.reshape(ndim, width).T

    states = width + ndim * groups
    base = width + 2 * ndim * groups
    sum_0 = from_dims(small[width:states])
    sum_1 = from_dims(small[states:base])
    omega_grad = small[base : base + groups].reshape(width)
    ffn_grad = small[base + groups : base + 2 * groups].reshape(width)
    qk_grad = small[base + 2 * groups : base + 2 * groups + 4]
    norm_grad = small[base + 3 * groups : base + 4 * groups].reshape(width)
    decay_grad = weight * sum_1
    inject_grad = eta * sum_0
    ema_grad = jnp.stack(
        [
            (inject_grad * ema_params[2] - decay_grad * damp) * alpha * (1.0 - alpha),
            -decay_grad * alpha * damp * (1.0 - damp),
            inject_grad * alpha,
            inject * sum_0,
        ]
    )
    return (
        block_output[None, None],
        input_grad[None, None],
        norm_grad + coeff * norm_gain,
        decayed(red[0], first_pack[0]),
        decayed(red[1], second_pack[0]),
        small[:width] + coeff * w_z.astype(F32),
        qk_grad + coeff * qk_affine,
        ema_grad,
        omega_grad,
        ffn_grad + coeff * ffn_gain,
    )


def solution(mesh):
    rows = P("section", "dp", "seq", None)
    packs = P("section", None, None)
    shares = P("section", "seq", None)
    return jax.shard_map(
        body,
        mesh=mesh,
        in_specs=(rows, rows, P(), packs, packs, P(), P(), P(), P(), P()),
        out_specs=(rows, rows, P(), shares, shares, P(), P(), P(), P(), P()),
        check_vma=False,
    )
```

```python
import functools

import jax
import jax.numpy as jnp
from jax import lax
from jax.experimental import pallas as pl
from jax.experimental.pallas import tpu as pltpu
from jax.sharding import PartitionSpec as P

MESH = pl.DeviceIdType.MESH
F32 = jnp.float32
BF16 = jnp.bfloat16
VALUE_WIDTH = 2048
BLOCK = 128
EPSILON = 1e-05
DECAY = 0.01
CH = 512
TILE = 32
LANES = 128
VMEM_LIMIT = 60 * 1024 * 1024
RECOMPUTE_OVER = 4


def dot(a, b):
    return lax.dot_general(a, b, (((1,), (0,)), ((), ())), preferred_element_type=F32)


def dot_nt(a, b):
    return lax.dot_general(a, b, (((1,), (1,)), ((), ())), preferred_element_type=F32)


def normed_rows(v):
    center = v - jnp.mean(v, axis=-1, keepdims=True)
    factor = lax.rsqrt(jnp.mean(center * center, axis=-1, keepdims=True) + EPSILON)
    return center * factor, factor


def norm_back(grad, gain, unit, factor):
    s = grad * gain
    return factor * (
        s
        - jnp.mean(s, axis=-1, keepdims=True)
        - unit * jnp.mean(s * unit, axis=-1, keepdims=True)
    )


def loop(count, body):
    lax.fori_loop(0, count, lambda i, c: (body(i), c)[1], 0)


def aligned(i, size):
    return pl.ds(pl.multiple_of(i * size, size), size)


def to_channel_rows(ref, row, tile):
    groups = tile.shape[1] // LANES
    for sub in range(tile.shape[0] // 8):
        for j in range(groups):
            ref[pl.ds((row + 8 * sub) * groups + j, 8, stride=groups), :] = tile[
                8 * sub : 8 * sub + 8, j * LANES : (j + 1) * LANES
            ]


def from_channel_rows(ref, row, rows, groups):
    tiles = []
    for sub in range(rows // 8):
        tiles.append(
            jnp.concatenate(
                [
                    ref[pl.ds((row + 8 * sub) * groups + j, 8, stride=groups), :]
                    for j in range(groups)
                ],
                axis=1,
            )
        )
    return jnp.concatenate(tiles, axis=0)


def bit_of(value, bit):
    return lax.rem(lax.div(value, 1 << bit), 2)


def flip(value, bit):
    return value + (1 - 2 * bit_of(value, bit)) * (1 << bit)


def rows_of(values):
    return [values[:, j * LANES : (j + 1) * LANES] for j in range(values.shape[1] // LANES)]


def add_all(terms):
    terms = list(terms)
    while len(terms) > 1:
        terms = [a + b for a, b in zip(terms[::2], terms[1::2])] + (
            [terms[-1]] if len(terms) % 2 else []
        )
    return terms[0]


def relay_kernel(
    n,
    x_own, c_own, gain, omega, fgain, q_r, w_r, qt_r, qk, wz, w1h, w2h,
    l_h, r_h, xs_h, gs_h, gxn_h, xx_h, cd_h, gp_h, h0_h, out_h, all_h, zg_o, misc_o,
    w1, w2, xc, xn, xs, rv, lv, vl, vsl, rs, ra, mlow, msl, cu, cc, cd, ps, gp,
    gm, zp, zs, zq, zk, pr, prl, tl, tr, h0, fg, fgr, gz, qks, tmp,
    w_sem, in_sem, o_sem, d2d_s, d2d_r, t_s, t_r, a_s, a_r,
):
    sec = lax.axis_index("section")
    seq = lax.axis_index("seq")
    rows, width = xc.shape
    tok = rows // 2
    groups = width // LANES
    ndim = q_r.shape[0]
    ff = w1.shape[1]
    vw = VALUE_WIDTH
    nblk = rows // BLOCK

    loads = []
    for k, (src, dst) in enumerate(((w1h, w1), (w2h, w2))):
        cp = pltpu.make_async_copy(src, dst, w_sem.at[k])
        cp.start()
        loads.append(cp)

    barrier = pltpu.get_barrier_semaphore()
    pl.semaphore_signal(barrier, inc=1, device_id={"section": 1 - sec}, device_id_type=MESH)
    for k in range(1, n):
        pl.semaphore_signal(
            barrier, inc=1, device_id={"seq": lax.rem(seq + k, n)}, device_id_type=MESH
        )
    pl.semaphore_wait(barrier, n)

    def to_sibling(src, dst, k):
        return pltpu.make_async_remote_copy(
            src_ref=src, dst_ref=dst, send_sem=d2d_s.at[k], recv_sem=d2d_r.at[k],
            device_id={"section": 1 - sec}, device_id_type=MESH,
        )

    def out_copy(src, dst, k):
        cp = pltpu.make_async_copy(src, dst, o_sem.at[k])
        cp.start()
        return cp

    def tail_copy(k):
        return pltpu.make_async_remote_copy(
            src_ref=tl, dst_ref=tr.at[k], send_sem=t_s.at[k], recv_sem=t_r.at[k],
            device_id={"seq": seq + k}, device_id_type=MESH,
        )

    def gather_copy(what, src, k):
        return pltpu.make_async_remote_copy(
            src_ref=src, dst_ref=all_h.at[what, k],
            send_sem=a_s.at[what, k], recv_sem=a_r.at[what, k],
            device_id={"seq": lax.rem(seq + k, n)}, device_id_type=MESH,
        )

    recompute = all_h.shape[1] > 1
    peers = range(1, n) if recompute else ()
    first_half, second_half = xc.at[pl.ds(0, tok)], xc.at[pl.ds(tok, tok)]

    def transpose_into(slot, src):
        def one(j):
            lv[slot, aligned(j, LANES), :] = src[:, aligned(j, LANES)].T

        loop(width // LANES, one)

    @pl.when(sec == 0)
    def _():
        give = to_sibling(c_own, first_half, 0)
        give.start()
        own = pltpu.make_async_copy(x_own, first_half, in_sem)
        own.start()
        own.wait()
        give.wait()
        outs = [out_copy(xc, xx_h, 0)]

        g = gain[...]

        def norm_tile(i):
            unit, _ = normed_rows(xc[aligned(i, TILE), :].astype(F32))
            tile = unit * g
            xn[aligned(i, TILE), :] = tile
            mlow[aligned(i, TILE), :] = tile.astype(BF16)
            to_channel_rows(xs, i * TILE, tile)

        loop(rows // TILE, norm_tile)
        xs_out = out_copy(xs, xs_h, 1)

        q = [q_r[j] for j in range(ndim)]
        for m in range(2):

            def tail_step(i, h):
                for u in range(8):
                    x = xs[pl.ds(pl.multiple_of((m * tok + i * 8 + u) * groups, groups), groups), :]
                    h = tuple(q[j] * h[j] + x for j in range(ndim))
                return h

            h = lax.fori_loop(
                0, tok // 8, tail_step, tuple(jnp.zeros((groups, LANES), F32) for _ in range(ndim))
            )
            for j in range(ndim):
                tl[m, j] = h[j]
        for k in range(1, n):

            @pl.when(seq + k < n)
            def _():
                tail_copy(k).start()

            @pl.when(seq - k < 0)
            def _():
                tr[k] = jnp.zeros(tr.shape[1:], F32)

        for cp in loads:
            cp.wait()
        transpose_into(0, mlow)

        def value_chunk(c):
            pre = dot(mlow[...], w1[:, aligned(c, CH)])
            sig = jax.nn.sigmoid(pre)
            vl[:, aligned(c, CH)] = (pre * sig).astype(BF16)
            vsl[:, aligned(c, CH)] = (sig * (1.0 + pre * (1.0 - sig))).astype(BF16)

        loop(vw // CH, value_chunk)

        for k in range(1, n):

            @pl.when(seq - k >= 0)
            def _():
                tail_copy(k).wait_recv()

        for m in range(2):
            for j in range(ndim):
                state = jnp.zeros((groups, LANES), F32)
                for k in range(n - 1, 0, -1):
                    state = state * qt_r[j] + tr[k, m, j]
                h0[m, j] = state
        outs.append(out_copy(h0, h0_h, 2))
        xs_out.wait()

        w = [w_r[j] for j in range(ndim)]
        for m in range(2):

            def scan_step(i, h):
                for u in range(8):
                    at = pl.ds(pl.multiple_of((m * tok + i * 8 + u) * groups, groups), groups)
                    x = xs[at, :]
                    h = tuple(q[j] * h[j] + x for j in range(ndim))
                    xs[at, :] = add_all(w[j] * h[j] for j in range(ndim))
                return h

            lax.fori_loop(0, tok // 8, scan_step, tuple(h0[m, j] for j in range(ndim)))

        om = omega[...]

        def mixed_tile(i):
            smooth = from_channel_rows(xs, i * TILE, TILE, groups)
            pre = smooth + om * xn[aligned(i, TILE), :]
            sig = jax.nn.sigmoid(pre)
            mlow[aligned(i, TILE), :] = (pre * sig).astype(BF16)
            msl[aligned(i, TILE), :] = (sig * (1.0 + pre * (1.0 - sig))).astype(BF16)

        loop(rows // TILE, mixed_tile)

        z_pre = dot(mlow[...], wz[...])
        sig = jax.nn.sigmoid(z_pre)
        zpart = z_pre * sig
        zp[...] = zpart
        zs[...] = sig * (1.0 + z_pre * (1.0 - sig))
        zq[...] = (zpart * qk[0:1, :] + qk[1:2, :]).astype(BF16)
        zk[...] = (zpart * qk[2:3, :] + qk[3:4, :]).astype(BF16)
        scale = qk.shape[1] ** -0.5
        row_ids = lax.broadcasted_iota(jnp.int32, (BLOCK, BLOCK), 0)
        col_ids = lax.broadcasted_iota(jnp.int32, (BLOCK, BLOCK), 1)
        for b in range(nblk):
            at = pl.ds(b * BLOCK, BLOCK)
            scores = jnp.where(row_ids >= col_ids, dot_nt(zq[at, :], zk[at, :]) * scale, -1e30)
            expo = jnp.exp(scores - jnp.max(scores, axis=-1, keepdims=True))
            probs = expo / jnp.sum(expo, axis=-1, keepdims=True)
            pr[at, :] = probs
            prl[at, :] = probs.astype(BF16)

        def reset_chunk(c):
            at = aligned(c, CH)
            pre = dot(mlow[...], w2[:, at])
            for b in range(nblk):
                part = pl.ds(b * BLOCK, BLOCK)
                att = dot(prl[part, :], vl[part, at])
                p = pre[b * BLOCK : (b + 1) * BLOCK]
                sig = jax.nn.sigmoid(p)
                reset = p * sig
                rs[part, at] = reset.astype(BF16)
                ra[part, at] = (att * (sig * (1.0 + p * (1.0 - sig)))).astype(BF16)
                rv[part, aligned(c + vw // CH, CH)] = (reset * att).astype(BF16)

        loop(vw // CH, reset_chunk)

        def cand_chunk(c):
            at = aligned(c, CH)
            update = jax.nn.sigmoid(dot(mlow[...], w2[:, aligned(c + vw // CH, CH)]))
            gm[:, at] = dot(mlow[...], w2[:, aligned(c + (vw + width) // CH, CH)])
            cand = gm[:, at] + dot_nt(rv[:, vw : 2 * vw], w1[at, vw : 2 * vw])
            x = xc[:, at].astype(F32)
            sig = jax.nn.sigmoid(cand)
            hidden = cand * sig
            keep = 1.0 - update
            ps[:, at] = (update * hidden + keep * x).astype(BF16)
            cu[:, at] = ((hidden - x) * update * keep).astype(BF16)
            cc[:, at] = (update * (sig * (1.0 + cand * (1.0 - sig)))).astype(BF16)
            cd[:, at] = keep.astype(BF16)

        loop(width // CH, cand_chunk)
        forth = to_sibling(ps, ps, 1)
        forth.start()
        outs.append(out_copy(cd, cd_h, 3))
        transpose_into(2, mlow)
        to_sibling(gp, gp, 2).wait_recv()
        outs.append(out_copy(gp, gp_h, 4))

        def direct_tile(i):
            at = aligned(i, TILE)
            grad = gp[at, :].astype(F32)
            rv[at, 3 * vw : 3 * vw + width] = (grad * cu[at, :].astype(F32)).astype(BF16)
            rv[at, 3 * vw + width :] = (grad * cc[at, :].astype(F32)).astype(BF16)

        loop(rows // TILE, direct_tile)

        def gated_chunk(c):
            at = aligned(c, CH)
            grad = dot(rv[:, 3 * vw + width :], w1[:, aligned(c + vw // CH, CH)])
            rv[:, aligned(c + 2 * vw // CH, CH)] = (grad * ra[:, at].astype(F32)).astype(BF16)
            rs[:, at] = (grad * rs[:, at].astype(F32)).astype(BF16)

        loop(vw // CH, gated_chunk)

        qks[...] = jnp.zeros_like(qks)

        def attention_back(b):
            at = aligned(b, BLOCK)
            probs = pr[at, :]
            tmp[0] = dot_nt(rs[at, :], vl[at, :])
            grad_probs = tmp[0]
            grad_scores = probs * (
                grad_probs - jnp.sum(grad_probs * probs, axis=-1, keepdims=True)
            )
            tmp[1] = dot(grad_scores.astype(BF16), zk[at, :])
            tmp[2] = dot(grad_scores.T.astype(BF16), zq[at, :])
            grad_query, grad_keys = tmp[1] * scale, tmp[2] * scale
            zpart = zp[at, :]
            for k, term in enumerate((grad_query * zpart, grad_query, grad_keys * zpart, grad_keys)):
                qks[k : k + 1, :] += jnp.sum(term, axis=0, keepdims=True)
            gz[at, :] = (
                (grad_query * qk[0:1, :] + grad_keys * qk[2:3, :]) * zs[at, :]
            ).astype(BF16)
            prl[at, :] = probs.T.astype(BF16)

        loop(nblk, attention_back)

        def grad_value_chunk(c):
            at = aligned(c, CH)
            for b in range(nblk):
                part = pl.ds(b * BLOCK, BLOCK)
                rv[part, at] = (
                    dot(prl[part, :], rs[part, at]) * vsl[part, at].astype(F32)
                ).astype(BF16)

        loop(vw // CH, grad_value_chunk)
        outs.append(out_copy(rv, r_h, 5))
        transpose_into(1, rv.at[:, pl.ds(3 * vw + width, width)])
        outs.append(out_copy(lv, l_h, 6))

        def mixed_chunk(c):
            at = aligned(c, CH)
            gm[:, at] = dot_nt(gz[...], wz[at, :])
            grad = (gm[:, at] + dot_nt(rv[:, 2 * vw :], w2[at, :])) * msl[:, at].astype(F32)
            fgr[0:1, at] = jnp.sum(grad * xn[:, at], axis=0, keepdims=True)
            xn[:, at] = grad * omega[:, at] + dot_nt(rv[:, 0:vw], w1[at, 0:vw])
            gm[:, at] = grad

        loop(width // CH, mixed_chunk)
        outs.append(out_copy(xn, gxn_h, 7))

        def spread_tile(i):
            to_channel_rows(xs, i * TILE, gm[aligned(i, TILE), :])

        loop(rows // TILE, spread_tile)
        outs.append(out_copy(xs, gs_h, 8))
        zg_o[...] = dot(lv[2], gz[...])
        for j, part in enumerate(rows_of(fgr[0:1, :])):
            misc_o[j : j + 1, :] = part
        to_sibling(fg, fg, 3).wait_recv()
        for j, part in enumerate(rows_of(fg[0:1, :])):
            misc_o[groups + j : groups + j + 1, :] = part
        misc_o[2 * groups : 3 * groups, :] = qks[...]
        misc_o[3 * groups :, :] = jnp.zeros((groups, LANES), F32)
        to_sibling(out_h, out_h, 4).wait_recv()
        forth.wait_send()
        for k in range(1, n):

            @pl.when(seq + k < n)
            def _():
                tail_copy(k).wait_send()

        for cp in outs:
            cp.wait()

    @pl.when(sec == 1)
    def _():
        give = to_sibling(x_own, second_half, 0)
        give.start()
        own = pltpu.make_async_copy(c_own, second_half, in_sem)
        own.start()
        own.wait()
        give.wait()
        for cp in loads:
            cp.wait()

        outs = []
        if recompute:
            outs.append(out_copy(xc, all_h.at[1, 0], 0))
        for k in peers:
            gather_copy(1, xc, k).start()

        def active_chunk(c):
            rv[:, aligned(c, CH)] = dot(xc[...], w2[:, aligned(c, CH)]).astype(BF16)

        loop(ff // CH, active_chunk)
        if not recompute:
            transpose_into(2, xc)
        to_sibling(ps, ps, 1).wait_recv()
        g = fgain[...]

        def norm_tile(i):
            at = aligned(i, TILE)
            unit, _ = normed_rows(ps[at, :].astype(F32))
            mlow[at, :] = (unit * g).astype(BF16)

        loop(rows // TILE, norm_tile)
        if recompute:
            outs.append(out_copy(mlow, all_h.at[0, 0], 1))
        for k in peers:
            gather_copy(0, mlow, k).start()
        xn[...] = jnp.zeros_like(xn)

        def hidden_chunk(c):
            at = aligned(c, CH)
            pre = dot(mlow[...], w1[:, at])
            sig = jax.nn.sigmoid(pre)
            rv[:, aligned(c + ff // CH, CH)] = (pre * sig).astype(BF16)
            grad = (rv[:, at].astype(F32) * (sig * (1.0 + pre * (1.0 - sig)))).astype(BF16)
            rv[:, at] = grad
            xn[...] += dot_nt(grad, w1[:, at])

        loop(ff // CH, hidden_chunk)
        outs.append(out_copy(rv, r_h, 5))
        fg[...] = jnp.zeros_like(fg)

        def back_tile(i):
            at = aligned(i, TILE)
            unit, factor = normed_rows(ps[at, :].astype(F32))
            grad = xn[at, :]
            fg[0:1, :] += jnp.sum(grad * unit, axis=0, keepdims=True)
            gp[at, :] = (
                xc[at, :].astype(F32) + norm_back(grad, g, unit, factor)
            ).astype(BF16)

        loop(rows // TILE, back_tile)
        back = to_sibling(gp, gp, 2)
        back.start()
        gains = to_sibling(fg, fg, 3)
        gains.start()
        if not recompute:
            transpose_into(0, mlow)
            transpose_into(1, mlow)
            outs.append(out_copy(lv, l_h, 6))

        def out_chunk(c):
            at = aligned(c, CH)
            xn[:, at] = ps[:, at].astype(F32) + dot_nt(rv[:, ff : 2 * ff], w2[at, :])

        loop(width // CH, out_chunk)
        result = to_sibling(xn.at[pl.ds(0, tok)], out_h, 4)
        result.start()
        outs.append(out_copy(xn.at[pl.ds(tok, tok)], out_h, 7))
        for cp in (back, gains, result):
            cp.wait_send()
        for what, src in enumerate((mlow, xc)):
            for k in peers:
                gather_copy(what, src, k).wait()
        for cp in outs:
            cp.wait()


def relay(n, x, c, gain, omega, fgain, q, w, qt, qk, wz, w1, w2):
    rows, width = 2 * x.shape[0], x.shape[1]
    ff, vw, zw = w1.shape[1], VALUE_WIDTH, wz.shape[1]
    groups = width // LANES
    ndim = q.shape[0]
    any_spec = pl.BlockSpec(memory_space=pl.ANY)
    vmem = pl.BlockSpec(memory_space=pltpu.VMEM)

    def shape(dims, kind):
        return jax.ShapeDtypeStruct(dims, kind)

    outs = [
        (shape((3, width, rows), BF16), any_spec),
        (shape((rows, 2 * ff), BF16), any_spec),
        (shape((rows * groups, LANES), F32), any_spec),
        (shape((rows * groups, LANES), F32), any_spec),
        (shape((rows, width), F32), any_spec),
        (shape((rows, width), BF16), any_spec),
        (shape((rows, width), BF16), any_spec),
        (shape((rows, width), BF16), any_spec),
        (shape((2, ndim, groups, LANES), F32), any_spec),
        (shape((rows // 2, width), F32), any_spec),
        (shape((2, n if n == RECOMPUTE_OVER else 1, rows, width), BF16), any_spec),
        (shape((width, zw), F32), vmem),
        (shape((4 * groups, LANES), F32), vmem),
    ]
    return pl.pallas_call(
        functools.partial(relay_kernel, n),
        out_shape=[o[0] for o in outs],
        in_specs=[any_spec, any_spec] + [vmem] * 8 + [any_spec, any_spec],
        out_specs=[o[1] for o in outs],
        scratch_shapes=[
            pltpu.VMEM((width, ff), BF16),
            pltpu.VMEM((width, ff), BF16),
            pltpu.VMEM((rows, width), BF16),
            pltpu.VMEM((rows, width), F32),
            pltpu.VMEM((rows * groups, LANES), F32),
            pltpu.VMEM((rows, 2 * ff), BF16),
            pltpu.VMEM((3, width, rows), BF16),
            pltpu.VMEM((rows, vw), BF16),
            pltpu.VMEM((rows, vw), BF16),
            pltpu.VMEM((rows, vw), BF16),
            pltpu.VMEM((rows, vw), BF16),
            pltpu.VMEM((rows, width), BF16),
            pltpu.VMEM((rows, width), BF16),
            pltpu.VMEM((rows, width), BF16),
            pltpu.VMEM((rows, width), BF16),
            pltpu.VMEM((rows, width), BF16),
            pltpu.VMEM((rows, width), BF16),
            pltpu.VMEM((rows, width), BF16),
            pltpu.VMEM((rows, width), F32),
            pltpu.VMEM((rows, zw), F32),
            pltpu.VMEM((rows, zw), F32),
            pltpu.VMEM((rows, zw), BF16),
            pltpu.VMEM((rows, zw), BF16),
            pltpu.VMEM((rows, BLOCK), F32),
            pltpu.VMEM((rows, BLOCK), BF16),
            pltpu.VMEM((2, ndim, groups, LANES), F32),
            pltpu.VMEM((n, 2, ndim, groups, LANES), F32),
            pltpu.VMEM((2, ndim, groups, LANES), F32),
            pltpu.VMEM((8, width), F32),
            pltpu.VMEM((8, width), F32),
            pltpu.VMEM((rows, zw), BF16),
            pltpu.VMEM((8, zw), F32),
            pltpu.VMEM((3, BLOCK, BLOCK), F32),
            pltpu.SemaphoreType.DMA((2,)),
            pltpu.SemaphoreType.DMA,
            pltpu.SemaphoreType.DMA((9,)),
            pltpu.SemaphoreType.DMA((5,)),
            pltpu.SemaphoreType.DMA((5,)),
            pltpu.SemaphoreType.DMA((n,)),
            pltpu.SemaphoreType.DMA((n,)),
            pltpu.SemaphoreType.DMA((2, n)),
            pltpu.SemaphoreType.DMA((2, n)),
        ],
        compiler_params=pltpu.CompilerParams(
            collective_id=0, has_side_effects=True, vmem_limit_bytes=VMEM_LIMIT
        ),
        name="relay",
    )(x, c, gain, omega, fgain, q, w, qt, qk, wz, w1, w2)


def reduce_kernel(
    n, nd, schedule,
    l_h, r_h, all_h, w1h, w2h, xs_h, gs_h, gxn_h, xx_h, cd_h, gp_h,
    h0, zg, misc, q_r, w_r, qt_r, gain,
    red_h, ig_h, sm_h,
    recvs, lv, rv, part, acc, zr1, zr2, xs, gs, gxn, xx, cd, gp, tl, tr, carry, sm, smr, smz,
    l_sem, r_sem, e_sem, x_s, x_r, z_s, z_r, o_sem, t_s, t_r, m_s, m_r, mo_sem, a_sem, w_sem, d_s, d_r,
):
    sec = lax.axis_index("section")
    seq = lax.axis_index("seq")
    dp = lax.axis_index("dp")
    steps = n.bit_length() - 1
    rows, width = gxn.shape
    block_rows = width // n
    pairs = part.shape[0] // (2 * width)
    recompute = all_h.shape[1] > 1
    tok = rows // 2
    groups = width // LANES
    ndim = q_r.shape[0]
    bit_orders = [
        [(s + color * (steps // 2)) % max(steps, 1) for s in range(steps)] for color in range(2)
    ]
    inner = (dp > 0) & (dp < nd - 1)
    outer_peer = jnp.where(dp < nd // 2, dp - 1, dp + 1)
    middle_peer = jnp.where(dp < nd // 2, dp + 1, dp - 1)

    def at_rows(ref, index, size):
        return ref.at[pl.ds(pl.multiple_of(index * size, size), size)]

    def part_at(t, color, p=0, count=1):
        start = ((t * 2 + color) * n + p) * block_rows
        return part.at[pl.ds(pl.multiple_of(start, block_rows), count * block_rows)]

    def recv_at(t, color, s, p=0, count=None):
        half = n >> (s + 1)
        start = ((t * 2 + color) * half + p) * block_rows
        return recvs[s].at[
            pl.ds(pl.multiple_of(start, block_rows), (count or half) * block_rows)
        ]

    def z_at(ref, t, color):
        return at_rows(ref, t * 2 + color, block_rows)

    def load_r(t, color):
        at = pl.ds(pl.multiple_of((t + color * pairs) * CH, CH), CH)
        return pltpu.make_async_copy(
            r_h.at[:, at], rv.at[lax.rem(t, 2), color], r_sem.at[lax.rem(t, 2), color]
        )

    for color in range(2):
        load_r(0, color).start()

    barrier = pltpu.get_barrier_semaphore()
    for k in range(1, n):
        pl.semaphore_signal(
            barrier, inc=1, device_id={"seq": lax.rem(seq + k, n)}, device_id_type=MESH
        )

    @pl.when(dp > 0)
    def _():
        pl.semaphore_signal(barrier, inc=1, device_id={"dp": dp - 1}, device_id_type=MESH)

    @pl.when(dp < nd - 1)
    def _():
        pl.semaphore_signal(barrier, inc=1, device_id={"dp": dp + 1}, device_id_type=MESH)

    @pl.when(sec == 1)
    def _():
        pl.semaphore_signal(barrier, inc=1, device_id={"section": 0}, device_id_type=MESH)

    pl.semaphore_wait(barrier, n - 1 + jnp.where(inner, 2, 1) + (1 - sec))

    def block_at(color, p):
        blk = seq
        for s in range(steps):
            if (p >> (steps - 1 - s)) & 1:
                blk = flip(blk, bit_orders[color][s])
        return blk

    def xy_copy(t, color, s):
        half = n >> (s + 1)
        return pltpu.make_async_remote_copy(
            src_ref=part_at(t, color, half, half),
            dst_ref=recv_at(t, color, s),
            send_sem=x_s.at[s, t, color],
            recv_sem=x_r.at[s, t, color],
            device_id={"seq": flip(seq, bit_orders[color][s])},
            device_id_type=MESH,
        )

    def z_copy(k, t, color):
        src, dst, peer = (
            (part_at(t, color), zr1, middle_peer),
            (part_at(t, color), zr2, middle_peer),
            (z_at(zr1, t, color), zr2, outer_peer),
        )[k]
        return pltpu.make_async_remote_copy(
            src_ref=src, dst_ref=z_at(dst, t, color),
            send_sem=z_s.at[0 if k < 2 else 1, t, color], recv_sem=z_r.at[min(k, 1), t, color],
            device_id={"dp": peer}, device_id_type=MESH,
        )

    def store(src, t, color):
        at = pl.ds(pl.multiple_of(t * CH, CH), CH)
        return pltpu.make_async_copy(src, red_h.at[color, :, at], o_sem.at[t, color])

    def produce(t):
        @pl.when(t + 1 < pairs)
        def _():
            for color in range(2):
                load_r(t + 1, color).start()

        for color in range(2):
            load_r(t, color).wait()
            slot = 2 if color else lax.div(t, pairs // 2)
            right = rv[lax.rem(t, 2), color]
            for p in range(n - 1, -1, -1):
                left = lv[slot, aligned(block_at(color, p), block_rows), :]
                part_at(t, color, p)[...] = dot(left, right).astype(BF16)
                if steps and p == n // 2:
                    xy_copy(t, color, 0).start()

    def add_into(total, term):
        total[...] = (total[...].astype(F32) + term[...].astype(F32)).astype(BF16)

    def token_block(what, g, half):
        return recvs[0].at[pl.ds(pl.multiple_of(((what * n + g) * 2 + half) * rows, rows), rows)]

    def token_copy(what, g, half):
        return pltpu.make_async_copy(
            all_h.at[what, g, :, pl.ds(half * CH, CH)], token_block(what, g, half),
            a_sem.at[what, g, half],
        )

    def weight_at(t, which):
        return recvs[1].at[
            pl.ds(pl.multiple_of((lax.rem(t, 2) * 2 + which) * width, width), width)
        ]

    def weight_copy(t, which):
        return pltpu.make_async_copy(
            (w1h, w2h)[which].at[:, pl.ds(pl.multiple_of(t * CH, CH), CH)], weight_at(t, which),
            w_sem.at[lax.rem(t, 2), which],
        )

    def own_rows(what, g):
        return part_at(g, what, 1)

    def hidden_at(which):
        return part_at(0, which, 2, rows // block_rows)

    def recompute_start():
        for which in range(2):
            weight_copy(0, which).start()
        for g in range(n):
            for what in range(2):
                for half in range(2):
                    token_copy(what, g, half).start()
        for g in range(n):
            for what in range(2):
                for half in range(2):
                    token_copy(what, g, half).wait()
                column = seq * block_rows
                block = token_block(what, g, lax.div(column, CH))
                own = block[:, pl.ds(pl.multiple_of(lax.rem(column, CH), block_rows), block_rows)]
                own_rows(what, g)[...] = own.T

    def recompute_chunk(t):
        @pl.when(t + 1 < pairs)
        def _():
            for which in range(2):
                load_r(t + 1, which).start()
                weight_copy(t + 1, which).start()

        for which in range(2):
            load_r(t, which).wait()
            weight_copy(t, which).wait()
            acc[which] = dot(own_rows(which, 0)[...], rv[lax.rem(t, 2), which])

        def one(i):
            g = i + 1
            w1c, w2c = weight_at(t, 0), weight_at(t, 1)
            pre = dot(token_block(0, g, 0)[...], w1c[0:CH, :]) + dot(
                token_block(0, g, 1)[...], w1c[CH:, :]
            )
            sig = jax.nn.sigmoid(pre)
            hidden_at(1)[...] = (pre * sig).astype(BF16)
            slope = sig * (1.0 + pre * (1.0 - sig))
            grad = dot(token_block(1, g, 0)[...], w2c[0:CH, :]) + dot(
                token_block(1, g, 1)[...], w2c[CH:, :]
            )
            hidden_at(0)[...] = (grad * slope).astype(BF16)
            for which in range(2):
                acc[which] += dot(own_rows(which, g)[...], hidden_at(which)[...])

        loop(n - 1, one)
        for which in range(2):
            part_at(t, which)[...] = acc[which].astype(BF16)

    def absorb(t, s):
        half = n >> (s + 1)
        for color in range(2):
            xy_copy(t, color, s).wait_recv()
            for p in range(half - 1, -1, -1):
                add_into(part_at(t, color, p), recv_at(t, color, s, p, 1))
                if s + 1 < steps and p == half // 2:
                    xy_copy(t, color, s + 1).start()

    def z_first(t):
        @pl.when(jnp.logical_not(inner))
        def _():
            for color in range(2):
                z_copy(0, t, color).start()

    def z_second(t):
        @pl.when(inner)
        def _():
            for color in range(2):
                z_copy(0, t, color).wait_recv()
                add_into(part_at(t, color), z_at(zr1, t, color))
                z_copy(1, t, color).start()

    def z_third(t):
        @pl.when(inner)
        def _():
            for color in range(2):
                z_copy(1, t, color).wait_recv()
                z_at(zr1, t, color)[...] = (
                    part_at(t, color)[...].astype(F32) + z_at(zr2, t, color)[...].astype(F32)
                ).astype(BF16)
                z_copy(2, t, color).start()
                store(z_at(zr1, t, color), t, color).start()

    def z_last(t):
        @pl.when(jnp.logical_not(inner))
        def _():
            for color in range(2):
                z_copy(2, t, color).wait_recv()
                store(z_at(zr2, t, color), t, color).start()

    def state_copy(k, way):
        return pltpu.make_async_remote_copy(
            src_ref=tl.at[way], dst_ref=tr.at[way, k],
            send_sem=t_s.at[way, k], recv_sem=t_r.at[way, k],
            device_id={"seq": seq + k if way == 0 else seq - k}, device_id_type=MESH,
        )

    def loads():
        return [
            pltpu.make_async_copy(src, dst, e_sem.at[k])
            for k, (src, dst) in enumerate(
                ((xs_h, xs), (gs_h, gs), (gxn_h, gxn), (xx_h, xx), (cd_h, cd), (gp_h, gp))
            )
        ]

    def channel_rows(t):
        return pl.ds(pl.multiple_of(t * groups, groups), groups)

    zeros = jnp.zeros((groups, LANES), F32)

    def ema_ends():
        for cp in loads()[:2]:
            cp.wait()
        q = [q_r[j] for j in range(ndim)]
        half = ndim // 2
        for m in range(2):
            for part_of in range(2):
                js = range(part_of * half, (part_of + 1) * half)

                def forth(i, state):
                    h, d = state
                    for u in range(8):
                        x = xs[channel_rows(m * tok + i * 8 + u), :]
                        d = tuple(q[j] * d[k] + h[k] for k, j in enumerate(js))
                        h = tuple(q[j] * h[k] + x for k, j in enumerate(js))
                    return h, d

                _, d = lax.fori_loop(
                    0, tok // 8, forth,
                    (tuple(h0[m, j] for j in js), tuple(zeros for _ in js)),
                )
                for k, j in enumerate(js):
                    tl[0, m, j] = d[k]

            def back(i, a):
                for u in range(8):
                    g = gs[channel_rows(m * tok + tok - 1 - (i * 8 + u)), :]
                    a = tuple(q[j] * a[j] + g for j in range(ndim))
                return a

            a = lax.fori_loop(0, tok // 8, back, tuple(zeros for _ in range(ndim)))
            for j in range(ndim):
                tl[1, m, j] = a[j]
        for way in range(2):
            for k in range(1, n):
                has = (seq + k < n) if way == 0 else (seq - k >= 0)
                gets = (seq - k >= 0) if way == 0 else (seq + k < n)

                @pl.when(has)
                def _():
                    state_copy(k, way).start()

                @pl.when(jnp.logical_not(gets))
                def _():
                    tr[way, k] = jnp.zeros(tr.shape[2:], F32)

    def ema_carries():
        for way in range(2):
            for k in range(1, n):
                gets = (seq - k >= 0) if way == 0 else (seq + k < n)

                @pl.when(gets)
                def _():
                    state_copy(k, way).wait_recv()

            for m in range(2):
                for j in range(ndim):
                    state = zeros
                    for k in range(n - 1, 0, -1):
                        state = state * qt_r[j] + tr[way, k, m, j]
                    carry[way, m, j] = state

    def ema_sums():
        half = ndim // 2
        for part_of in range(2):
            js = range(part_of * half, (part_of + 1) * half)
            q = [q_r[j] for j in js]
            total = tuple(zeros for _ in range(2 * half))
            for m in range(2):

                def forth(i, state):
                    h, d, s0, s1 = state
                    for u in range(4):
                        at = channel_rows(m * tok + i * 4 + u)
                        x, g = xs[at, :], gs[at, :]
                        d = tuple(q[k] * d[k] + h[k] for k in range(half))
                        h = tuple(q[k] * h[k] + x for k in range(half))
                        s0 = tuple(s0[k] + g * h[k] for k in range(half))
                        s1 = tuple(s1[k] + g * d[k] for k in range(half))
                    return h, d, s0, s1

                _, _, s0, s1 = lax.fori_loop(
                    0, tok // 4, forth,
                    (
                        tuple(h0[m, j] for j in js),
                        tuple(carry[0, m, j] for j in js),
                        total[:half],
                        total[half:],
                    ),
                )
                total = s0 + s1
            for k, j in enumerate(js):
                sm[pl.ds(width + j * groups, groups), :] = total[k]
                sm[pl.ds(width + (ndim + j) * groups, groups), :] = total[half + k]

    def ema_adjoint():
        q = [q_r[j] for j in range(ndim)]
        w = [w_r[j] for j in range(ndim)]
        for m in range(2):

            def back(i, a):
                for u in range(8):
                    at = channel_rows(m * tok + tok - 1 - (i * 8 + u))
                    g = gs[at, :]
                    a = tuple(q[j] * a[j] + g for j in range(ndim))
                    xs[at, :] = add_all(w[j] * a[j] for j in range(ndim))
                return a

            lax.fori_loop(0, tok // 8, back, tuple(carry[1, m, j] for j in range(ndim)))

    base = width + 2 * ndim * groups

    def own_grad():
        return pltpu.make_async_copy(gxn.at[pl.ds(0, tok)], ig_h, mo_sem.at[0])

    def to_sibling(src, dst, k):
        return pltpu.make_async_remote_copy(
            src_ref=src, dst_ref=dst, send_sem=d_s.at[k], recv_sem=d_r.at[k],
            device_id={"section": 1 - sec}, device_id_type=MESH,
        )

    def give_grad():
        return to_sibling(gxn.at[pl.ds(tok, tok)], ig_h, 0)

    def give_small(src):
        return to_sibling(src, sm_h, 1)

    def input_grads():
        for cp in loads()[2:]:
            cp.wait()
        sm[0:width, :] = zg[...]
        sm[pl.ds(base, 3 * groups), :] = misc[0 : 3 * groups, :]
        g = gain[...]

        def tile(i, total):
            at = aligned(i, TILE)
            unit, factor = normed_rows(xx[at, :].astype(F32))
            grad = gxn[at, :] + from_channel_rows(xs, i * TILE, TILE, groups)
            gxn[at, :] = norm_back(grad, g, unit, factor) + gp[at, :].astype(F32) * cd[
                at, :
            ].astype(F32)
            return total + jnp.sum(grad * unit, axis=0, keepdims=True)

        total = lax.fori_loop(0, rows // TILE, tile, jnp.zeros((1, width), F32))
        for j, piece in enumerate(rows_of(total)):
            sm[base + 3 * groups + j : base + 3 * groups + j + 1, :] = piece
        own_grad().start()
        give_grad().start()

    def small_copy(k):
        return pltpu.make_async_remote_copy(
            src_ref=sm, dst_ref=smr.at[k], send_sem=m_s.at[k], recv_sem=m_r.at[k],
            device_id={"seq": flip(seq, k)}, device_id_type=MESH,
        )

    def small_z(k):
        src, dst, peer = (
            (sm, smz.at[0], middle_peer),
            (sm, smz.at[1], middle_peer),
            (sm, smz.at[1], outer_peer),
        )[k]
        return pltpu.make_async_remote_copy(
            src_ref=src, dst_ref=dst,
            send_sem=m_s.at[steps + (0 if k < 2 else 1)],
            recv_sem=m_r.at[steps + min(k, 1)],
            device_id={"dp": peer}, device_id_type=MESH,
        )

    def small_add(k):
        small_copy(k).wait()
        sm[...] += smr[k]

    def small_z_first():
        @pl.when(jnp.logical_not(inner))
        def _():
            small_z(0).start()

    def small_z_second():
        @pl.when(inner)
        def _():
            small_z(0).wait_recv()
            sm[...] += smz[0]
            small_z(1).start()

    def small_z_third():
        @pl.when(inner)
        def _():
            small_z(1).wait()
            sm[...] += smz[1]
            small_z(2).start()
            pltpu.make_async_copy(sm, sm_h, mo_sem.at[1]).start()
            give_small(sm).start()

    def small_z_last():
        @pl.when(jnp.logical_not(inner))
        def _():
            small_z(2).wait_recv()
            pltpu.make_async_copy(smz.at[1], sm_h, mo_sem.at[1]).start()
            give_small(smz.at[1]).start()

    first_lag, z_lag, mega_at, ticks = schedule
    mega_work = [
        lambda: [cp.start() for cp in loads()], ema_ends, ema_carries, ema_sums, ema_adjoint, input_grads
    ]
    mega_ticks = list(mega_at)
    for k in range(steps):
        mega_work.append(lambda k=k: small_copy(k).start())
        mega_work.append(lambda k=k: small_add(k))
        mega_ticks += [mega_ticks[-1], mega_ticks[-1] + 2]
    for stage in (small_z_first, small_z_second, small_z_third, small_z_last):
        mega_work.append(stage)
        mega_ticks.append(mega_ticks[-1] + 1)

    def at_lag(t, lag, stage):
        @pl.when((t >= lag) & (t - lag < pairs))
        def _():
            stage(t - lag)

    def z_stages(t, lag):
        at_lag(t, lag, z_first)
        for k, stage in enumerate((z_second, z_third, z_last)):
            at_lag(t, lag + (k + 1) * z_lag, stage)

    def sum_tick(t):
        at_lag(t, 0, produce)
        for s in range(steps):
            at_lag(t, (s + 1) * first_lag, lambda u, s=s: absorb(u, s))
        z_stages(t, steps * first_lag)

    def mega_tick(t):
        sum_tick(t)
        for when in sorted(set(mega_ticks)):
            work = [f for f, m in zip(mega_work, mega_ticks) if m == when]

            @pl.when(t == when)
            def _():
                for f in work:
                    f()

    def recompute_tick(t):
        at_lag(t, 0, recompute_chunk)
        z_stages(t, 0)

    sum_ticks = pairs + steps * first_lag + 3 * z_lag

    def drain(summed):
        def one(t):
            for color in range(2):
                if summed:
                    for s in range(steps):
                        xy_copy(t, color, s).wait_send()

                @pl.when(inner)
                def _():
                    z_copy(1, t, color).wait_send()
                    z_copy(2, t, color).wait_send()
                    store(z_at(zr1, t, color), t, color).wait()

                @pl.when(jnp.logical_not(inner))
                def _():
                    z_copy(0, t, color).wait_send()
                    store(z_at(zr2, t, color), t, color).wait()

        loop(pairs, one)

    load_l = pltpu.make_async_copy(l_h, lv, l_sem)

    @pl.when(sec == 0)
    def _():
        load_l.start()
        load_l.wait()
        loop(max(sum_ticks, mega_ticks[-1] + 1), mega_tick)
        drain(True)

    @pl.when(sec == 1)
    def _():
        if recompute:
            recompute_start()
            loop(pairs + 3 * z_lag, recompute_tick)
        else:
            load_l.start()
            load_l.wait()
            loop(sum_ticks, sum_tick)
        drain(not recompute)

    @pl.when(sec == 0)
    def _():
        for way in range(2):
            for k in range(1, n):
                has = (seq + k < n) if way == 0 else (seq - k >= 0)

                @pl.when(has)
                def _():
                    state_copy(k, way).wait_send()

        @pl.when(inner)
        def _():
            small_z(2).wait_send()
            pltpu.make_async_copy(sm, sm_h, mo_sem.at[1]).wait()
            give_small(sm).wait_send()

        @pl.when(jnp.logical_not(inner))
        def _():
            small_z(0).wait_send()
            pltpu.make_async_copy(smz.at[1], sm_h, mo_sem.at[1]).wait()
            give_small(smz.at[1]).wait_send()

        own_grad().wait()
        give_grad().wait_send()

    @pl.when(sec == 1)
    def _():
        give_grad().wait_recv()
        give_small(sm).wait_recv()


SCHEDULE = (2, 1, (1, 2, 3, 4, 5, 6), 0)


def reduce_grads(n, nd, l, r, both, w1, w2, xs, gs, gxn, xx, cd, gp, h0, zg, misc, q, w, qt, gain):
    rows, width = gxn.shape
    groups = width // LANES
    ndim = q.shape[0]
    ff = r.shape[1] // 2
    pairs = ff // CH
    block_rows = width // n
    steps = n.bit_length() - 1
    small_rows = width + 2 * ndim * groups + 4 * groups
    any_spec = pl.BlockSpec(memory_space=pl.ANY)
    vmem = pl.BlockSpec(memory_space=pltpu.VMEM)

    def kernel(*refs):
        fixed = refs[: 18 + 3]
        rest = list(refs[18 + 3 :])
        recvs = rest[:steps]
        reduce_kernel(n, nd, SCHEDULE, *fixed, recvs, *rest[steps:])

    return pl.pallas_call(
        kernel,
        out_shape=[
            jax.ShapeDtypeStruct((2, block_rows, ff), BF16),
            jax.ShapeDtypeStruct((rows // 2, width), F32),
            jax.ShapeDtypeStruct((small_rows, LANES), F32),
        ],
        in_specs=[any_spec] * 11 + [vmem] * 7,
        out_specs=[any_spec] * 3,
        scratch_shapes=[
            pltpu.VMEM((pairs * 2 * (n >> (s + 1)) * block_rows, CH), BF16) for s in range(steps)
        ]
        + [
            pltpu.VMEM((3, width, rows), BF16),
            pltpu.VMEM((2, 2, rows, CH), BF16),
            pltpu.VMEM((pairs * 2 * width, CH), BF16),
            pltpu.VMEM((2, block_rows, CH), F32),
            pltpu.VMEM((pairs * 2 * block_rows, CH), BF16),
            pltpu.VMEM((pairs * 2 * block_rows, CH), BF16),
            pltpu.VMEM((rows * groups, LANES), F32),
            pltpu.VMEM((rows * groups, LANES), F32),
            pltpu.VMEM((rows, width), F32),
            pltpu.VMEM((rows, width), BF16),
            pltpu.VMEM((rows, width), BF16),
            pltpu.VMEM((rows, width), BF16),
            pltpu.VMEM((2, 2, ndim, groups, LANES), F32),
            pltpu.VMEM((2, n, 2, ndim, groups, LANES), F32),
            pltpu.VMEM((2, 2, ndim, groups, LANES), F32),
            pltpu.VMEM((small_rows, LANES), F32),
            pltpu.VMEM((max(steps, 1), small_rows, LANES), F32),
            pltpu.VMEM((2, small_rows, LANES), F32),
            pltpu.SemaphoreType.DMA,
            pltpu.SemaphoreType.DMA((2, 2)),
            pltpu.SemaphoreType.DMA((6,)),
            pltpu.SemaphoreType.DMA((max(steps, 1), pairs, 2)),
            pltpu.SemaphoreType.DMA((max(steps, 1), pairs, 2)),
            pltpu.SemaphoreType.DMA((2, pairs, 2)),
            pltpu.SemaphoreType.DMA((2, pairs, 2)),
            pltpu.SemaphoreType.DMA((pairs, 2)),
            pltpu.SemaphoreType.DMA((2, n)),
            pltpu.SemaphoreType.DMA((2, n)),
            pltpu.SemaphoreType.DMA((steps + 2,)),
            pltpu.SemaphoreType.DMA((steps + 2,)),
            pltpu.SemaphoreType.DMA((2,)),
            pltpu.SemaphoreType.DMA((2, n, 2)),
            pltpu.SemaphoreType.DMA((2, 2)),
            pltpu.SemaphoreType.DMA((2,)),
            pltpu.SemaphoreType.DMA((2,)),
        ],
        compiler_params=pltpu.CompilerParams(
            collective_id=1, has_side_effects=True, vmem_limit_bytes=VMEM_LIMIT
        ),
        name="reduce_grads",
    )(l, r, both, w1, w2, xs, gs, gxn, xx, cd, gp, h0, zg, misc, q, w, qt, gain)


def body(
    inputs, cotangent, norm_gain, first_pack, second_pack, w_z, qk_affine, ema_params, omega, ffn_gain
):
    n = lax.axis_size("seq")
    nd = lax.axis_size("dp")
    tok, width = inputs.shape[2:]
    groups = width // LANES
    ndim = ema_params.shape[2]

    alpha = jax.nn.sigmoid(ema_params[0])
    damp = jax.nn.sigmoid(ema_params[1])
    inject = alpha * ema_params[2]
    eta = ema_params[3]
    weight = eta * inject

    def by_dim(a):
        return a.T.reshape(ndim, groups, LANES)

    q = by_dim(1.0 - alpha * damp)
    w = by_dim(weight)
    qt = lax.integer_pow(q, tok)

    def line(v):
        return v.reshape(1, width)

    l, r, xs, gs, gxn, xx, cd, gp, h0, block_output, both, zg, misc = relay(
        n, inputs[0, 0], cotangent[0, 0], line(norm_gain), line(omega), line(ffn_gain),
        q, w, qt, qk_affine, w_z, first_pack[0], second_pack[0],
    )
    red, input_grad, small = reduce_grads(
        n, nd, l, r, both, first_pack[0], second_pack[0], xs, gs, gxn, xx, cd, gp, h0, zg, misc,
        q, w, qt, line(norm_gain),
    )

    coeff = DECAY * 2 * nd * n * tok
    block_rows = width // n
    seq = lax.axis_index("seq")

    def decayed(share, pack):
        own = lax.dynamic_slice_in_dim(pack, seq * block_rows, block_rows, 0)
        return (share.astype(F32) + coeff * own.astype(F32))[None]

    def from_dims(rows):
        return rows.reshape(ndim, width).T

    states = width + ndim * groups
    base = width + 2 * ndim * groups
    sum_0 = from_dims(small[width:states])
    sum_1 = from_dims(small[states:base])
    omega_grad = small[base : base + groups].reshape(width)
    ffn_grad = small[base + groups : base + 2 * groups].reshape(width)
    qk_grad = small[base + 2 * groups : base + 2 * groups + 4]
    norm_grad = small[base + 3 * groups : base + 4 * groups].reshape(width)
    decay_grad = weight * sum_1
    inject_grad = eta * sum_0
    ema_grad = jnp.stack(
        [
            (inject_grad * ema_params[2] - decay_grad * damp) * alpha * (1.0 - alpha),
            -decay_grad * alpha * damp * (1.0 - damp),
            inject_grad * alpha,
            inject * sum_0,
        ]
    )
    return (
        block_output[None, None],
        input_grad[None, None],
        norm_grad + coeff * norm_gain,
        decayed(red[0], first_pack[0]),
        decayed(red[1], second_pack[0]),
        small[:width] + coeff * w_z.astype(F32),
        qk_grad + coeff * qk_affine,
        ema_grad,
        omega_grad,
        ffn_grad + coeff * ffn_gain,
    )


def solution(mesh):
    rows = P("section", "dp", "seq", None)
    packs = P("section", None, None)
    shares = P("section", "seq", None)
    return jax.shard_map(
        body,
        mesh=mesh,
        in_specs=(rows, rows, P(), packs, packs, P(), P(), P(), P(), P()),
        out_specs=(rows, rows, P(), shares, shares, P(), P(), P(), P(), P()),
        check_vma=False,
    )
```

```python
import functools

import jax
import jax.numpy as jnp
from jax import lax
from jax.experimental import pallas as pl
from jax.experimental.pallas import tpu as pltpu
from jax.sharding import PartitionSpec as P

MESH = pl.DeviceIdType.MESH
F32 = jnp.float32
BF16 = jnp.bfloat16
VALUE_WIDTH = 2048
BLOCK = 128
EPSILON = 1e-05
DECAY = 0.01
CH = 512
WINDOW = 2
HIDDEN = 1024
TILE = 128
TILE_SMALL = 64
LANES = 128
VMEM_LIMIT = 60 * 1024 * 1024
RECOMPUTE_OVER = 4


def dot(a, b):
    return lax.dot_general(a, b, (((1,), (0,)), ((), ())), preferred_element_type=F32)


def dot_nt(a, b):
    return lax.dot_general(a, b, (((1,), (1,)), ((), ())), preferred_element_type=F32)


def normed_rows(v):
    center = v - jnp.mean(v, axis=-1, keepdims=True)
    factor = lax.rsqrt(jnp.mean(center * center, axis=-1, keepdims=True) + EPSILON)
    return center * factor, factor


def norm_back(grad, gain, unit, factor):
    s = grad * gain
    return factor * (
        s
        - jnp.mean(s, axis=-1, keepdims=True)
        - unit * jnp.mean(s * unit, axis=-1, keepdims=True)
    )


def loop(count, body):
    lax.fori_loop(0, count, lambda i, c: (body(i), c)[1], 0)


def aligned(i, size):
    return pl.ds(pl.multiple_of(i * size, size), size)


def to_channel_rows(ref, row, tile):
    groups = tile.shape[1] // LANES
    for sub in range(tile.shape[0] // 8):
        for j in range(groups):
            ref[pl.ds((row + 8 * sub) * groups + j, 8, stride=groups), :] = tile[
                8 * sub : 8 * sub + 8, j * LANES : (j + 1) * LANES
            ]


def from_channel_rows(ref, row, rows, groups):
    tiles = []
    for sub in range(rows // 8):
        tiles.append(
            jnp.concatenate(
                [
                    ref[pl.ds((row + 8 * sub) * groups + j, 8, stride=groups), :]
                    for j in range(groups)
                ],
                axis=1,
            )
        )
    return jnp.concatenate(tiles, axis=0)


def bit_of(value, bit):
    return lax.rem(lax.div(value, 1 << bit), 2)


def flip(value, bit):
    return value + (1 - 2 * bit_of(value, bit)) * (1 << bit)


def rows_of(values):
    return [values[:, j * LANES : (j + 1) * LANES] for j in range(values.shape[1] // LANES)]


def add_all(terms):
    terms = list(terms)
    while len(terms) > 1:
        terms = [a + b for a, b in zip(terms[::2], terms[1::2])] + (
            [terms[-1]] if len(terms) % 2 else []
        )
    return terms[0]


def set_rates(raw, steps, q_r, w_r, qt_r):
    for j in range(q_r.shape[0]):
        alpha = jax.nn.sigmoid(raw[0, j])
        decay = 1.0 - alpha * jax.nn.sigmoid(raw[1, j])
        q_r[j] = decay
        w_r[j] = raw[3, j] * (alpha * raw[2, j])
        power, base, left = None, decay, steps
        while left:
            if left & 1:
                power = base if power is None else power * base
            base, left = base * base, left >> 1
        qt_r[j] = power


def relay_kernel(
    n,
    x_own, c_own, gain, omega, fgain, raw, qk, wz, w1h, w2h,
    l_h, r_h, xs_h, gs_h, gxn_h, xx_h, cd_h, gp_h, h0_h, out_h, all_h, zg_o, misc_o,
    w1, w2, xc, xn, xs, rv, lv, vl, vsl, rs, ra, mlow, msl, cu, cc, cd, ps, gp,
    gm, zp, zs, zq, zk, pr, prl, tl, tr, h0, fg, fgr, gz, qks, tmp, q_r, w_r, qt_r,
    w_sem, in_sem, o_sem, d2d_s, d2d_r, t_s, t_r, a_s, a_r,
):
    sec = lax.axis_index("section")
    seq = lax.axis_index("seq")
    rows, width = xc.shape
    tok = rows // 2
    groups = width // LANES
    ndim = q_r.shape[0]
    set_rates(raw, tok, q_r, w_r, qt_r)
    ff = w1.shape[1]
    vw = VALUE_WIDTH
    blocks = tok // BLOCK
    zw = qk.shape[1]
    scale = zw**-0.5
    gates, cand_at = 2 * vw, 3 * vw + width
    recompute = all_h.shape[1] > 1
    halves = [pl.ds(m * tok, tok) for m in range(2)]

    barrier = pltpu.get_barrier_semaphore()
    pl.semaphore_signal(barrier, inc=1, device_id={"section": 1 - sec}, device_id_type=MESH)
    for k in range(1, n):
        pl.semaphore_signal(
            barrier, inc=1, device_id={"seq": lax.rem(seq + k, n)}, device_id_type=MESH
        )

    def to_sibling(src, dst, k):
        return pltpu.make_async_remote_copy(
            src_ref=src, dst_ref=dst, send_sem=d2d_s.at[k], recv_sem=d2d_r.at[k],
            device_id={"section": 1 - sec}, device_id_type=MESH,
        )

    def half_to_sibling(ref, m, k):
        return to_sibling(ref.at[halves[m]], ref.at[halves[m]], k + m)

    outs = []

    def out_copy(src, dst):
        cp = pltpu.make_async_copy(src, dst, o_sem.at[len(outs)])
        cp.start()
        outs.append(cp)
        return len(outs) - 1

    def load_weights(parts):
        loads = []
        for k, (src, dst, start, size) in enumerate(parts):
            at = pl.ds(start, size)
            cp = pltpu.make_async_copy(src.at[:, at], dst.at[:, at], w_sem.at[k])
            cp.start()
            loads.append(cp)
        return loads

    def tail_copy(m, k):
        return pltpu.make_async_remote_copy(
            src_ref=tl.at[m], dst_ref=tr.at[m, k], send_sem=t_s.at[m, k], recv_sem=t_r.at[m, k],
            device_id={"seq": seq + k}, device_id_type=MESH,
        )

    def gather_copies(what, src, m, hop):
        copies = []
        half = tok // 2
        for way in range(2):
            at = pl.ds(m * tok + way * half, half)
            first, second = (0, 1) if way == 0 else (1, 0)
            if hop == 0:
                moves = [(src.at[at], 1 << first, first, 0)]
            else:
                moves = [
                    (src.at[at], 1 << second, second, 1),
                    (all_h.at[what, 1 << first, at], 3, second, 2),
                ]
            for source, slot, bit, k in moves:
                copies.append(
                    pltpu.make_async_remote_copy(
                        src_ref=source, dst_ref=all_h.at[what, slot, at],
                        send_sem=a_s.at[what, m, way * 3 + k],
                        recv_sem=a_r.at[what, m, way * 3 + k],
                        device_id={"seq": flip(seq, bit)}, device_id_type=MESH,
                    )
                )
        return copies

    def gather_start(what, src, m):
        if recompute:
            for cp in gather_copies(what, src, m, 0):
                cp.start()

    def gather_forward(what, src, m):
        if recompute:
            for cp in gather_copies(what, src, m, 0):
                cp.wait_recv()
            for cp in gather_copies(what, src, m, 1):
                cp.start()

    def gather_end(what, src, m):
        if recompute:
            for cp in gather_copies(what, src, m, 0):
                cp.wait_send()
            for cp in gather_copies(what, src, m, 1):
                cp.wait()

    def tiles(m, body):
        count = tok // TILE
        loop(count, lambda i: body(i + m * count))

    def transpose_into(slot, src, m):
        def one(j):
            lv[slot, aligned(j, LANES), halves[m]] = src[halves[m], aligned(j, LANES)].T

        loop(width // LANES, one)

    def normalise(m):
        g = gain[...]

        def norm_tile(i):
            unit, _ = normed_rows(xc[aligned(i, TILE), :].astype(F32))
            tile = unit * g
            xn[aligned(i, TILE), :] = tile
            mlow[aligned(i, TILE), :] = tile.astype(BF16)
            to_channel_rows(xs, i * TILE, tile)

        tiles(m, norm_tile)

    def channel_rows(t):
        return pl.ds(pl.multiple_of(t * groups, groups), groups)

    def local_states(m):
        q = [q_r[j] for j in range(ndim)]

        def step(i, h):
            for u in range(8):
                x = xs[channel_rows(m * tok + i * 8 + u), :]
                h = tuple(q[j] * h[j] + x for j in range(ndim))
            return h

        zeros = jnp.zeros((groups, LANES), F32)
        h = lax.fori_loop(0, tok // 8, step, tuple(zeros for _ in range(ndim)))
        for j in range(ndim):
            tl[m, j] = h[j]

    def send_states(m):
        for k in range(1, n):

            @pl.when(seq + k < n)
            def _():
                tail_copy(m, k).start()

            @pl.when(seq - k < 0)
            def _():
                tr[m, k] = jnp.zeros(tr.shape[2:], F32)

    def values(m):
        at_m = halves[m]
        transpose_into(0, mlow, m)

        def value_chunk(c):
            pre = dot(mlow[at_m, :], w1[:, aligned(c, CH)])
            sig = jax.nn.sigmoid(pre)
            vl[at_m, aligned(c, CH)] = (pre * sig).astype(BF16)
            vsl[at_m, aligned(c, CH)] = (sig * (1.0 + pre * (1.0 - sig))).astype(BF16)

        loop(vw // CH, value_chunk)

    def start_states(m):
        for k in range(1, n):

            @pl.when(seq - k >= 0)
            def _():
                tail_copy(m, k).wait_recv()

        for j in range(ndim):
            state = jnp.zeros((groups, LANES), F32)
            for k in range(n - 1, 0, -1):
                state = state * qt_r[j] + tr[m, k, j]
            h0[m, j] = state
        out_copy(h0.at[m], h0_h.at[m])

    def smooth(m):
        q = [q_r[j] for j in range(ndim)]
        w = [w_r[j] for j in range(ndim)]

        def step(i, h):
            for u in range(8):
                at = channel_rows(m * tok + i * 8 + u)
                x = xs[at, :]
                h = tuple(q[j] * h[j] + x for j in range(ndim))
                xs[at, :] = add_all(w[j] * h[j] for j in range(ndim))
            return h

        lax.fori_loop(0, tok // 8, step, tuple(h0[m, j] for j in range(ndim)))
        om = omega[...]

        def mixed_tile(i):
            pre = from_channel_rows(xs, i * TILE, TILE, groups) + om * xn[aligned(i, TILE), :]
            sig = jax.nn.sigmoid(pre)
            mlow[aligned(i, TILE), :] = (pre * sig).astype(BF16)
            msl[aligned(i, TILE), :] = (sig * (1.0 + pre * (1.0 - sig))).astype(BF16)

        tiles(m, mixed_tile)

    def attention(m):
        at_m = halves[m]
        tmz = dot(mlow[at_m, :], wz[...])
        sig = jax.nn.sigmoid(tmz)
        zpart = tmz * sig
        zp[at_m, :] = zpart
        zs[at_m, :] = sig * (1.0 + tmz * (1.0 - sig))
        zq[at_m, :] = (zpart * qk[0:1, :] + qk[1:2, :]).astype(BF16)
        zk[at_m, :] = (zpart * qk[2:3, :] + qk[3:4, :]).astype(BF16)
        row_ids = lax.broadcasted_iota(jnp.int32, (BLOCK, BLOCK), 0)
        col_ids = lax.broadcasted_iota(jnp.int32, (BLOCK, BLOCK), 1)
        for b in range(blocks):
            at = pl.ds(m * tok + b * BLOCK, BLOCK)
            scores = jnp.where(row_ids >= col_ids, dot_nt(zq[at, :], zk[at, :]) * scale, -1e30)
            expo = jnp.exp(scores - jnp.max(scores, axis=-1, keepdims=True))
            probs = expo / jnp.sum(expo, axis=-1, keepdims=True)
            pr[at, :] = probs
            prl[at, :] = probs.astype(BF16)

    def gate(m):
        at_m = halves[m]

        def reset_chunk(c):
            at = aligned(c, CH)
            pre = dot(mlow[at_m, :], w2[:, at])
            for b in range(blocks):
                part = pl.ds(m * tok + b * BLOCK, BLOCK)
                att = dot(prl[part, :], vl[part, at])
                p = pre[b * BLOCK : (b + 1) * BLOCK]
                sig = jax.nn.sigmoid(p)
                reset = p * sig
                rs[part, at] = reset.astype(BF16)
                ra[part, at] = (att * (sig * (1.0 + p * (1.0 - sig)))).astype(BF16)
                rv[part, aligned(c + vw // CH, CH)] = (reset * att).astype(BF16)

        loop(vw // CH, reset_chunk)

    def finish(m):
        at_m = halves[m]

        def cand_chunk(c):
            at = aligned(c, CH)
            update = jax.nn.sigmoid(dot(mlow[at_m, :], w2[:, aligned(c + vw // CH, CH)]))
            gm[at_m, at] = dot(mlow[at_m, :], w2[:, aligned(c + (vw + width) // CH, CH)])
            cand = gm[at_m, at] + dot_nt(rv[at_m, vw : 2 * vw], w1[at, vw : 2 * vw])
            x = xc[at_m, at].astype(F32)
            sig = jax.nn.sigmoid(cand)
            hidden = cand * sig
            keep = 1.0 - update
            ps[at_m, at] = (update * hidden + keep * x).astype(BF16)
            cu[at_m, at] = ((hidden - x) * update * keep).astype(BF16)
            cc[at_m, at] = (update * (sig * (1.0 + cand * (1.0 - sig)))).astype(BF16)
            cd[at_m, at] = keep.astype(BF16)

        loop(width // CH, cand_chunk)

    def backward(m):
        at_m = halves[m]
        first = m * blocks

        def direct_tile(i):
            at = aligned(i, TILE)
            grad = gp[at, :].astype(F32)
            rv[at, 3 * vw : cand_at] = (grad * cu[at, :].astype(F32)).astype(BF16)
            rv[at, cand_at:] = (grad * cc[at, :].astype(F32)).astype(BF16)

        tiles(m, direct_tile)

        def gated_chunk(c):
            at = aligned(c, CH)
            grad = dot(rv[at_m, cand_at:], w1[:, aligned(c + vw // CH, CH)])
            rv[at_m, aligned(c + gates // CH, CH)] = (grad * ra[at_m, at].astype(F32)).astype(BF16)
            rs[at_m, at] = (grad * rs[at_m, at].astype(F32)).astype(BF16)

        loop(vw // CH, gated_chunk)

        def attention_back(b):
            at = aligned(first + b, BLOCK)
            probs = pr[at, :]
            tmp[0] = dot_nt(rs[at, :], vl[at, :])
            grad_probs = tmp[0]
            grad_scores = probs * (
                grad_probs - jnp.sum(grad_probs * probs, axis=-1, keepdims=True)
            )
            tmp[1] = dot(grad_scores.astype(BF16), zk[at, :])
            tmp[2] = dot(grad_scores.T.astype(BF16), zq[at, :])
            grad_query, grad_keys = tmp[1] * scale, tmp[2] * scale
            zpart = zp[at, :]
            for k, term in enumerate((grad_query * zpart, grad_query, grad_keys * zpart, grad_keys)):
                qks[k : k + 1, :] += jnp.sum(term, axis=0, keepdims=True)
            gz[at, :] = (
                (grad_query * qk[0:1, :] + grad_keys * qk[2:3, :]) * zs[at, :]
            ).astype(BF16)
            prl[at, :] = probs.T.astype(BF16)

        loop(blocks, attention_back)

        def grad_value_chunk(c):
            at = aligned(c, CH)
            for b in range(blocks):
                part = pl.ds((first + b) * BLOCK, BLOCK)
                rv[part, at] = (
                    dot(prl[part, :], rs[part, at]) * vsl[part, at].astype(F32)
                ).astype(BF16)

        loop(vw // CH, grad_value_chunk)
        out_copy(rv.at[at_m], r_h.at[at_m])
        transpose_into(1, rv.at[:, pl.ds(cand_at, width)], m)

        def mixed_chunk(c):
            at = aligned(c, CH)
            gm[at_m, at] = dot_nt(gz[at_m, :], wz[at, :])
            grad = (gm[at_m, at] + dot_nt(rv[at_m, gates:], w2[at, :])) * msl[at_m, at].astype(F32)
            fgr[0:1, at] += jnp.sum(grad * xn[at_m, at], axis=0, keepdims=True)
            xn[at_m, at] = grad * omega[:, at] + dot_nt(rv[at_m, 0:vw], w1[at, 0:vw])
            gm[at_m, at] = grad

        loop(width // CH, mixed_chunk)
        out_copy(xn.at[at_m], gxn_h.at[at_m])
        tiles(m, lambda i: to_channel_rows(xs, i * TILE, gm[aligned(i, TILE), :]))
        of_m = pl.ds(m * tok * groups, tok * groups)
        out_copy(xs.at[of_m], gs_h.at[of_m])

    def own_rows(src, m):
        return pltpu.make_async_copy(src, xc.at[halves[m]], in_sem)

    @pl.when(sec == 0)
    def _():
        own_rows(x_own, 0).start()
        load_weights(((w1h, w1, 0, vw), (w2h, w2, 0, ff), (w1h, w1, vw, vw)))
        own_rows(x_own, 0).wait()
        normalise(0)
        local_states(0)

    @pl.when(sec == 1)
    def _():
        own_rows(c_own, 1).start()
        load_weights(((w2h, w2, 0, ff), (w1h, w1, 0, ff)))

    pl.semaphore_wait(barrier, n)

    def wait_weights(k, src, dst, start, size):
        at = pl.ds(start, size)
        pltpu.make_async_copy(src.at[:, at], dst.at[:, at], w_sem.at[k]).wait()

    @pl.when(sec == 0)
    def _():
        give = to_sibling(c_own, xc.at[halves[0]], 0)
        give.start()
        fgr[...] = jnp.zeros_like(fgr)
        qks[...] = jnp.zeros_like(qks)
        send_states(0)
        give.wait()
        out_copy(xc, xx_h)
        normalise(1)
        local_states(1)
        send_states(1)
        saved = out_copy(xs, xs_h)
        wait_weights(0, w1h, w1, 0, vw)
        for m in range(2):
            values(m)
            start_states(m)
            if m == 0:
                outs[saved].wait()
                outs[saved] = None
            smooth(m)
            if m == 0:
                wait_weights(1, w2h, w2, 0, ff)
            attention(m)
            gate(m)
            if m == 0:
                wait_weights(2, w1h, w1, vw, vw)
            finish(m)
            half_to_sibling(ps, m, 1).start()
            transpose_into(2, mlow, m)
        out_copy(cd, cd_h)
        for m in range(2):
            half_to_sibling(gp, m, 3).wait_recv()
            backward(m)
        out_copy(gp, gp_h)
        out_copy(lv, l_h)
        zg_o[...] = dot(lv[2], gz[...])
        for j, part in enumerate(rows_of(fgr[0:1, :])):
            misc_o[j : j + 1, :] = part
        to_sibling(fg, fg, 5).wait_recv()
        for j, part in enumerate(rows_of(fg[0:1, :])):
            misc_o[groups + j : groups + j + 1, :] = part
        misc_o[2 * groups : 3 * groups, :] = qks[...]
        misc_o[3 * groups :, :] = jnp.zeros((groups, LANES), F32)
        if not recompute:
            to_sibling(out_h, out_h, 6).wait_recv()
        for m in range(2):
            half_to_sibling(ps, m, 1).wait_send()
            for k in range(1, n):

                @pl.when(seq + k < n)
                def _():
                    tail_copy(m, k).wait_send()

        for cp in outs:
            if cp is not None:
                cp.wait()

    outs.clear()

    @pl.when(sec == 1)
    def _():
        give = to_sibling(x_own, xc.at[halves[1]], 0)
        give.start()
        own_rows(c_own, 1).wait()
        wait_weights(0, w2h, w2, 0, ff)

        def active_chunk(c, m):
            rv[halves[m], aligned(c, CH)] = dot(xc[halves[m], :], w2[:, aligned(c, CH)]).astype(BF16)

        loop(ff // CH, lambda c: active_chunk(c, 1))
        give.wait()
        if recompute:
            out_copy(xc, all_h.at[1, 0])
        loop(ff // CH, lambda c: active_chunk(c, 0))
        for m in range(2):
            gather_start(1, xc, m)
        if not recompute:
            for m in range(2):
                transpose_into(2, xc, m)
        wait_weights(1, w1h, w1, 0, ff)
        fg[...] = jnp.zeros_like(fg)
        g = fgain[...]
        for m in range(2):
            gather_forward(1, xc, m)
        for m in range(2):
            at_m = halves[m]
            half_to_sibling(ps, m, 1).wait_recv()

            def norm_tile(i):
                at = aligned(i, TILE)
                unit, _ = normed_rows(ps[at, :].astype(F32))
                mlow[at, :] = (unit * g).astype(BF16)

            tiles(m, norm_tile)
            gather_start(0, mlow, m)
            xn[at_m, :] = jnp.zeros((tok, width), F32)

            def hidden_chunk(c):
                at = aligned(c, HIDDEN)
                pre = dot(mlow[at_m, :], w1[:, at])
                sig = jax.nn.sigmoid(pre)
                rv[at_m, aligned(c + ff // HIDDEN, HIDDEN)] = (pre * sig).astype(BF16)
                grad = (
                    rv[at_m, at].astype(F32) * (sig * (1.0 + pre * (1.0 - sig)))
                ).astype(BF16)
                rv[at_m, at] = grad
                xn[at_m, :] += dot_nt(grad, w1[:, at])

            loop(ff // HIDDEN, hidden_chunk)

            def back_tile(i):
                at = aligned(i, TILE)
                unit, factor = normed_rows(ps[at, :].astype(F32))
                grad = xn[at, :]
                fg[0:1, :] += jnp.sum(grad * unit, axis=0, keepdims=True)
                gp[at, :] = (
                    xc[at, :].astype(F32) + norm_back(grad, g, unit, factor)
                ).astype(BF16)

            tiles(m, back_tile)
            half_to_sibling(gp, m, 3).start()
            gather_forward(0, mlow, m)
        gains = to_sibling(fg, fg, 5)
        gains.start()
        out_copy(rv, r_h)
        sent = [gains] + [half_to_sibling(gp, m, 3) for m in range(2)]
        if recompute:
            out_copy(mlow, all_h.at[0, 0])
            out_copy(ps, gp_h)
        else:
            for slot in range(2):
                for m in range(2):
                    transpose_into(slot, mlow, m)
            out_copy(lv, l_h)

            def out_chunk(c):
                at = aligned(c, CH)
                xn[:, at] = ps[:, at].astype(F32) + dot_nt(rv[:, ff : 2 * ff], w2[at, :])

            loop(width // CH, out_chunk)
            result = to_sibling(xn.at[halves[0]], out_h, 6)
            result.start()
            sent.append(result)
            out_copy(xn.at[halves[1]], out_h)
        for cp in sent:
            cp.wait_send()
        for what, src in enumerate((mlow, xc)):
            for m in range(2):
                gather_end(what, src, m)
        for cp in outs:
            cp.wait()


def relay(n, x, c, gain, omega, fgain, raw, qk, wz, w1, w2):
    rows, width = 2 * x.shape[0], x.shape[1]
    ff, vw, zw = w1.shape[1], VALUE_WIDTH, wz.shape[1]
    groups = width // LANES
    ndim = raw.shape[1]
    any_spec = pl.BlockSpec(memory_space=pl.ANY)
    vmem = pl.BlockSpec(memory_space=pltpu.VMEM)

    def shape(dims, kind):
        return jax.ShapeDtypeStruct(dims, kind)

    outs = [
        (shape((3, width, rows), BF16), any_spec),
        (shape((rows, 2 * ff), BF16), any_spec),
        (shape((rows * groups, LANES), F32), any_spec),
        (shape((rows * groups, LANES), F32), any_spec),
        (shape((rows, width), F32), any_spec),
        (shape((rows, width), BF16), any_spec),
        (shape((rows, width), BF16), any_spec),
        (shape((rows, width), BF16), any_spec),
        (shape((2, ndim, groups, LANES), F32), any_spec),
        (shape((rows // 2, width), F32), any_spec),
        (shape((2, n if n == RECOMPUTE_OVER else 1, rows, width), BF16), any_spec),
        (shape((width, zw), F32), vmem),
        (shape((4 * groups, LANES), F32), vmem),
    ]
    return pl.pallas_call(
        functools.partial(relay_kernel, n),
        out_shape=[o[0] for o in outs],
        in_specs=[any_spec, any_spec] + [vmem] * 6 + [any_spec, any_spec],
        out_specs=[o[1] for o in outs],
        scratch_shapes=[
            pltpu.VMEM((width, ff), BF16),
            pltpu.VMEM((width, ff), BF16),
            pltpu.VMEM((rows, width), BF16),
            pltpu.VMEM((rows, width), F32),
            pltpu.VMEM((rows * groups, LANES), F32),
            pltpu.VMEM((rows, 2 * ff), BF16),
            pltpu.VMEM((3, width, rows), BF16),
            pltpu.VMEM((rows, vw), BF16),
            pltpu.VMEM((rows, vw), BF16),
            pltpu.VMEM((rows, vw), BF16),
            pltpu.VMEM((rows, vw), BF16),
            pltpu.VMEM((rows, width), BF16),
            pltpu.VMEM((rows, width), BF16),
            pltpu.VMEM((rows, width), BF16),
            pltpu.VMEM((rows, width), BF16),
            pltpu.VMEM((rows, width), BF16),
            pltpu.VMEM((rows, width), BF16),
            pltpu.VMEM((rows, width), BF16),
            pltpu.VMEM((rows, width), F32),
            pltpu.VMEM((rows, zw), F32),
            pltpu.VMEM((rows, zw), F32),
            pltpu.VMEM((rows, zw), BF16),
            pltpu.VMEM((rows, zw), BF16),
            pltpu.VMEM((rows, BLOCK), F32),
            pltpu.VMEM((rows, BLOCK), BF16),
            pltpu.VMEM((2, ndim, groups, LANES), F32),
            pltpu.VMEM((2, n, ndim, groups, LANES), F32),
            pltpu.VMEM((2, ndim, groups, LANES), F32),
            pltpu.VMEM((8, width), F32),
            pltpu.VMEM((8, width), F32),
            pltpu.VMEM((rows, zw), BF16),
            pltpu.VMEM((8, zw), F32),
            pltpu.VMEM((3, BLOCK, BLOCK), F32),
            pltpu.VMEM((ndim, groups, LANES), F32),
            pltpu.VMEM((ndim, groups, LANES), F32),
            pltpu.VMEM((ndim, groups, LANES), F32),
            pltpu.SemaphoreType.DMA((3,)),
            pltpu.SemaphoreType.DMA,
            pltpu.SemaphoreType.DMA((20,)),
            pltpu.SemaphoreType.DMA((7,)),
            pltpu.SemaphoreType.DMA((7,)),
            pltpu.SemaphoreType.DMA((2, n)),
            pltpu.SemaphoreType.DMA((2, n)),
            pltpu.SemaphoreType.DMA((2, 2, 6)),
            pltpu.SemaphoreType.DMA((2, 2, 6)),
        ],
        compiler_params=pltpu.CompilerParams(
            collective_id=0, has_side_effects=True, vmem_limit_bytes=VMEM_LIMIT
        ),
        name="relay",
    )(x, c, gain, omega, fgain, raw, qk, wz, w1, w2)


def reduce_kernel(
    n, nd, schedule,
    l_h, r_h, all_h, w1h, w2h, xs_h, gs_h, gxn_h, xx_h, cd_h, gp_h,
    h0, zg, misc, raw, gain,
    red_h, ig_h, sm_h, out_h,
    recvs, lv, rv, part, acc, zr1, zr2, xs, gs, gxn, xx, cd, gp, tl, tr, carry, sm, smr, smz, wzp, wzr, wzz, q_r, w_r, qt_r,
    l_sem, r_sem, e_sem, x_s, x_r, z_s, z_r, o_sem, t_s, t_r, m_s, m_r, mo_sem, a_sem, w_sem, d_s, d_r, u_s, u_r, ready,
):
    sec = lax.axis_index("section")
    seq = lax.axis_index("seq")
    dp = lax.axis_index("dp")
    steps = n.bit_length() - 1
    rows, width = gxn.shape
    block_rows = width // n
    pairs = part.shape[0] // (2 * width)
    recompute = all_h.shape[1] > 1
    tok = rows // 2
    groups = width // LANES
    ndim = q_r.shape[0]
    set_rates(raw, rows // 2, q_r, w_r, qt_r)
    bit_orders = [
        [(s + color * (steps // 2)) % max(steps, 1) for s in range(steps)] for color in range(2)
    ]
    inner = (dp > 0) & (dp < nd - 1)
    outer_peer = jnp.where(dp < nd // 2, dp - 1, dp + 1)
    middle_peer = jnp.where(dp < nd // 2, dp + 1, dp - 1)

    def at_rows(ref, index, size):
        return ref.at[pl.ds(pl.multiple_of(index * size, size), size)]

    def part_at(t, color, p=0, count=1):
        start = ((t * 2 + color) * n + p) * block_rows
        return part.at[pl.ds(pl.multiple_of(start, block_rows), count * block_rows)]

    def recv_at(t, color, s, p=0, count=None):
        half = n >> (s + 1)
        start = ((t * 2 + color) * half + p) * block_rows
        return recvs[s].at[
            pl.ds(pl.multiple_of(start, block_rows), (count or half) * block_rows)
        ]

    def z_at(ref, t, color):
        return at_rows(ref, t * 2 + color, block_rows)

    def load_r(t, color):
        at = pl.ds(pl.multiple_of((t + color * pairs) * CH, CH), CH)
        return pltpu.make_async_copy(
            r_h.at[:, at], rv.at[lax.rem(t, 2), color], r_sem.at[lax.rem(t, 2), color]
        )

    for color in range(2):
        load_r(0, color).start()

    load_l = pltpu.make_async_copy(l_h, lv, l_sem)

    @pl.when((sec == 0) | (not recompute))
    def _():
        load_l.start()

    barrier = pltpu.get_barrier_semaphore()
    for k in range(1, n):
        pl.semaphore_signal(
            barrier, inc=1, device_id={"seq": lax.rem(seq + k, n)}, device_id_type=MESH
        )

    @pl.when(dp > 0)
    def _():
        pl.semaphore_signal(barrier, inc=1, device_id={"dp": dp - 1}, device_id_type=MESH)

    @pl.when(dp < nd - 1)
    def _():
        pl.semaphore_signal(barrier, inc=1, device_id={"dp": dp + 1}, device_id_type=MESH)

    @pl.when(sec == 1)
    def _():
        pl.semaphore_signal(barrier, inc=1, device_id={"section": 0}, device_id_type=MESH)

    def block_at(color, p):
        blk = seq
        for s in range(steps):
            if (p >> (steps - 1 - s)) & 1:
                blk = flip(blk, bit_orders[color][s])
        return blk

    def xy_copy(t, color, s):
        half = n >> (s + 1)
        return pltpu.make_async_remote_copy(
            src_ref=part_at(t, color, half, half),
            dst_ref=recv_at(t, color, s),
            send_sem=x_s.at[s, t, color],
            recv_sem=x_r.at[s, t, color],
            device_id={"seq": flip(seq, bit_orders[color][s])},
            device_id_type=MESH,
        )

    def z_copy(k, t, color):
        src, dst, peer = (
            (part_at(t, color), zr1, middle_peer),
            (part_at(t, color), zr2, middle_peer),
            (z_at(zr1, t, color), zr2, outer_peer),
        )[k]
        return pltpu.make_async_remote_copy(
            src_ref=src, dst_ref=z_at(dst, t, color),
            send_sem=z_s.at[0 if k < 2 else 1, t, color], recv_sem=z_r.at[min(k, 1), t, color],
            device_id={"dp": peer}, device_id_type=MESH,
        )

    def store(src, t, color):
        at = pl.ds(pl.multiple_of(t * CH, CH), CH)
        return pltpu.make_async_copy(src, red_h.at[color, :, at], o_sem.at[t, color])

    def launch(copy, t):
        @pl.when(t >= WINDOW)
        def _():
            copy(t - WINDOW).wait_send()

        copy(t).start()

    def produce(t, color):
        @pl.when(t + 1 < pairs)
        def _():
            load_r(t + 1, color).start()

        load_r(t, color).wait()
        slot = 2 if color else lax.div(t, pairs // 2)
        right = rv[lax.rem(t, 2), color]
        for p in range(n - 1, -1, -1):
            left = lv[slot, aligned(block_at(color, p), block_rows), :]
            part_at(t, color, p)[...] = dot(left, right).astype(BF16)
            if steps and p == n // 2:
                launch(lambda u: xy_copy(u, color, 0), t)

    def add_into(total, term):
        total[...] = total[...] + term[...]

    def token_block(what, g, half):
        return recvs[0].at[pl.ds(pl.multiple_of(((what * n + g) * 2 + half) * rows, rows), rows)]

    def token_copy(what, g, half):
        return pltpu.make_async_copy(
            all_h.at[what, g, :, pl.ds(half * CH, CH)], token_block(what, g, half),
            a_sem.at[what, g, half],
        )

    def weight_at(t, which):
        return recvs[1].at[
            pl.ds(pl.multiple_of((lax.rem(t, 2) * 2 + which) * width, width), width)
        ]

    def weight_copy(t, which):
        return pltpu.make_async_copy(
            (w1h, w2h)[which].at[:, pl.ds(pl.multiple_of(t * CH, CH), CH)], weight_at(t, which),
            w_sem.at[lax.rem(t, 2), which],
        )

    def own_rows(what, g):
        return part_at(g, what, 1)

    def hidden_at(which):
        return part_at(0, which, 2, rows // block_rows)

    def recompute_start():
        for which in range(2):
            weight_copy(0, which).start()
        for g in range(n):
            for what in range(2):
                for half in range(2):
                    token_copy(what, g, half).start()
        pltpu.make_async_copy(gp_h, gp, e_sem.at[5]).start()

    def prepare_group(g):
        for what in range(2):
            for half in range(2):
                token_copy(what, g, half).wait()
            column = seq * block_rows
            block = token_block(what, g, lax.div(column, CH))
            own = block[:, pl.ds(pl.multiple_of(lax.rem(column, CH), block_rows), block_rows)]
            own_rows(what, g)[...] = own.T

    def recompute_piece(t, g):
        @pl.when(t == 0)
        def _():
            prepare_group(g)

        if g == 0:

            @pl.when(t + 1 < pairs)
            def _():
                for which in range(2):
                    load_r(t + 1, which).start()
                    weight_copy(t + 1, which).start()

            for which in range(2):
                load_r(t, which).wait()
                weight_copy(t, which).wait()
                acc[which] = dot(own_rows(which, 0)[...], rv[lax.rem(t, 2), which])
        else:
            w1c, w2c = weight_at(t, 0), weight_at(t, 1)
            pre = dot(token_block(0, g, 0)[...], w1c[0:CH, :]) + dot(
                token_block(0, g, 1)[...], w1c[CH:, :]
            )
            sig = jax.nn.sigmoid(pre)
            hidden_at(1)[...] = (pre * sig).astype(BF16)
            slope = sig * (1.0 + pre * (1.0 - sig))
            grad = dot(token_block(1, g, 0)[...], w2c[0:CH, :]) + dot(
                token_block(1, g, 1)[...], w2c[CH:, :]
            )
            hidden_at(0)[...] = (grad * slope).astype(BF16)
            for which in range(2):
                acc[which] += dot(own_rows(which, g)[...], hidden_at(which)[...])
        if g == n - 1:
            for which in range(2):
                part_at(t, which)[...] = acc[which].astype(BF16)

    def output_load(c):
        if c == 0:
            pltpu.make_async_copy(gp_h, gp, e_sem.at[5]).wait()
            gxn[...] = gp[...].astype(F32)
        load_r(c, 1).start()
        weight_copy(c, 1).start()

    def output_chunk(c):
        load_r(c, 1).wait()
        weight_copy(c, 1).wait()
        gxn[...] += dot_nt(rv[c % 2, 1], weight_at(c, 1)[...])
        if c + 1 < pairs:
            output_load(c + 1)
        else:
            pl.semaphore_wait(ready, 1)
            own_output().start()
            give_output().start()

    def absorb(t, color, s):
        half = n >> (s + 1)
        xy_copy(t, color, s).wait_recv()
        for p in range(half - 1, -1, -1):
            add_into(part_at(t, color, p), recv_at(t, color, s, p, 1))
            if s + 1 < steps and p == half // 2:
                launch(lambda u: xy_copy(u, color, s + 1), t)

    def z_first(t, color):
        @pl.when(jnp.logical_not(inner))
        def _():
            launch(lambda u: z_copy(0, u, color), t)

    def z_second(t, color):
        @pl.when(inner)
        def _():
            z_copy(0, t, color).wait_recv()
            add_into(part_at(t, color), z_at(zr1, t, color))
            launch(lambda u: z_copy(1, u, color), t)

    def z_third(t, color):
        @pl.when(inner)
        def _():
            z_copy(1, t, color).wait_recv()
            z_at(zr1, t, color)[...] = part_at(t, color)[...] + z_at(zr2, t, color)[...]
            launch(lambda u: z_copy(2, u, color), t)
            store(z_at(zr1, t, color), t, color).start()

    def z_last(t, color):
        @pl.when(jnp.logical_not(inner))
        def _():
            z_copy(2, t, color).wait_recv()
            store(z_at(zr2, t, color), t, color).start()

    z_stages = (z_first, z_second, z_third, z_last)

    def state_copy(k, way):
        return pltpu.make_async_remote_copy(
            src_ref=tl.at[way], dst_ref=tr.at[way, k],
            send_sem=t_s.at[way, k], recv_sem=t_r.at[way, k],
            device_id={"seq": seq + k if way == 0 else seq - k}, device_id_type=MESH,
        )

    def loads():
        return [
            pltpu.make_async_copy(src, dst, e_sem.at[k])
            for k, (src, dst) in enumerate(
                ((xs_h, xs), (gs_h, gs), (gxn_h, gxn), (xx_h, xx), (cd_h, cd), (gp_h, gp))
            )
        ]

    def channel_rows(t):
        return pl.ds(pl.multiple_of(t * groups, groups), groups)

    zeros = jnp.zeros((groups, LANES), F32)

    def ema_ends():
        for cp in loads()[:2]:
            cp.wait()
        q = [q_r[j] for j in range(ndim)]
        half = ndim // 2
        for m in range(2):
            for part_of in range(2):
                js = range(part_of * half, (part_of + 1) * half)

                def forth(i, state):
                    h, d = state
                    for u in range(8):
                        x = xs[channel_rows(m * tok + i * 8 + u), :]
                        d = tuple(q[j] * d[k] + h[k] for k, j in enumerate(js))
                        h = tuple(q[j] * h[k] + x for k, j in enumerate(js))
                    return h, d

                _, d = lax.fori_loop(
                    0, tok // 8, forth,
                    (tuple(h0[m, j] for j in js), tuple(zeros for _ in js)),
                )
                for k, j in enumerate(js):
                    tl[0, m, j] = d[k]

            def back(i, a):
                for u in range(8):
                    g = gs[channel_rows(m * tok + tok - 1 - (i * 8 + u)), :]
                    a = tuple(q[j] * a[j] + g for j in range(ndim))
                return a

            a = lax.fori_loop(0, tok // 8, back, tuple(zeros for _ in range(ndim)))
            for j in range(ndim):
                tl[1, m, j] = a[j]
        for way in range(2):
            for k in range(1, n):
                has = (seq + k < n) if way == 0 else (seq - k >= 0)
                gets = (seq - k >= 0) if way == 0 else (seq + k < n)

                @pl.when(has)
                def _():
                    state_copy(k, way).start()

                @pl.when(jnp.logical_not(gets))
                def _():
                    tr[way, k] = jnp.zeros(tr.shape[2:], F32)

    def ema_carries():
        for way in range(2):
            for k in range(1, n):
                gets = (seq - k >= 0) if way == 0 else (seq + k < n)

                @pl.when(gets)
                def _():
                    state_copy(k, way).wait_recv()

            for m in range(2):
                for j in range(ndim):
                    state = zeros
                    for k in range(n - 1, 0, -1):
                        state = state * qt_r[j] + tr[way, k, m, j]
                    carry[way, m, j] = state

    def ema_sums():
        half = ndim // 2
        for part_of in range(2):
            js = range(part_of * half, (part_of + 1) * half)
            q = [q_r[j] for j in js]
            total = tuple(zeros for _ in range(2 * half))
            for m in range(2):

                def forth(i, state):
                    h, d, s0, s1 = state
                    for u in range(4):
                        at = channel_rows(m * tok + i * 4 + u)
                        x, g = xs[at, :], gs[at, :]
                        d = tuple(q[k] * d[k] + h[k] for k in range(half))
                        h = tuple(q[k] * h[k] + x for k in range(half))
                        s0 = tuple(s0[k] + g * h[k] for k in range(half))
                        s1 = tuple(s1[k] + g * d[k] for k in range(half))
                    return h, d, s0, s1

                _, _, s0, s1 = lax.fori_loop(
                    0, tok // 4, forth,
                    (
                        tuple(h0[m, j] for j in js),
                        tuple(carry[0, m, j] for j in js),
                        total[:half],
                        total[half:],
                    ),
                )
                total = s0 + s1
            for k, j in enumerate(js):
                sm[pl.ds(width + j * groups, groups), :] = total[k]
                sm[pl.ds(width + (ndim + j) * groups, groups), :] = total[half + k]

    def ema_adjoint():
        q = [q_r[j] for j in range(ndim)]
        w = [w_r[j] for j in range(ndim)]
        for m in range(2):

            def back(i, a):
                for u in range(8):
                    at = channel_rows(m * tok + tok - 1 - (i * 8 + u))
                    g = gs[at, :]
                    a = tuple(q[j] * a[j] + g for j in range(ndim))
                    xs[at, :] = add_all(w[j] * a[j] for j in range(ndim))
                return a

            lax.fori_loop(0, tok // 8, back, tuple(carry[1, m, j] for j in range(ndim)))

    base = width + 2 * ndim * groups

    def own_grad():
        return pltpu.make_async_copy(gxn.at[pl.ds(0, tok)], ig_h, mo_sem.at[0])

    def to_sibling(src, dst, k):
        return pltpu.make_async_remote_copy(
            src_ref=src, dst_ref=dst, send_sem=d_s.at[k], recv_sem=d_r.at[k],
            device_id={"section": 1 - sec}, device_id_type=MESH,
        )

    def give_grad():
        return to_sibling(gxn.at[pl.ds(tok, tok)], ig_h, 0)

    def give_small():
        return to_sibling(sm, sm_h, 1)

    def give_output():
        return to_sibling(gxn.at[pl.ds(0, tok)], out_h, 2)

    def own_output():
        return pltpu.make_async_copy(gxn.at[pl.ds(tok, tok)], out_h, mo_sem.at[0])

    def input_grads():
        for cp in loads()[2:]:
            cp.wait()
        sm[pl.ds(base, 3 * groups), :] = misc[0 : 3 * groups, :]
        g = gain[...]

        def tile(i, total):
            at = aligned(i, TILE_SMALL)
            unit, factor = normed_rows(xx[at, :].astype(F32))
            grad = gxn[at, :] + from_channel_rows(xs, i * TILE_SMALL, TILE_SMALL, groups)
            gxn[at, :] = norm_back(grad, g, unit, factor) + gp[at, :].astype(F32) * cd[
                at, :
            ].astype(F32)
            return total + jnp.sum(grad * unit, axis=0, keepdims=True)

        total = lax.fori_loop(0, rows // TILE_SMALL, tile, jnp.zeros((1, width), F32))
        for j, piece in enumerate(rows_of(total)):
            sm[base + 3 * groups + j : base + 3 * groups + j + 1, :] = piece
        own_grad().start()
        give_grad().start()

    late = pl.ds(width, sm.shape[0] - width)

    def small_copy(k):
        return pltpu.make_async_remote_copy(
            src_ref=sm.at[late], dst_ref=smr.at[k], send_sem=m_s.at[k], recv_sem=m_r.at[k],
            device_id={"seq": flip(seq, k)}, device_id_type=MESH,
        )

    def small_z(k):
        dst, peer = ((0, middle_peer), (1, middle_peer), (1, outer_peer))[k]
        return pltpu.make_async_remote_copy(
            src_ref=sm.at[late], dst_ref=smz.at[dst],
            send_sem=m_s.at[steps + (0 if k < 2 else 1)],
            recv_sem=m_r.at[steps + min(k, 1)],
            device_id={"dp": peer}, device_id_type=MESH,
        )

    def small_add(k):
        small_copy(k).wait()
        sm[late, :] += smr[k]
        if k + 1 < steps:
            small_copy(k + 1).start()

    def small_z_first():
        @pl.when(jnp.logical_not(inner))
        def _():
            small_z(0).start()

    def small_z_second():
        @pl.when(inner)
        def _():
            small_z(0).wait_recv()
            sm[late, :] += smz[0]
            small_z(1).start()

    def small_z_third():
        @pl.when(inner)
        def _():
            small_z(1).wait()
            sm[late, :] += smz[1]
            small_z(2).start()

    def small_z_last():
        @pl.when(jnp.logical_not(inner))
        def _():
            small_z(0).wait_send()
            small_z(2).wait_recv()
            sm[late, :] = smz[1]

    def wz_rows(p, count=1):
        return pl.ds(p * block_rows, count * block_rows)

    def wz_start():
        for p in range(n):
            wzp[wz_rows(p), :] = zg[aligned(block_at(0, p), block_rows), :]
        if steps:
            wz_copy(0).start()

    def wz_copy(s):
        half = n >> (s + 1)
        return pltpu.make_async_remote_copy(
            src_ref=wzp.at[wz_rows(half, half)], dst_ref=wzr.at[wz_rows(half, half)],
            send_sem=u_s.at[s], recv_sem=u_r.at[s],
            device_id={"seq": flip(seq, bit_orders[0][s])}, device_id_type=MESH,
        )

    def wz_add(s):
        half = n >> (s + 1)
        wz_copy(s).wait()
        wzp[wz_rows(0, half), :] += wzr[wz_rows(half, half), :]
        if s + 1 < steps:
            wz_copy(s + 1).start()

    def wz_z(k):
        dst, peer = ((0, middle_peer), (1, middle_peer), (1, outer_peer))[k]
        return pltpu.make_async_remote_copy(
            src_ref=wzp.at[wz_rows(0)], dst_ref=wzz.at[dst],
            send_sem=u_s.at[2 * steps + (0 if k < 2 else 1)],
            recv_sem=u_r.at[2 * steps + min(k, 1)],
            device_id={"dp": peer}, device_id_type=MESH,
        )

    def wz_z_first():
        @pl.when(jnp.logical_not(inner))
        def _():
            wz_z(0).start()

    def wz_z_second():
        @pl.when(inner)
        def _():
            wz_z(0).wait_recv()
            wzp[wz_rows(0), :] += wzz[0]
            wz_z(1).start()

    def wz_z_third():
        @pl.when(inner)
        def _():
            wz_z(1).wait()
            wzp[wz_rows(0), :] += wzz[1]
            wz_z(2).start()

    def wz_z_last():
        @pl.when(jnp.logical_not(inner))
        def _():
            wz_z(0).wait_send()
            wz_z(2).wait_recv()
            wzp[wz_rows(0), :] = wzz[1]

        if steps:
            wz_back(steps - 1).start()

    def wz_back(s):
        half = n >> (s + 1)
        return pltpu.make_async_remote_copy(
            src_ref=wzp.at[wz_rows(0, half)], dst_ref=wzp.at[wz_rows(half, half)],
            send_sem=u_s.at[steps + s], recv_sem=u_r.at[steps + s],
            device_id={"seq": flip(seq, bit_orders[0][s])}, device_id_type=MESH,
        )

    def wz_spread(s):
        wz_back(s).wait()
        if s:
            wz_back(s - 1).start()

    def small_end():
        for p in range(n):
            sm[aligned(block_at(0, p), block_rows), :] = wzp[wz_rows(p), :]
        own_small().start()
        give_small().start()

    def own_small():
        return pltpu.make_async_copy(sm, sm_h, mo_sem.at[1])

    sum_lag, z_lag, z_lag_1, mega_at, wz_at = schedule
    mega_work = [
        lambda: [cp.start() for cp in loads()], ema_ends, ema_carries, ema_sums, ema_adjoint, input_grads
    ]
    mega_ticks = list(mega_at)
    if steps:
        mega_work.append(lambda: small_copy(0).start())
        mega_ticks.append(mega_ticks[-1])
    for stage in [functools.partial(small_add, k) for k in range(steps)] + [
        small_z_first, small_z_second, small_z_third, small_z_last
    ]:
        mega_work.append(stage)
        mega_ticks.append(mega_ticks[-1] + (stage != small_z_first))
    last = mega_ticks[-1]
    at = wz_at
    for stage in (
        [wz_start]
        + [functools.partial(wz_add, s) for s in range(steps)]
        + [wz_z_first, wz_z_second, wz_z_third, wz_z_last]
        + [functools.partial(wz_spread, s) for s in range(steps - 1, -1, -1)]
    ):
        mega_work.append(stage)
        mega_ticks.append(at)
        at += stage not in (wz_z_first,)
    mega_work.append(small_end)
    mega_ticks.append(max(last, at))

    sum_stages = [(0, produce)]
    for s in range(steps):
        sum_stages.append(((s + 1) * sum_lag, functools.partial(absorb, s=s)))
    for lag, stage in zip(z_lag, z_stages):
        sum_stages.append((steps * sum_lag + lag, stage))
    sum_ticks = 2 * pairs + sum_stages[-1][0]

    def sum_tick(pair, parity):
        for lag, stage in sum_stages:
            t = pair + (parity - lag) // 2

            @pl.when((t >= 0) & (t < pairs))
            def _():
                stage(t, (parity - lag) % 2)

    def sum_pair(pair):
        for parity in range(2):
            sum_tick(pair, parity)

    def mega_pair(pair):
        for parity in range(2):
            sum_tick(pair, parity)
            for when in sorted(set(mega_ticks)):
                if when % 2 == parity:
                    work = [f for f, m in zip(mega_work, mega_ticks) if m == when]

                    @pl.when(pair == when // 2)
                    def _():
                        for f in work:
                            f()

    recompute_stages = [
        (n + color * (n // 2) + lag, color, stage)
        for color in range(2)
        for lag, stage in zip(z_lag_1, z_stages)
    ]
    recompute_pairs = pairs + max(lag for lag, _, _ in recompute_stages) // n + 1

    def recompute_pair(pair):
        for g in range(n):

            @pl.when(pair < pairs)
            def _():
                recompute_piece(pair, g)

            for lag, color, stage in recompute_stages:
                if lag % n == g:
                    t = pair - lag // n

                    @pl.when((t >= 0) & (t < pairs))
                    def _():
                        stage(t, color)

            if g == n - 1:

                @pl.when(pair == pairs - 1)
                def _():
                    output_load(0)

            for c in range(pairs):
                if c % n == g:

                    @pl.when(pair == pairs + c // n)
                    def _():
                        output_chunk(c)

    def drain(summed):
        def sent(i):
            t = pairs - WINDOW + i
            for color in range(2):
                if summed:
                    for s in range(steps):
                        xy_copy(t, color, s).wait_send()

                @pl.when(inner)
                def _():
                    z_copy(1, t, color).wait_send()
                    z_copy(2, t, color).wait_send()

                @pl.when(jnp.logical_not(inner))
                def _():
                    z_copy(0, t, color).wait_send()

        def stored(t):
            for color in range(2):
                store(z_at(zr1, t, color), t, color).wait()

        loop(WINDOW, sent)
        loop(pairs, stored)

    if recompute:

        @pl.when(sec == 1)
        def _():
            recompute_start()

    pl.semaphore_wait(barrier, n - 1 + jnp.where(inner, 2, 1) + (1 - sec))

    @pl.when(sec == 0)
    def _():
        pl.semaphore_signal(ready, inc=1, device_id={"section": 1}, device_id_type=MESH)

    @pl.when(sec == 0)
    def _():
        load_l.wait()
        loop((max(sum_ticks, max(mega_ticks) + 1) + 1) // 2, mega_pair)
        drain(True)

    @pl.when(sec == 1)
    def _():
        if recompute:
            loop(max(recompute_pairs, pairs + (pairs + n - 1) // n), recompute_pair)
        else:
            load_l.wait()
            loop((sum_ticks + 1) // 2, sum_pair)
        drain(not recompute)

    @pl.when(sec == 0)
    def _():
        for way in range(2):
            for k in range(1, n):
                has = (seq + k < n) if way == 0 else (seq - k >= 0)

                @pl.when(has)
                def _():
                    state_copy(k, way).wait_send()

        @pl.when(inner)
        def _():
            small_z(2).wait_send()
            wz_z(2).wait_send()

        own_small().wait()
        give_small().wait_send()
        if recompute:
            give_output().wait_recv()

        own_grad().wait()
        give_grad().wait_send()

    @pl.when(sec == 1)
    def _():
        if recompute:
            own_output().wait()
            give_output().wait_send()
        else:
            pl.semaphore_wait(ready, 1)
        give_grad().wait_recv()
        give_small().wait_recv()


SCHEDULE = (2, (0, 2, 4, 6), (0, 3, 6, 9), (4, 6, 8, 9, 10, 11), 1)


def reduce_grads(n, nd, l, r, both, w1, w2, xs, gs, gxn, xx, cd, gp, h0, zg, misc, raw, gain):
    rows, width = gxn.shape
    groups = width // LANES
    ndim = raw.shape[1]
    ff = r.shape[1] // 2
    pairs = ff // CH
    block_rows = width // n
    steps = n.bit_length() - 1
    small_rows = width + 2 * ndim * groups + 4 * groups
    any_spec = pl.BlockSpec(memory_space=pl.ANY)
    vmem = pl.BlockSpec(memory_space=pltpu.VMEM)

    def kernel(*refs):
        fixed = refs[: 16 + 4]
        rest = list(refs[16 + 4 :])
        recvs = rest[:steps]
        reduce_kernel(n, nd, SCHEDULE, *fixed, recvs, *rest[steps:])

    return pl.pallas_call(
        kernel,
        out_shape=[
            jax.ShapeDtypeStruct((2, block_rows, ff), BF16),
            jax.ShapeDtypeStruct((rows // 2, width), F32),
            jax.ShapeDtypeStruct((small_rows, LANES), F32),
            jax.ShapeDtypeStruct((rows // 2, width), F32),
        ],
        in_specs=[any_spec] * 11 + [vmem] * 5,
        out_specs=[any_spec] * 4,
        scratch_shapes=[
            pltpu.VMEM((pairs * 2 * (n >> (s + 1)) * block_rows, CH), BF16) for s in range(steps)
        ]
        + [
            pltpu.VMEM((3, width, rows), BF16),
            pltpu.VMEM((2, 2, rows, CH), BF16),
            pltpu.VMEM((pairs * 2 * width, CH), BF16),
            pltpu.VMEM((2, block_rows, CH), F32),
            pltpu.VMEM((pairs * 2 * block_rows, CH), BF16),
            pltpu.VMEM((pairs * 2 * block_rows, CH), BF16),
            pltpu.VMEM((rows * groups, LANES), F32),
            pltpu.VMEM((rows * groups, LANES), F32),
            pltpu.VMEM((rows, width), F32),
            pltpu.VMEM((rows, width), BF16),
            pltpu.VMEM((rows, width), BF16),
            pltpu.VMEM((rows, width), BF16),
            pltpu.VMEM((2, 2, ndim, groups, LANES), F32),
            pltpu.VMEM((2, n, 2, ndim, groups, LANES), F32),
            pltpu.VMEM((2, 2, ndim, groups, LANES), F32),
            pltpu.VMEM((small_rows, LANES), F32),
            pltpu.VMEM((max(steps, 1), small_rows - width, LANES), F32),
            pltpu.VMEM((2, small_rows - width, LANES), F32),
            pltpu.VMEM((width, LANES), F32),
            pltpu.VMEM((width, LANES), F32),
            pltpu.VMEM((2, block_rows, LANES), F32),
            pltpu.VMEM((ndim, groups, LANES), F32),
            pltpu.VMEM((ndim, groups, LANES), F32),
            pltpu.VMEM((ndim, groups, LANES), F32),
            pltpu.SemaphoreType.DMA,
            pltpu.SemaphoreType.DMA((2, 2)),
            pltpu.SemaphoreType.DMA((6,)),
            pltpu.SemaphoreType.DMA((max(steps, 1), pairs, 2)),
            pltpu.SemaphoreType.DMA((max(steps, 1), pairs, 2)),
            pltpu.SemaphoreType.DMA((2, pairs, 2)),
            pltpu.SemaphoreType.DMA((2, pairs, 2)),
            pltpu.SemaphoreType.DMA((pairs, 2)),
            pltpu.SemaphoreType.DMA((2, n)),
            pltpu.SemaphoreType.DMA((2, n)),
            pltpu.SemaphoreType.DMA((steps + 2,)),
            pltpu.SemaphoreType.DMA((steps + 2,)),
            pltpu.SemaphoreType.DMA((2,)),
            pltpu.SemaphoreType.DMA((2, n, 2)),
            pltpu.SemaphoreType.DMA((2, 2)),
            pltpu.SemaphoreType.DMA((3,)),
            pltpu.SemaphoreType.DMA((3,)),
            pltpu.SemaphoreType.DMA((2 * steps + 2,)),
            pltpu.SemaphoreType.DMA((2 * steps + 2,)),
            pltpu.SemaphoreType.REGULAR,
        ],
        compiler_params=pltpu.CompilerParams(
            collective_id=1, has_side_effects=True, vmem_limit_bytes=VMEM_LIMIT
        ),
        name="reduce_grads",
    )(l, r, both, w1, w2, xs, gs, gxn, xx, cd, gp, h0, zg, misc, raw, gain)


def finish_kernel(
    coeff, seq_ref, red, w1, w2, sm_h, raw, gain, fgain, wz, qk, out_h, ig_h,
    first, second, z_o, qk_o, ema_o, norm_o, omega_o, ffn_o, out_o, ig_o,
    sm, sems,
):
    width, groups = wz.shape[0], gain.shape[1] // LANES
    ndim = raw.shape[1]
    load = pltpu.make_async_copy(sm_h, sm, sems)

    @pl.when(pl.program_id(0) == 0)
    def _():
        load.start()

    out_o[...] = out_h[...]
    ig_o[...] = ig_h[...]

    first[...] = red[0].astype(F32) + coeff * w1[...].astype(F32)
    second[...] = red[1].astype(F32) + coeff * w2[...].astype(F32)

    @pl.when(pl.program_id(0) == pl.num_programs(0) - 1)
    def _():
        load.wait()
        z_o[...] = sm[0:width, :] + coeff * wz[...].astype(F32)
        base = width + 2 * ndim * groups
        for j in range(groups):
            at = slice(j * LANES, (j + 1) * LANES)
            omega_o[:, at] = sm[base + j : base + j + 1, :]
            ffn_o[:, at] = sm[base + groups + j : base + groups + j + 1, :] + coeff * fgain[:, at]
            norm_o[:, at] = (
                sm[base + 3 * groups + j : base + 3 * groups + j + 1, :] + coeff * gain[:, at]
            )
        qk_o[...] = sm[base + 2 * groups : base + 2 * groups + 4, :] + coeff * qk[...]
        for j in range(ndim):
            sum_0 = sm[width + j * groups : width + (j + 1) * groups, :]
            sum_1 = sm[width + (ndim + j) * groups : width + (ndim + j + 1) * groups, :]
            alpha, damp = jax.nn.sigmoid(raw[0, j]), jax.nn.sigmoid(raw[1, j])
            inject = alpha * raw[2, j]
            inject_grad = raw[3, j] * sum_0
            decay_grad = raw[3, j] * inject * sum_1
            ema_o[0, j] = (inject_grad * raw[2, j] - decay_grad * damp) * alpha * (1.0 - alpha)
            ema_o[1, j] = -decay_grad * alpha * damp * (1.0 - damp)
            ema_o[2, j] = inject_grad * alpha
            ema_o[3, j] = inject * sum_0


def finish(coeff, seq, red, w1, w2, small, raw, gain, fgain, wz, qk, out, grad):
    block_rows, ff = red.shape[1:]
    any_spec = pl.BlockSpec(memory_space=pl.ANY)
    vmem = pl.BlockSpec(memory_space=pltpu.VMEM)
    tiles = block_rows // TILE_SMALL
    own = pl.BlockSpec((TILE_SMALL, ff), lambda j, s: (s[0] * tiles + j, 0))
    share = pl.BlockSpec((TILE_SMALL, ff), lambda j, s: (j, 0))
    rows = pl.BlockSpec((out.shape[0] // tiles, out.shape[1]), lambda j, s: (j, 0))

    def shape(dims):
        return jax.ShapeDtypeStruct(dims, F32)

    return pl.pallas_call(
        functools.partial(finish_kernel, coeff),
        grid_spec=pltpu.PrefetchScalarGridSpec(
            num_scalar_prefetch=1,
            grid=(tiles,),
            in_specs=[pl.BlockSpec((2, TILE_SMALL, ff), lambda j, s: (0, j, 0)), own, own]
            + [any_spec]
            + [vmem] * 5
            + [rows] * 2,
            out_specs=[share, share] + [vmem] * 6 + [rows] * 2,
            scratch_shapes=[
                pltpu.VMEM(small.shape, F32),
                pltpu.SemaphoreType.DMA,
            ],
        ),
        out_shape=[
            shape((block_rows, ff)),
            shape((block_rows, ff)),
            shape(wz.shape),
            shape(qk.shape),
            shape(raw.shape),
            shape(gain.shape),
            shape(gain.shape),
            shape(gain.shape),
            shape(out.shape),
            shape(grad.shape),
        ],
        compiler_params=pltpu.CompilerParams(vmem_limit_bytes=VMEM_LIMIT),
        name="finish",
    )(seq, red, w1, w2, small, raw, gain, fgain, wz, qk, out, grad)


def body(
    inputs, cotangent, norm_gain, first_pack, second_pack, w_z, qk_affine, ema_params, omega, ffn_gain
):
    n = lax.axis_size("seq")
    nd = lax.axis_size("dp")
    tok, width = inputs.shape[2:]
    groups = width // LANES
    ndim = ema_params.shape[2]

    raw = jnp.swapaxes(ema_params, 1, 2).reshape(4, ndim, groups, LANES)

    def line(v):
        return v.reshape(1, width)

    l, r, xs, gs, gxn, xx, cd, gp, h0, block_output, both, zg, misc = relay(
        n, inputs[0, 0], cotangent[0, 0], line(norm_gain), line(omega), line(ffn_gain),
        raw, qk_affine, w_z, first_pack[0], second_pack[0],
    )
    red, input_grad, small, late_output = reduce_grads(
        n, nd, l, r, both, first_pack[0], second_pack[0], xs, gs, gxn, xx, cd, gp, h0, zg, misc,
        raw, line(norm_gain),
    )

    if n == RECOMPUTE_OVER:
        block_output = late_output
    coeff = DECAY * 2 * nd * n * tok
    grads = finish(
        coeff, lax.axis_index("seq").reshape(1), red, first_pack[0], second_pack[0],
        small, raw, line(norm_gain), line(ffn_gain), w_z, qk_affine, block_output, input_grad,
    )
    first, second, z_grad, qk_grad, ema_grad, norm_grad, omega_grad, ffn_grad, output, in_grad = grads
    return (
        output[None, None],
        in_grad[None, None],
        norm_grad.reshape(width),
        first[None],
        second[None],
        z_grad,
        qk_grad,
        jnp.swapaxes(ema_grad.reshape(4, ndim, width), 1, 2),
        omega_grad.reshape(width),
        ffn_grad.reshape(width),
    )


def solution(mesh):
    rows = P("section", "dp", "seq", None)
    packs = P("section", None, None)
    shares = P("section", "seq", None)
    return jax.shard_map(
        body,
        mesh=mesh,
        in_specs=(rows, rows, P(), packs, packs, P(), P(), P(), P(), P()),
        out_specs=(rows, rows, P(), shares, shares, P(), P(), P(), P(), P()),
        check_vma=False,
    )
```

```python
import functools

import jax
import jax.numpy as jnp
from jax import lax
from jax.experimental import pallas as pl
from jax.experimental.pallas import tpu as pltpu
from jax.sharding import PartitionSpec as P

MESH = pl.DeviceIdType.MESH
F32 = jnp.float32
BF16 = jnp.bfloat16
VALUE_WIDTH = 2048
BLOCK = 128
EPSILON = 1e-05
DECAY = 0.01
CH = 512
WINDOW = 4
SUM_WINDOW = 3
CUTS = 2
HIDDEN = 1024
TILE = 128
TILE_SMALL = 64
LANES = 128
VMEM_LIMIT = 60 * 1024 * 1024
RECOMPUTE_OVER = 4


def dot(a, b):
    return lax.dot_general(a, b, (((1,), (0,)), ((), ())), preferred_element_type=F32)


def dot_nt(a, b):
    return lax.dot_general(a, b, (((1,), (1,)), ((), ())), preferred_element_type=F32)


def normed_rows(v):
    center = v - jnp.mean(v, axis=-1, keepdims=True)
    factor = lax.rsqrt(jnp.mean(center * center, axis=-1, keepdims=True) + EPSILON)
    return center * factor, factor


def norm_back(grad, gain, unit, factor):
    s = grad * gain
    return factor * (
        s
        - jnp.mean(s, axis=-1, keepdims=True)
        - unit * jnp.mean(s * unit, axis=-1, keepdims=True)
    )


def loop(count, body, unroll=1):
    lax.fori_loop(0, count, lambda i, c: (body(i), c)[1], 0, unroll=unroll)


def aligned(i, size):
    return pl.ds(pl.multiple_of(i * size, size), size)


def to_channel_rows(ref, row, tile):
    groups = tile.shape[1] // LANES
    for sub in range(tile.shape[0] // 8):
        for j in range(groups):
            ref[pl.ds((row + 8 * sub) * groups + j, 8, stride=groups), :] = tile[
                8 * sub : 8 * sub + 8, j * LANES : (j + 1) * LANES
            ]


def from_channel_rows(ref, row, rows, groups):
    tiles = []
    for sub in range(rows // 8):
        tiles.append(
            jnp.concatenate(
                [
                    ref[pl.ds((row + 8 * sub) * groups + j, 8, stride=groups), :]
                    for j in range(groups)
                ],
                axis=1,
            )
        )
    return jnp.concatenate(tiles, axis=0)


def bit_of(value, bit):
    return lax.rem(lax.div(value, 1 << bit), 2)


def flip(value, bit):
    return value + (1 - 2 * bit_of(value, bit)) * (1 << bit)


def rows_of(values):
    return [values[:, j * LANES : (j + 1) * LANES] for j in range(values.shape[1] // LANES)]


def add_all(terms):
    terms = list(terms)
    while len(terms) > 1:
        terms = [a + b for a, b in zip(terms[::2], terms[1::2])] + (
            [terms[-1]] if len(terms) % 2 else []
        )
    return terms[0]


def set_rates(raw, steps, q_r, w_r, qt_r):
    for j in range(q_r.shape[0]):
        alpha = jax.nn.sigmoid(raw[0, j])
        decay = 1.0 - alpha * jax.nn.sigmoid(raw[1, j])
        q_r[j] = decay
        w_r[j] = raw[3, j] * (alpha * raw[2, j])
        power, base, left = None, decay, steps
        while left:
            if left & 1:
                power = base if power is None else power * base
            base, left = base * base, left >> 1
        qt_r[j] = power


def relay_kernel(
    n,
    x_own, c_own, gain, omega, fgain, raw, qk, wz, w1h, w2h,
    l_h, r_h, xs_h, gs_h, gxn_h, xx_h, cd_h, gp_h, h0_h, out_h, all_h, zg_o, misc_o,
    w1, w2, xc, xn, xs, rv, lv, vl, vsl, rs, ra, mlow, msl, cu, cc, cd, ps, gp,
    gm, zp, zs, zq, zk, pr, prl, tl, tr, h0, fg, fgr, gz, qks, tmp, q_r, w_r, qt_r,
    w_sem, in_sem, o_sem, d2d_s, d2d_r, t_s, t_r, a_s, a_r,
):
    sec = lax.axis_index("section")
    seq = lax.axis_index("seq")
    rows, width = xc.shape
    tok = rows // 2
    groups = width // LANES
    ndim = q_r.shape[0]
    set_rates(raw, tok, q_r, w_r, qt_r)
    ff = w1.shape[1]
    vw = VALUE_WIDTH
    blocks = tok // BLOCK
    zw = qk.shape[1]
    scale = zw**-0.5
    gates, cand_at = 2 * vw, 3 * vw + width
    recompute = all_h.shape[1] > 1
    halves = [pl.ds(m * tok, tok) for m in range(2)]

    barrier = pltpu.get_barrier_semaphore()
    pl.semaphore_signal(barrier, inc=1, device_id={"section": 1 - sec}, device_id_type=MESH)
    for k in range(1, n):
        pl.semaphore_signal(
            barrier, inc=1, device_id={"seq": lax.rem(seq + k, n)}, device_id_type=MESH
        )

    def to_sibling(src, dst, k):
        return pltpu.make_async_remote_copy(
            src_ref=src, dst_ref=dst, send_sem=d2d_s.at[k], recv_sem=d2d_r.at[k],
            device_id={"section": 1 - sec}, device_id_type=MESH,
        )

    def half_to_sibling(ref, m, k):
        return to_sibling(ref.at[halves[m]], ref.at[halves[m]], k + m)

    outs = []

    def out_copy(src, dst):
        cp = pltpu.make_async_copy(src, dst, o_sem.at[len(outs)])
        cp.start()
        outs.append(cp)
        return len(outs) - 1

    def load_weights(parts):
        loads = []
        for k, (src, dst, start, size) in enumerate(parts):
            at = pl.ds(start, size)
            cp = pltpu.make_async_copy(src.at[:, at], dst.at[:, at], w_sem.at[k])
            cp.start()
            loads.append(cp)
        return loads

    def tail_copy(m, k):
        return pltpu.make_async_remote_copy(
            src_ref=tl.at[m], dst_ref=tr.at[m, k], send_sem=t_s.at[m, k], recv_sem=t_r.at[m, k],
            device_id={"seq": seq + k}, device_id_type=MESH,
        )

    def gather_copies(what, src, m, hop):
        copies = []
        half = tok // 2
        for way in range(2):
            at = pl.ds(m * tok + way * half, half)
            first, second = (0, 1) if way == 0 else (1, 0)
            if hop == 0:
                moves = [(src.at[at], 1 << first, first, 0)]
            else:
                moves = [
                    (src.at[at], 1 << second, second, 1),
                    (all_h.at[what, 1 << first, at], 3, second, 2),
                ]
            for source, slot, bit, k in moves:
                copies.append(
                    pltpu.make_async_remote_copy(
                        src_ref=source, dst_ref=all_h.at[what, slot, at],
                        send_sem=a_s.at[what, m, way * 3 + k],
                        recv_sem=a_r.at[what, m, way * 3 + k],
                        device_id={"seq": flip(seq, bit)}, device_id_type=MESH,
                    )
                )
        return copies

    def gather_start(what, src, m):
        if recompute:
            for cp in gather_copies(what, src, m, 0):
                cp.start()

    def gather_forward(what, src, m):
        if recompute:
            for cp in gather_copies(what, src, m, 0):
                cp.wait_recv()
            for cp in gather_copies(what, src, m, 1):
                cp.start()

    def gather_end(what, src, m):
        if recompute:
            for cp in gather_copies(what, src, m, 0):
                cp.wait_send()
            for cp in gather_copies(what, src, m, 1):
                cp.wait()

    def tiles(m, body):
        count = tok // TILE
        loop(count, lambda i: body(i + m * count))

    def transpose_into(slot, src, m):
        def one(j):
            lv[slot, aligned(j, LANES), halves[m]] = src[halves[m], aligned(j, LANES)].T

        loop(width // LANES, one)

    def normalise(m):
        g = gain[...]

        def norm_tile(i):
            unit, _ = normed_rows(xc[aligned(i, TILE), :].astype(F32))
            tile = unit * g
            xn[aligned(i, TILE), :] = tile
            mlow[aligned(i, TILE), :] = tile.astype(BF16)
            to_channel_rows(xs, i * TILE, tile)

        tiles(m, norm_tile)

    def channel_rows(t):
        return pl.ds(pl.multiple_of(t * groups, groups), groups)

    def local_states(m):
        q = [q_r[j] for j in range(ndim)]

        def step(i, h):
            for u in range(8):
                x = xs[channel_rows(m * tok + i * 8 + u), :]
                h = tuple(q[j] * h[j] + x for j in range(ndim))
            return h

        zeros = jnp.zeros((groups, LANES), F32)
        h = lax.fori_loop(0, tok // 8, step, tuple(zeros for _ in range(ndim)))
        for j in range(ndim):
            tl[m, j] = h[j]

    def send_states(m):
        for k in range(1, n):

            @pl.when(seq + k < n)
            def _():
                tail_copy(m, k).start()

            @pl.when(seq - k < 0)
            def _():
                tr[m, k] = jnp.zeros(tr.shape[2:], F32)

    def values(m):
        at_m = halves[m]
        transpose_into(0, mlow, m)

        def value_chunk(c):
            pre = dot(mlow[at_m, :], w1[:, aligned(c, CH)])
            sig = jax.nn.sigmoid(pre)
            vl[at_m, aligned(c, CH)] = (pre * sig).astype(BF16)
            vsl[at_m, aligned(c, CH)] = (sig * (1.0 + pre * (1.0 - sig))).astype(BF16)

        loop(vw // CH, value_chunk)

    def start_states(m):
        for k in range(1, n):

            @pl.when(seq - k >= 0)
            def _():
                tail_copy(m, k).wait_recv()

        for j in range(ndim):
            state = jnp.zeros((groups, LANES), F32)
            for k in range(n - 1, 0, -1):
                state = state * qt_r[j] + tr[m, k, j]
            h0[m, j] = state
        out_copy(h0.at[m], h0_h.at[m])

    def smooth(m):
        q = [q_r[j] for j in range(ndim)]
        w = [w_r[j] for j in range(ndim)]

        def step(i, h):
            for u in range(8):
                at = channel_rows(m * tok + i * 8 + u)
                x = xs[at, :]
                h = tuple(q[j] * h[j] + x for j in range(ndim))
                xs[at, :] = add_all(w[j] * h[j] for j in range(ndim))
            return h

        lax.fori_loop(0, tok // 8, step, tuple(h0[m, j] for j in range(ndim)))
        om = omega[...]

        def mixed_tile(i):
            pre = from_channel_rows(xs, i * TILE, TILE, groups) + om * xn[aligned(i, TILE), :]
            sig = jax.nn.sigmoid(pre)
            mlow[aligned(i, TILE), :] = (pre * sig).astype(BF16)
            msl[aligned(i, TILE), :] = (sig * (1.0 + pre * (1.0 - sig))).astype(BF16)

        tiles(m, mixed_tile)

    def attention(m):
        at_m = halves[m]
        tmz = dot(mlow[at_m, :], wz[...])
        sig = jax.nn.sigmoid(tmz)
        zpart = tmz * sig
        zp[at_m, :] = zpart
        zs[at_m, :] = sig * (1.0 + tmz * (1.0 - sig))
        zq[at_m, :] = (zpart * qk[0:1, :] + qk[1:2, :]).astype(BF16)
        zk[at_m, :] = (zpart * qk[2:3, :] + qk[3:4, :]).astype(BF16)
        row_ids = lax.broadcasted_iota(jnp.int32, (BLOCK, BLOCK), 0)
        col_ids = lax.broadcasted_iota(jnp.int32, (BLOCK, BLOCK), 1)
        for b in range(blocks):
            at = pl.ds(m * tok + b * BLOCK, BLOCK)
            scores = jnp.where(row_ids >= col_ids, dot_nt(zq[at, :], zk[at, :]) * scale, -1e30)
            expo = jnp.exp(scores - jnp.max(scores, axis=-1, keepdims=True))
            probs = expo / jnp.sum(expo, axis=-1, keepdims=True)
            pr[at, :] = probs
            prl[at, :] = probs.astype(BF16)

    def gate(m):
        at_m = halves[m]

        def reset_chunk(c):
            at = aligned(c, CH)
            pre = dot(mlow[at_m, :], w2[:, at])
            for b in range(blocks):
                part = pl.ds(m * tok + b * BLOCK, BLOCK)
                att = dot(prl[part, :], vl[part, at])
                p = pre[b * BLOCK : (b + 1) * BLOCK]
                sig = jax.nn.sigmoid(p)
                reset = p * sig
                rs[part, at] = reset.astype(BF16)
                ra[part, at] = (att * (sig * (1.0 + p * (1.0 - sig)))).astype(BF16)
                rv[part, aligned(c + vw // CH, CH)] = (reset * att).astype(BF16)

        loop(vw // CH, reset_chunk)

    def finish(m):
        at_m = halves[m]

        def cand_chunk(c):
            at = aligned(c, CH)
            update = jax.nn.sigmoid(dot(mlow[at_m, :], w2[:, aligned(c + vw // CH, CH)]))
            gm[at_m, at] = dot(mlow[at_m, :], w2[:, aligned(c + (vw + width) // CH, CH)])
            cand = gm[at_m, at] + dot_nt(rv[at_m, vw : 2 * vw], w1[at, vw : 2 * vw])
            x = xc[at_m, at].astype(F32)
            sig = jax.nn.sigmoid(cand)
            hidden = cand * sig
            keep = 1.0 - update
            ps[at_m, at] = (update * hidden + keep * x).astype(BF16)
            cu[at_m, at] = ((hidden - x) * update * keep).astype(BF16)
            cc[at_m, at] = (update * (sig * (1.0 + cand * (1.0 - sig)))).astype(BF16)
            cd[at_m, at] = keep.astype(BF16)

        loop(width // CH, cand_chunk)

    def backward(m):
        at_m = halves[m]
        first = m * blocks

        def direct_tile(i):
            at = aligned(i, TILE)
            grad = gp[at, :].astype(F32)
            rv[at, 3 * vw : cand_at] = (grad * cu[at, :].astype(F32)).astype(BF16)
            rv[at, cand_at:] = (grad * cc[at, :].astype(F32)).astype(BF16)

        tiles(m, direct_tile)

        def gated_chunk(c):
            at = aligned(c, CH)
            grad = dot(rv[at_m, cand_at:], w1[:, aligned(c + vw // CH, CH)])
            rv[at_m, aligned(c + gates // CH, CH)] = (grad * ra[at_m, at].astype(F32)).astype(BF16)
            rs[at_m, at] = (grad * rs[at_m, at].astype(F32)).astype(BF16)

        loop(vw // CH, gated_chunk)

        def attention_back(b):
            at = aligned(first + b, BLOCK)
            probs = pr[at, :]
            tmp[0] = dot_nt(rs[at, :], vl[at, :])
            grad_probs = tmp[0]
            grad_scores = probs * (
                grad_probs - jnp.sum(grad_probs * probs, axis=-1, keepdims=True)
            )
            tmp[1] = dot(grad_scores.astype(BF16), zk[at, :])
            tmp[2] = dot(grad_scores.T.astype(BF16), zq[at, :])
            grad_query, grad_keys = tmp[1] * scale, tmp[2] * scale
            zpart = zp[at, :]
            for k, term in enumerate((grad_query * zpart, grad_query, grad_keys * zpart, grad_keys)):
                qks[k : k + 1, :] += jnp.sum(term, axis=0, keepdims=True)
            gz[at, :] = (
                (grad_query * qk[0:1, :] + grad_keys * qk[2:3, :]) * zs[at, :]
            ).astype(BF16)
            prl[at, :] = probs.T.astype(BF16)

        loop(blocks, attention_back)

        def grad_value_chunk(c):
            at = aligned(c, CH)
            for b in range(blocks):
                part = pl.ds((first + b) * BLOCK, BLOCK)
                rv[part, at] = (
                    dot(prl[part, :], rs[part, at]) * vsl[part, at].astype(F32)
                ).astype(BF16)

        loop(vw // CH, grad_value_chunk)
        out_copy(rv.at[at_m], r_h.at[at_m])
        transpose_into(1, rv.at[:, pl.ds(cand_at, width)], m)
        out_copy(lv.at[1, :, at_m], l_h.at[1, :, at_m])

        def mixed_chunk(c):
            at = aligned(c, CH)
            gm[at_m, at] = dot_nt(gz[at_m, :], wz[at, :])
            grad = (gm[at_m, at] + dot_nt(rv[at_m, gates:], w2[at, :])) * msl[at_m, at].astype(F32)
            fgr[0:1, at] += jnp.sum(grad * xn[at_m, at], axis=0, keepdims=True)
            xn[at_m, at] = grad * omega[:, at] + dot_nt(rv[at_m, 0:vw], w1[at, 0:vw])
            gm[at_m, at] = grad

        loop(width // CH, mixed_chunk)
        out_copy(xn.at[at_m], gxn_h.at[at_m])
        tiles(m, lambda i: to_channel_rows(xs, i * TILE, gm[aligned(i, TILE), :]))
        of_m = pl.ds(m * tok * groups, tok * groups)
        out_copy(xs.at[of_m], gs_h.at[of_m])

    def own_rows(src, m):
        return pltpu.make_async_copy(src, xc.at[halves[m]], in_sem)

    @pl.when(sec == 0)
    def _():
        own_rows(x_own, 0).start()
        load_weights(((w1h, w1, 0, vw), (w2h, w2, 0, ff), (w1h, w1, vw, vw)))
        own_rows(x_own, 0).wait()
        normalise(0)
        local_states(0)

    @pl.when(sec == 1)
    def _():
        own_rows(c_own, 1).start()
        load_weights(((w2h, w2, 0, ff), (w1h, w1, 0, ff)))

    pl.semaphore_wait(barrier, n)

    def wait_weights(k, src, dst, start, size):
        at = pl.ds(start, size)
        pltpu.make_async_copy(src.at[:, at], dst.at[:, at], w_sem.at[k]).wait()

    @pl.when(sec == 0)
    def _():
        give = to_sibling(c_own, xc.at[halves[0]], 0)
        give.start()
        fgr[...] = jnp.zeros_like(fgr)
        qks[...] = jnp.zeros_like(qks)
        send_states(0)
        give.wait()
        out_copy(xc, xx_h)
        normalise(1)
        local_states(1)
        send_states(1)
        saved = out_copy(xs, xs_h)
        wait_weights(0, w1h, w1, 0, vw)
        for m in range(2):
            values(m)
            start_states(m)
            if m == 0:
                outs[saved].wait()
                outs[saved] = None
            smooth(m)
            if m == 0:
                wait_weights(1, w2h, w2, 0, ff)
            attention(m)
            gate(m)
            if m == 0:
                wait_weights(2, w1h, w1, vw, vw)
            finish(m)
            half_to_sibling(ps, m, 1).start()
            transpose_into(2, mlow, m)
            for slot in (0, 2):
                out_copy(lv.at[slot, :, halves[m]], l_h.at[slot, :, halves[m]])
        out_copy(cd, cd_h)
        for m in range(2):
            half_to_sibling(gp, m, 3).wait_recv()
            backward(m)
        out_copy(gp, gp_h)
        zg_o[...] = dot(lv[2], gz[...])
        for j, part in enumerate(rows_of(fgr[0:1, :])):
            misc_o[j : j + 1, :] = part
        to_sibling(fg, fg, 5).wait_recv()
        for j, part in enumerate(rows_of(fg[0:1, :])):
            misc_o[groups + j : groups + j + 1, :] = part
        misc_o[2 * groups : 3 * groups, :] = qks[...]
        misc_o[3 * groups :, :] = jnp.zeros((groups, LANES), F32)
        if not recompute:
            to_sibling(out_h, out_h, 6).wait_recv()
        for m in range(2):
            half_to_sibling(ps, m, 1).wait_send()
            for k in range(1, n):

                @pl.when(seq + k < n)
                def _():
                    tail_copy(m, k).wait_send()

        for cp in outs:
            if cp is not None:
                cp.wait()

    outs.clear()

    @pl.when(sec == 1)
    def _():
        give = to_sibling(x_own, xc.at[halves[1]], 0)
        give.start()
        own_rows(c_own, 1).wait()
        wait_weights(0, w2h, w2, 0, ff)

        def active_chunk(c, m):
            rv[halves[m], aligned(c, CH)] = dot(xc[halves[m], :], w2[:, aligned(c, CH)]).astype(BF16)

        loop(ff // CH, lambda c: active_chunk(c, 1))
        give.wait()
        if recompute:
            out_copy(xc, all_h.at[1, 0])
        loop(ff // CH, lambda c: active_chunk(c, 0))
        for m in range(2):
            gather_start(1, xc, m)
        if not recompute:
            for m in range(2):
                transpose_into(2, xc, m)
        wait_weights(1, w1h, w1, 0, ff)
        fg[...] = jnp.zeros_like(fg)
        g = fgain[...]
        for m in range(2):
            gather_forward(1, xc, m)
        for m in range(2):
            at_m = halves[m]
            half_to_sibling(ps, m, 1).wait_recv()

            def norm_tile(i):
                at = aligned(i, TILE)
                unit, _ = normed_rows(ps[at, :].astype(F32))
                mlow[at, :] = (unit * g).astype(BF16)

            tiles(m, norm_tile)
            gather_start(0, mlow, m)
            xn[at_m, :] = jnp.zeros((tok, width), F32)

            def hidden_chunk(c):
                at = aligned(c, HIDDEN)
                pre = dot(mlow[at_m, :], w1[:, at])
                sig = jax.nn.sigmoid(pre)
                rv[at_m, aligned(c + ff // HIDDEN, HIDDEN)] = (pre * sig).astype(BF16)
                grad = (
                    rv[at_m, at].astype(F32) * (sig * (1.0 + pre * (1.0 - sig)))
                ).astype(BF16)
                rv[at_m, at] = grad
                xn[at_m, :] += dot_nt(grad, w1[:, at])

            loop(ff // HIDDEN, hidden_chunk, unroll=2)

            def back_tile(i):
                at = aligned(i, TILE)
                unit, factor = normed_rows(ps[at, :].astype(F32))
                grad = xn[at, :]
                fg[0:1, :] += jnp.sum(grad * unit, axis=0, keepdims=True)
                gp[at, :] = (
                    xc[at, :].astype(F32) + norm_back(grad, g, unit, factor)
                ).astype(BF16)

            tiles(m, back_tile)
            half_to_sibling(gp, m, 3).start()
            gather_forward(0, mlow, m)
        gains = to_sibling(fg, fg, 5)
        gains.start()
        out_copy(rv, r_h)
        sent = [gains] + [half_to_sibling(gp, m, 3) for m in range(2)]
        if recompute:
            out_copy(mlow, all_h.at[0, 0])
            out_copy(ps, gp_h)
        else:
            for slot in range(2):
                for m in range(2):
                    transpose_into(slot, mlow, m)
            out_copy(lv, l_h)

            def out_chunk(c):
                at = aligned(c, CH)
                xn[:, at] = ps[:, at].astype(F32) + dot_nt(rv[:, ff : 2 * ff], w2[at, :])

            loop(width // CH, out_chunk)
            result = to_sibling(xn.at[halves[0]], out_h, 6)
            result.start()
            sent.append(result)
            out_copy(xn.at[halves[1]], out_h)
        for cp in sent:
            cp.wait_send()
        for what, src in enumerate((mlow, xc)):
            for m in range(2):
                gather_end(what, src, m)
        for cp in outs:
            cp.wait()


def relay(n, x, c, gain, omega, fgain, raw, qk, wz, w1, w2):
    rows, width = 2 * x.shape[0], x.shape[1]
    ff, vw, zw = w1.shape[1], VALUE_WIDTH, wz.shape[1]
    groups = width // LANES
    ndim = raw.shape[1]
    any_spec = pl.BlockSpec(memory_space=pl.ANY)
    vmem = pl.BlockSpec(memory_space=pltpu.VMEM)

    def shape(dims, kind):
        return jax.ShapeDtypeStruct(dims, kind)

    outs = [
        (shape((3, width, rows), BF16), any_spec),
        (shape((rows, 2 * ff), BF16), any_spec),
        (shape((rows * groups, LANES), F32), any_spec),
        (shape((rows * groups, LANES), F32), any_spec),
        (shape((rows, width), F32), any_spec),
        (shape((rows, width), BF16), any_spec),
        (shape((rows, width), BF16), any_spec),
        (shape((rows, width), BF16), any_spec),
        (shape((2, ndim, groups, LANES), F32), any_spec),
        (shape((rows // 2, width), F32), any_spec),
        (shape((2, n if n == RECOMPUTE_OVER else 1, rows, width), BF16), any_spec),
        (shape((width, zw), F32), vmem),
        (shape((4 * groups, LANES), F32), vmem),
    ]
    return pl.pallas_call(
        functools.partial(relay_kernel, n),
        out_shape=[o[0] for o in outs],
        in_specs=[any_spec, any_spec] + [vmem] * 6 + [any_spec, any_spec],
        out_specs=[o[1] for o in outs],
        scratch_shapes=[
            pltpu.VMEM((width, ff), BF16),
            pltpu.VMEM((width, ff), BF16),
            pltpu.VMEM((rows, width), BF16),
            pltpu.VMEM((rows, width), F32),
            pltpu.VMEM((rows * groups, LANES), F32),
            pltpu.VMEM((rows, 2 * ff), BF16),
            pltpu.VMEM((3, width, rows), BF16),
            pltpu.VMEM((rows, vw), BF16),
            pltpu.VMEM((rows, vw), BF16),
            pltpu.VMEM((rows, vw), BF16),
            pltpu.VMEM((rows, vw), BF16),
            pltpu.VMEM((rows, width), BF16),
            pltpu.VMEM((rows, width), BF16),
            pltpu.VMEM((rows, width), BF16),
            pltpu.VMEM((rows, width), BF16),
            pltpu.VMEM((rows, width), BF16),
            pltpu.VMEM((rows, width), BF16),
            pltpu.VMEM((rows, width), BF16),
            pltpu.VMEM((rows, width), F32),
            pltpu.VMEM((rows, zw), F32),
            pltpu.VMEM((rows, zw), F32),
            pltpu.VMEM((rows, zw), BF16),
            pltpu.VMEM((rows, zw), BF16),
            pltpu.VMEM((rows, BLOCK), F32),
            pltpu.VMEM((rows, BLOCK), BF16),
            pltpu.VMEM((2, ndim, groups, LANES), F32),
            pltpu.VMEM((2, n, ndim, groups, LANES), F32),
            pltpu.VMEM((2, ndim, groups, LANES), F32),
            pltpu.VMEM((8, width), F32),
            pltpu.VMEM((8, width), F32),
            pltpu.VMEM((rows, zw), BF16),
            pltpu.VMEM((8, zw), F32),
            pltpu.VMEM((3, BLOCK, BLOCK), F32),
            pltpu.VMEM((ndim, groups, LANES), F32),
            pltpu.VMEM((ndim, groups, LANES), F32),
            pltpu.VMEM((ndim, groups, LANES), F32),
            pltpu.SemaphoreType.DMA((3,)),
            pltpu.SemaphoreType.DMA,
            pltpu.SemaphoreType.DMA((20,)),
            pltpu.SemaphoreType.DMA((7,)),
            pltpu.SemaphoreType.DMA((7,)),
            pltpu.SemaphoreType.DMA((2, n)),
            pltpu.SemaphoreType.DMA((2, n)),
            pltpu.SemaphoreType.DMA((2, 2, 6)),
            pltpu.SemaphoreType.DMA((2, 2, 6)),
        ],
        compiler_params=pltpu.CompilerParams(
            collective_id=0, has_side_effects=True, vmem_limit_bytes=VMEM_LIMIT
        ),
        name="relay",
    )(x, c, gain, omega, fgain, raw, qk, wz, w1, w2)


def reduce_kernel(
    n, nd, schedule,
    l_h, r_h, all_h, w1h, w2h, xs_h, gs_h, gxn_h, xx_h, cd_h, gp_h,
    h0, zg, misc, raw, gain,
    red_h, ig_h, sm_h, out_h,
    recvs, lv, rv, part, acc, zr1, zr2, xs, gs, gxn, xx, cd, gp, tl, tr, carry, sm, smr, smz, wzp, wzr, wzz, q_r, w_r, qt_r,
    l_sem, r_sem, e_sem, x_s, x_r, z_s, z_r, o_sem, t_s, t_r, m_s, m_r, mo_sem, a_sem, w_sem, d_s, d_r, u_s, u_r, ready,
):
    sec = lax.axis_index("section")
    seq = lax.axis_index("seq")
    dp = lax.axis_index("dp")
    steps = n.bit_length() - 1
    rows, width = gxn.shape
    block_rows = width // n
    pairs = part.shape[0] // (2 * width)
    recompute = all_h.shape[1] > 1
    tok = rows // 2
    groups = width // LANES
    ndim = q_r.shape[0]
    set_rates(raw, rows // 2, q_r, w_r, qt_r)
    bit_orders = [
        [(s + color * (steps // 2)) % max(steps, 1) for s in range(steps)] for color in range(2)
    ]
    inner = (dp > 0) & (dp < nd - 1)
    outer_peer = jnp.where(dp < nd // 2, dp - 1, dp + 1)
    middle_peer = jnp.where(dp < nd // 2, dp + 1, dp - 1)

    def at_rows(ref, index, size):
        return ref.at[pl.ds(pl.multiple_of(index * size, size), size)]

    def part_at(t, color, p=0, count=1):
        start = ((t * 2 + color) * n + p) * block_rows
        return part.at[pl.ds(pl.multiple_of(start, block_rows), count * block_rows)]

    def part_rows(s):
        return (n >> (s + 1)) * block_rows // CUTS

    def sent_at(t, color, s, i):
        size = part_rows(s)
        start = (t * 2 + color) * n * block_rows + (2 * CUTS - 1 - i) * size
        return part.at[pl.ds(pl.multiple_of(start, size), size)]

    def kept_at(t, color, s, i):
        size = part_rows(s)
        start = (t * 2 + color) * n * block_rows + (CUTS - 1 - i) * size
        return part.at[pl.ds(pl.multiple_of(start, size), size)]

    def recv_at(t, color, s, i):
        if s == 0:
            rows_at = pl.ds(pl.multiple_of((t * CUTS + i) * part_rows(0), part_rows(0)), part_rows(0))
            return recvs[0].at[rows_at, pl.ds(color * CH, CH)]
        return at_rows(recvs[s], (t * 2 + color) * CUTS + i, part_rows(s))

    piece = block_rows // CUTS
    pieces = 2 * pairs * CUTS

    def own_at(v):
        unit, i = lax.div(v, CUTS), lax.rem(v, CUTS)
        start = unit * n * block_rows + (CUTS - 1 - i) * piece
        return part.at[pl.ds(pl.multiple_of(start, piece), piece)]

    def z_at(ref, v):
        return at_rows(ref, v, piece)

    def load_r(t, color):
        at = pl.ds(pl.multiple_of((t + color * pairs) * CH, CH), CH)
        return pltpu.make_async_copy(
            r_h.at[:, at], rv.at[lax.rem(t, 2), color], r_sem.at[lax.rem(t, 2), color]
        )

    for color in range(2):
        load_r(0, color).start()

    load_l = pltpu.make_async_copy(l_h, lv, l_sem)

    @pl.when((sec == 0) | (not recompute))
    def _():
        load_l.start()

    barrier = pltpu.get_barrier_semaphore()
    for k in range(1, n):
        pl.semaphore_signal(
            barrier, inc=1, device_id={"seq": lax.rem(seq + k, n)}, device_id_type=MESH
        )

    @pl.when(dp > 0)
    def _():
        pl.semaphore_signal(barrier, inc=1, device_id={"dp": dp - 1}, device_id_type=MESH)

    @pl.when(dp < nd - 1)
    def _():
        pl.semaphore_signal(barrier, inc=1, device_id={"dp": dp + 1}, device_id_type=MESH)

    @pl.when(sec == 1)
    def _():
        pl.semaphore_signal(barrier, inc=1, device_id={"section": 0}, device_id_type=MESH)

    def block_at(color, p):
        blk = seq
        for s in range(steps):
            if (p >> (steps - 1 - s)) & 1:
                blk = flip(blk, bit_orders[color][s])
        return blk

    def xy_copy(t, color, s, i):
        return pltpu.make_async_remote_copy(
            src_ref=sent_at(t, color, s, i),
            dst_ref=recv_at(t, color, s, i),
            send_sem=x_s.at[s, color, t * CUTS + i],
            recv_sem=x_r.at[s, color, t * CUTS + i],
            device_id={"seq": flip(seq, bit_orders[color][s])},
            device_id_type=MESH,
        )

    def z_copy(k, v):
        src, dst, peer = (
            (own_at(v), zr1, middle_peer),
            (own_at(v), zr2, middle_peer),
            (z_at(zr1, v), zr2, outer_peer),
        )[k]
        return pltpu.make_async_remote_copy(
            src_ref=src, dst_ref=z_at(dst, v),
            send_sem=z_s.at[0 if k < 2 else 1, v], recv_sem=z_r.at[min(k, 1), v],
            device_id={"dp": peer}, device_id_type=MESH,
        )

    def store(ref, v):
        unit, i = lax.div(v, CUTS), lax.rem(v, CUTS)
        t, color = lax.div(unit, 2), lax.rem(unit, 2)
        rows_at = pl.ds(pl.multiple_of((CUTS - 1 - i) * piece, piece), piece)
        columns_at = pl.ds(pl.multiple_of(t * CH, CH), CH)
        return pltpu.make_async_copy(z_at(ref, v), red_h.at[color, rows_at, columns_at], o_sem.at[v])

    def launch_xy(t, color, s, i):
        @pl.when(t >= SUM_WINDOW)
        def _():
            xy_copy(t - SUM_WINDOW, color, s, i).wait_send()

        xy_copy(t, color, s, i).start()

    def launch_z(k, v):
        @pl.when(v >= WINDOW)
        def _():
            z_copy(k, v - WINDOW).wait_send()

        z_copy(k, v).start()

    def launch_next(t, color, s, i):
        if s < steps and i < CUTS // 2:
            for k in range(2):
                launch_xy(t, color, s, 2 * i + k)

    def produce(t, color, i):
        if i == 0:

            @pl.when(t + 1 < pairs)
            def _():
                load_r(t + 1, color).start()

            load_r(t, color).wait()
        slot = 2 if color else lax.div(t, pairs // 2)
        share = n // CUTS
        for p in range(n - 1 - i * share, n - 1 - (i + 1) * share, -1):
            left = lv[slot, aligned(block_at(color, p), block_rows), :]
            part_at(t, color, p)[...] = dot(left, rv[lax.rem(t, 2), color]).astype(BF16)
        launch_next(t, color, 0, i)

    def add_into(total, term):
        total[...] = total[...] + term[...]

    def token_block(what, g):
        return recvs[0].at[pl.ds(pl.multiple_of((what * n + g) * rows, rows), rows)]

    def token_copy(what, g):
        return pltpu.make_async_copy(all_h.at[what, g], token_block(what, g), a_sem.at[what, g])

    def weight_at(t, which):
        return recvs[1].at[
            pl.ds(pl.multiple_of((lax.rem(t, 2) * 2 + which) * width, width), width)
        ]

    def weight_copy(t, which):
        return pltpu.make_async_copy(
            (w1h, w2h)[which].at[:, pl.ds(pl.multiple_of(t * CH, CH), CH)], weight_at(t, which),
            w_sem.at[lax.rem(t, 2), which],
        )

    def own_rows(what, g):
        return part_at(g, what, 1)

    def hidden_at(which):
        return part_at(0, which, 2, rows // block_rows)

    def recompute_start():
        for which in range(2):
            weight_copy(0, which).start()
        for g in range(n):
            for what in range(2):
                token_copy(what, g).start()
        pltpu.make_async_copy(gp_h, gp, e_sem.at[5]).start()

    def prepare_group(g):
        for what in range(2):
            token_copy(what, g).wait()
            own = token_block(what, g)[:, aligned(seq, block_rows)]
            own_rows(what, g)[...] = own.T

    def recompute_piece(t, g):
        @pl.when(t == 0)
        def _():
            prepare_group(g)

        if g == 0:

            @pl.when(t + 1 < pairs)
            def _():
                for which in range(2):
                    load_r(t + 1, which).start()
                    weight_copy(t + 1, which).start()

            for which in range(2):
                load_r(t, which).wait()
                weight_copy(t, which).wait()
                acc[which] = dot(own_rows(which, 0)[...], rv[lax.rem(t, 2), which])
        else:
            w1c, w2c = weight_at(t, 0), weight_at(t, 1)
            pre = dot(token_block(0, g)[...], w1c[...])
            sig = jax.nn.sigmoid(pre)
            hidden_at(1)[...] = (pre * sig).astype(BF16)
            slope = sig * (1.0 + pre * (1.0 - sig))
            grad = dot(token_block(1, g)[...], w2c[...])
            hidden_at(0)[...] = (grad * slope).astype(BF16)
            for which in range(2):
                acc[which] += dot(own_rows(which, g)[...], hidden_at(which)[...])
        if g == n - 1:
            for which in range(2):
                part_at(t, which)[...] = acc[which].astype(BF16)

    def output_load(c):
        if c == 0:
            pltpu.make_async_copy(gp_h, gp, e_sem.at[5]).wait()
            gxn[...] = gp[...].astype(F32)
        load_r(c, 1).start()
        weight_copy(c, 1).start()

    def output_chunk(c):
        load_r(c, 1).wait()
        weight_copy(c, 1).wait()
        gxn[...] += dot_nt(rv[c % 2, 1], weight_at(c, 1)[...])
        if c + 1 < pairs:
            output_load(c + 1)
        else:
            pl.semaphore_wait(ready, 1)
            own_output().start()
            give_output().start()

    def absorb(t, color, i, s):
        xy_copy(t, color, s, i).wait_recv()
        add_into(kept_at(t, color, s, i), recv_at(t, color, s, i))
        launch_next(t, color, s + 1, i)

    def z_first(v):
        @pl.when(jnp.logical_not(inner))
        def _():
            launch_z(0, v)

    def z_second(v):
        @pl.when(inner)
        def _():
            z_copy(0, v).wait_recv()
            add_into(own_at(v), z_at(zr1, v))
            launch_z(1, v)

    def z_third(v):
        @pl.when(inner)
        def _():
            z_copy(1, v).wait_recv()
            z_at(zr1, v)[...] = own_at(v)[...] + z_at(zr2, v)[...]
            launch_z(2, v)
            store(zr1, v).start()

    def z_last(v):
        @pl.when(jnp.logical_not(inner))
        def _():
            z_copy(2, v).wait_recv()
            store(zr2, v).start()

    z_stages = (z_first, z_second, z_third, z_last)

    def state_copy(k, way):
        return pltpu.make_async_remote_copy(
            src_ref=tl.at[way], dst_ref=tr.at[way, k],
            send_sem=t_s.at[way, k], recv_sem=t_r.at[way, k],
            device_id={"seq": seq + k if way == 0 else seq - k}, device_id_type=MESH,
        )

    def loads():
        return [
            pltpu.make_async_copy(src, dst, e_sem.at[k])
            for k, (src, dst) in enumerate(
                ((xs_h, xs), (gs_h, gs), (gxn_h, gxn), (xx_h, xx), (cd_h, cd), (gp_h, gp))
            )
        ]

    def channel_rows(t):
        return pl.ds(pl.multiple_of(t * groups, groups), groups)

    zeros = jnp.zeros((groups, LANES), F32)

    def ema_ends():
        for cp in loads()[:2]:
            cp.wait()
        q = [q_r[j] for j in range(ndim)]
        half = ndim // 2
        for m in range(2):
            for part_of in range(2):
                js = range(part_of * half, (part_of + 1) * half)

                def forth(i, state):
                    h, d = state
                    for u in range(8):
                        x = xs[channel_rows(m * tok + i * 8 + u), :]
                        d = tuple(q[j] * d[k] + h[k] for k, j in enumerate(js))
                        h = tuple(q[j] * h[k] + x for k, j in enumerate(js))
                    return h, d

                _, d = lax.fori_loop(
                    0, tok // 8, forth,
                    (tuple(h0[m, j] for j in js), tuple(zeros for _ in js)),
                )
                for k, j in enumerate(js):
                    tl[0, m, j] = d[k]

            def back(i, a):
                for u in range(8):
                    g = gs[channel_rows(m * tok + tok - 1 - (i * 8 + u)), :]
                    a = tuple(q[j] * a[j] + g for j in range(ndim))
                return a

            a = lax.fori_loop(0, tok // 8, back, tuple(zeros for _ in range(ndim)))
            for j in range(ndim):
                tl[1, m, j] = a[j]
        for way in range(2):
            for k in range(1, n):
                has = (seq + k < n) if way == 0 else (seq - k >= 0)
                gets = (seq - k >= 0) if way == 0 else (seq + k < n)

                @pl.when(has)
                def _():
                    state_copy(k, way).start()

                @pl.when(jnp.logical_not(gets))
                def _():
                    tr[way, k] = jnp.zeros(tr.shape[2:], F32)

    def ema_carries():
        for way in range(2):
            for k in range(1, n):
                gets = (seq - k >= 0) if way == 0 else (seq + k < n)

                @pl.when(gets)
                def _():
                    state_copy(k, way).wait_recv()

            for m in range(2):
                for j in range(ndim):
                    state = zeros
                    for k in range(n - 1, 0, -1):
                        state = state * qt_r[j] + tr[way, k, m, j]
                    carry[way, m, j] = state

    def ema_sums():
        half = ndim // 2
        for part_of in range(2):
            js = range(part_of * half, (part_of + 1) * half)
            q = [q_r[j] for j in js]
            total = tuple(zeros for _ in range(2 * half))
            for m in range(2):

                def forth(i, state):
                    h, d, s0, s1 = state
                    for u in range(4):
                        at = channel_rows(m * tok + i * 4 + u)
                        x, g = xs[at, :], gs[at, :]
                        d = tuple(q[k] * d[k] + h[k] for k in range(half))
                        h = tuple(q[k] * h[k] + x for k in range(half))
                        s0 = tuple(s0[k] + g * h[k] for k in range(half))
                        s1 = tuple(s1[k] + g * d[k] for k in range(half))
                    return h, d, s0, s1

                _, _, s0, s1 = lax.fori_loop(
                    0, tok // 4, forth,
                    (
                        tuple(h0[m, j] for j in js),
                        tuple(carry[0, m, j] for j in js),
                        total[:half],
                        total[half:],
                    ),
                )
                total = s0 + s1
            for k, j in enumerate(js):
                sm[pl.ds(width + j * groups, groups), :] = total[k]
                sm[pl.ds(width + (ndim + j) * groups, groups), :] = total[half + k]

    def ema_adjoint():
        q = [q_r[j] for j in range(ndim)]
        w = [w_r[j] for j in range(ndim)]
        for m in range(2):

            def back(i, a):
                for u in range(8):
                    at = channel_rows(m * tok + tok - 1 - (i * 8 + u))
                    g = gs[at, :]
                    a = tuple(q[j] * a[j] + g for j in range(ndim))
                    xs[at, :] = add_all(w[j] * a[j] for j in range(ndim))
                return a

            lax.fori_loop(0, tok // 8, back, tuple(carry[1, m, j] for j in range(ndim)))

    base = width + 2 * ndim * groups

    def own_grad():
        return pltpu.make_async_copy(gxn.at[pl.ds(0, tok)], ig_h, mo_sem.at[0])

    def to_sibling(src, dst, k):
        return pltpu.make_async_remote_copy(
            src_ref=src, dst_ref=dst, send_sem=d_s.at[k], recv_sem=d_r.at[k],
            device_id={"section": 1 - sec}, device_id_type=MESH,
        )

    def give_grad():
        return to_sibling(gxn.at[pl.ds(tok, tok)], ig_h, 0)

    def give_small():
        return to_sibling(sm, sm_h, 1)

    def give_output():
        return to_sibling(gxn.at[pl.ds(0, tok)], out_h, 2)

    def own_output():
        return pltpu.make_async_copy(gxn.at[pl.ds(tok, tok)], out_h, mo_sem.at[0])

    def input_grads():
        for cp in loads()[2:]:
            cp.wait()
        sm[pl.ds(base, 3 * groups), :] = misc[0 : 3 * groups, :]
        g = gain[...]

        def tile(i, total):
            at = aligned(i, TILE_SMALL)
            unit, factor = normed_rows(xx[at, :].astype(F32))
            grad = gxn[at, :] + from_channel_rows(xs, i * TILE_SMALL, TILE_SMALL, groups)
            gxn[at, :] = norm_back(grad, g, unit, factor) + gp[at, :].astype(F32) * cd[
                at, :
            ].astype(F32)
            return total + jnp.sum(grad * unit, axis=0, keepdims=True)

        total = lax.fori_loop(0, rows // TILE_SMALL, tile, jnp.zeros((1, width), F32))
        for j, piece in enumerate(rows_of(total)):
            sm[base + 3 * groups + j : base + 3 * groups + j + 1, :] = piece
        own_grad().start()
        give_grad().start()

    late = pl.ds(width, sm.shape[0] - width)

    def small_copy(k):
        return pltpu.make_async_remote_copy(
            src_ref=sm.at[late], dst_ref=smr.at[k], send_sem=m_s.at[k], recv_sem=m_r.at[k],
            device_id={"seq": flip(seq, k)}, device_id_type=MESH,
        )

    def small_z(k):
        dst, peer = ((0, middle_peer), (1, middle_peer), (1, outer_peer))[k]
        return pltpu.make_async_remote_copy(
            src_ref=sm.at[late], dst_ref=smz.at[dst],
            send_sem=m_s.at[steps + (0 if k < 2 else 1)],
            recv_sem=m_r.at[steps + min(k, 1)],
            device_id={"dp": peer}, device_id_type=MESH,
        )

    def small_add(k):
        small_copy(k).wait()
        sm[late, :] += smr[k]
        if k + 1 < steps:
            small_copy(k + 1).start()

    def small_z_first():
        @pl.when(jnp.logical_not(inner))
        def _():
            small_z(0).start()

    def small_z_second():
        @pl.when(inner)
        def _():
            small_z(0).wait_recv()
            sm[late, :] += smz[0]
            small_z(1).start()

    def small_z_third():
        @pl.when(inner)
        def _():
            small_z(1).wait()
            sm[late, :] += smz[1]
            small_z(2).start()

    def small_z_last():
        @pl.when(jnp.logical_not(inner))
        def _():
            small_z(0).wait_send()
            small_z(2).wait_recv()
            sm[late, :] = smz[1]

    def wz_rows(p, count=1):
        return pl.ds(p * block_rows, count * block_rows)

    def wz_start():
        for p in range(n):
            wzp[wz_rows(p), :] = zg[aligned(block_at(0, p), block_rows), :]
        if steps:
            wz_copy(0).start()

    def wz_copy(s):
        half = n >> (s + 1)
        return pltpu.make_async_remote_copy(
            src_ref=wzp.at[wz_rows(half, half)], dst_ref=wzr.at[wz_rows(half, half)],
            send_sem=u_s.at[s], recv_sem=u_r.at[s],
            device_id={"seq": flip(seq, bit_orders[0][s])}, device_id_type=MESH,
        )

    def wz_add(s):
        half = n >> (s + 1)
        wz_copy(s).wait()
        wzp[wz_rows(0, half), :] += wzr[wz_rows(half, half), :]
        if s + 1 < steps:
            wz_copy(s + 1).start()

    def wz_z(k):
        dst, peer = ((0, middle_peer), (1, middle_peer), (1, outer_peer))[k]
        return pltpu.make_async_remote_copy(
            src_ref=wzp.at[wz_rows(0)], dst_ref=wzz.at[dst],
            send_sem=u_s.at[2 * steps + (0 if k < 2 else 1)],
            recv_sem=u_r.at[2 * steps + min(k, 1)],
            device_id={"dp": peer}, device_id_type=MESH,
        )

    def wz_z_first():
        @pl.when(jnp.logical_not(inner))
        def _():
            wz_z(0).start()

    def wz_z_second():
        @pl.when(inner)
        def _():
            wz_z(0).wait_recv()
            wzp[wz_rows(0), :] += wzz[0]
            wz_z(1).start()

    def wz_z_third():
        @pl.when(inner)
        def _():
            wz_z(1).wait()
            wzp[wz_rows(0), :] += wzz[1]
            wz_z(2).start()

    def wz_z_last():
        @pl.when(jnp.logical_not(inner))
        def _():
            wz_z(0).wait_send()
            wz_z(2).wait_recv()
            wzp[wz_rows(0), :] = wzz[1]

        if steps:
            wz_back(steps - 1).start()

    def wz_back(s):
        half = n >> (s + 1)
        return pltpu.make_async_remote_copy(
            src_ref=wzp.at[wz_rows(0, half)], dst_ref=wzp.at[wz_rows(half, half)],
            send_sem=u_s.at[steps + s], recv_sem=u_r.at[steps + s],
            device_id={"seq": flip(seq, bit_orders[0][s])}, device_id_type=MESH,
        )

    def wz_spread(s):
        wz_back(s).wait()
        if s:
            wz_back(s - 1).start()

    def small_end():
        for p in range(n):
            sm[aligned(block_at(0, p), block_rows), :] = wzp[wz_rows(p), :]
        own_small().start()
        give_small().start()

    def own_small():
        return pltpu.make_async_copy(sm, sm_h, mo_sem.at[1])

    sum_lag, z_lag, z_lag_1, mega_at, wz_at, small_gap, wz_gap = schedule
    mega_work = [
        lambda: [cp.start() for cp in loads()], ema_ends, ema_carries, ema_sums, ema_adjoint, input_grads
    ]
    mega_ticks = list(mega_at)
    if steps:
        mega_work.append(lambda: small_copy(0).start())
        mega_ticks.append(mega_ticks[-1])
    for stage in [functools.partial(small_add, k) for k in range(steps)] + [
        small_z_first, small_z_second, small_z_third, small_z_last
    ]:
        mega_work.append(stage)
        mega_ticks.append(mega_ticks[-1] + small_gap * (stage != small_z_first))
    last = mega_ticks[-1]
    at = wz_at
    for stage in (
        [wz_start]
        + [functools.partial(wz_add, s) for s in range(steps)]
        + [wz_z_first, wz_z_second, wz_z_third, wz_z_last]
        + [functools.partial(wz_spread, s) for s in range(steps - 1, -1, -1)]
    ):
        mega_work.append(stage)
        mega_ticks.append(at)
        at += wz_gap * (stage not in (wz_z_first,))
    mega_work.append(small_end)
    mega_ticks.append(max(last, at))

    ticks = 2 * CUTS

    def z_work(pair, tick, lags):
        for lag, stage in zip(lags, z_stages):
            v = ticks * pair + tick - lag

            @pl.when((v >= 0) & (v < pieces))
            def _():
                stage(v)

    sum_stages = [(0, produce)]
    for s in range(steps):
        sum_stages.append(((s + 1) * sum_lag, functools.partial(absorb, s=s)))
    sum_z = [steps * sum_lag + lag for lag in z_lag]
    sum_pairs = pairs + -(-sum_z[-1] // ticks)

    def sum_tick(pair, tick):
        for lag, stage in sum_stages:
            unit, i = divmod(tick - lag, CUTS)
            t = pair + unit // 2

            @pl.when((t >= 0) & (t < pairs))
            def _():
                stage(t, unit % 2, i)

        z_work(pair, tick, sum_z)

    def sum_pair(pair):
        for tick in range(ticks):
            sum_tick(pair, tick)

    def mega_pair(pair):
        for tick in range(ticks):
            sum_tick(pair, tick)
            for when in sorted(set(mega_ticks)):
                if when % ticks == tick:
                    work = [f for f, m in zip(mega_work, mega_ticks) if m == when]

                    @pl.when(pair == when // ticks)
                    def _():
                        for f in work:
                            f()

    recompute_z = [ticks + lag for lag in z_lag_1]
    recompute_pairs = pairs + -(-recompute_z[-1] // ticks)

    def recompute_pair(pair):
        for g in range(n):

            @pl.when(pair < pairs)
            def _():
                recompute_piece(pair, g)

            for tick in range(g * ticks // n, (g + 1) * ticks // n):
                z_work(pair, tick, recompute_z)

            if g == n - 1:

                @pl.when(pair == pairs - 1)
                def _():
                    output_load(0)

            for c in range(pairs):
                if c % n == g:

                    @pl.when(pair == pairs + c // n)
                    def _():
                        output_chunk(c)

    def drain(summed):
        def sent(c):
            v = pieces - WINDOW + c

            @pl.when(inner)
            def _():
                z_copy(1, v).wait_send()
                z_copy(2, v).wait_send()

            @pl.when(jnp.logical_not(inner))
            def _():
                z_copy(0, v).wait_send()

        if summed:
            for color in range(2):
                for s in range(steps):
                    for i in range(CUTS):
                        for t in range(pairs - SUM_WINDOW, pairs):
                            xy_copy(t, color, s, i).wait_send()
        loop(WINDOW, sent)
        loop(pieces, lambda v: store(zr1, v).wait())

    if recompute:

        @pl.when(sec == 1)
        def _():
            recompute_start()

    pl.semaphore_wait(barrier, n - 1 + jnp.where(inner, 2, 1) + (1 - sec))

    @pl.when(sec == 0)
    def _():
        pl.semaphore_signal(ready, inc=1, device_id={"section": 1}, device_id_type=MESH)

    @pl.when(sec == 0)
    def _():
        load_l.wait()
        loop(max(sum_pairs, max(mega_ticks) // ticks + 1), mega_pair)
        drain(True)

    @pl.when(sec == 1)
    def _():
        if recompute:
            loop(max(recompute_pairs, pairs + (pairs + n - 1) // n), recompute_pair)
        else:
            load_l.wait()
            loop(sum_pairs, sum_pair)
        drain(not recompute)

    @pl.when(sec == 0)
    def _():
        for way in range(2):
            for k in range(1, n):
                has = (seq + k < n) if way == 0 else (seq - k >= 0)

                @pl.when(has)
                def _():
                    state_copy(k, way).wait_send()

        @pl.when(inner)
        def _():
            small_z(2).wait_send()
            wz_z(2).wait_send()

        own_small().wait()
        give_small().wait_send()
        if recompute:
            give_output().wait_recv()

        own_grad().wait()
        give_grad().wait_send()

    @pl.when(sec == 1)
    def _():
        if recompute:
            own_output().wait()
            give_output().wait_send()
        else:
            pl.semaphore_wait(ready, 1)
        give_grad().wait_recv()
        give_small().wait_recv()


SCHEDULE = (8, (0, 3, 6, 9), (0, 3, 6, 9), (8, 12, 16, 18, 20, 22), 2, 2, 4)


def reduce_grads(n, nd, l, r, both, w1, w2, xs, gs, gxn, xx, cd, gp, h0, zg, misc, raw, gain):
    rows, width = gxn.shape
    groups = width // LANES
    ndim = raw.shape[1]
    ff = r.shape[1] // 2
    pairs = ff // CH
    block_rows = width // n
    steps = n.bit_length() - 1
    small_rows = width + 2 * ndim * groups + 4 * groups
    any_spec = pl.BlockSpec(memory_space=pl.ANY)
    vmem = pl.BlockSpec(memory_space=pltpu.VMEM)

    def kernel(*refs):
        fixed = refs[: 16 + 4]
        rest = list(refs[16 + 4 :])
        recvs = rest[:steps]
        reduce_kernel(n, nd, SCHEDULE, *fixed, recvs, *rest[steps:])

    return pl.pallas_call(
        kernel,
        out_shape=[
            jax.ShapeDtypeStruct((2, block_rows, ff), BF16),
            jax.ShapeDtypeStruct((rows // 2, width), F32),
            jax.ShapeDtypeStruct((small_rows, LANES), F32),
            jax.ShapeDtypeStruct((rows // 2, width), F32),
        ],
        in_specs=[any_spec] * 11 + [vmem] * 5,
        out_specs=[any_spec] * 4,
        scratch_shapes=[
            pltpu.VMEM(
                (pairs * (n >> (s + 1)) * block_rows * (1 if s == 0 else 2), CH * (2 if s == 0 else 1)),
                BF16,
            )
            for s in range(steps)
        ]
        + [
            pltpu.VMEM((3, width, rows), BF16),
            pltpu.VMEM((2, 2, rows, CH), BF16),
            pltpu.VMEM((pairs * 2 * width, CH), BF16),
            pltpu.VMEM((2, block_rows, CH), F32),
            pltpu.VMEM((pairs * 2 * block_rows, CH), BF16),
            pltpu.VMEM((pairs * 2 * block_rows, CH), BF16),
            pltpu.VMEM((rows * groups, LANES), F32),
            pltpu.VMEM((rows * groups, LANES), F32),
            pltpu.VMEM((rows, width), F32),
            pltpu.VMEM((rows, width), BF16),
            pltpu.VMEM((rows, width), BF16),
            pltpu.VMEM((rows, width), BF16),
            pltpu.VMEM((2, 2, ndim, groups, LANES), F32),
            pltpu.VMEM((2, n, 2, ndim, groups, LANES), F32),
            pltpu.VMEM((2, 2, ndim, groups, LANES), F32),
            pltpu.VMEM((small_rows, LANES), F32),
            pltpu.VMEM((max(steps, 1), small_rows - width, LANES), F32),
            pltpu.VMEM((2, small_rows - width, LANES), F32),
            pltpu.VMEM((width, LANES), F32),
            pltpu.VMEM((width, LANES), F32),
            pltpu.VMEM((2, block_rows, LANES), F32),
            pltpu.VMEM((ndim, groups, LANES), F32),
            pltpu.VMEM((ndim, groups, LANES), F32),
            pltpu.VMEM((ndim, groups, LANES), F32),
            pltpu.SemaphoreType.DMA,
            pltpu.SemaphoreType.DMA((2, 2)),
            pltpu.SemaphoreType.DMA((6,)),
            pltpu.SemaphoreType.DMA((steps, 2, pairs * CUTS)),
            pltpu.SemaphoreType.DMA((steps, 2, pairs * CUTS)),
            pltpu.SemaphoreType.DMA((2, 2 * pairs * CUTS)),
            pltpu.SemaphoreType.DMA((2, 2 * pairs * CUTS)),
            pltpu.SemaphoreType.DMA((2 * pairs * CUTS,)),
            pltpu.SemaphoreType.DMA((2, n)),
            pltpu.SemaphoreType.DMA((2, n)),
            pltpu.SemaphoreType.DMA((steps + 2,)),
            pltpu.SemaphoreType.DMA((steps + 2,)),
            pltpu.SemaphoreType.DMA((2,)),
            pltpu.SemaphoreType.DMA((2, n)),
            pltpu.SemaphoreType.DMA((2, 2)),
            pltpu.SemaphoreType.DMA((3,)),
            pltpu.SemaphoreType.DMA((3,)),
            pltpu.SemaphoreType.DMA((2 * steps + 2,)),
            pltpu.SemaphoreType.DMA((2 * steps + 2,)),
            pltpu.SemaphoreType.REGULAR,
        ],
        compiler_params=pltpu.CompilerParams(
            collective_id=1, has_side_effects=True, vmem_limit_bytes=VMEM_LIMIT
        ),
        name="reduce_grads",
    )(l, r, both, w1, w2, xs, gs, gxn, xx, cd, gp, h0, zg, misc, raw, gain)


def finish_kernel(
    coeff, seq_ref, red, w1, w2, sm_h, raw, gain, fgain, wz, qk, out_h, ig_h,
    first, second, z_o, qk_o, ema_o, norm_o, omega_o, ffn_o, out_o, ig_o,
    sm, sems,
):
    width, groups = wz.shape[0], gain.shape[1] // LANES
    ndim = raw.shape[1]
    load = pltpu.make_async_copy(sm_h, sm, sems)

    @pl.when(pl.program_id(0) == 0)
    def _():
        load.start()

    out_o[...] = out_h[...]
    ig_o[...] = ig_h[...]

    first[...] = red[0].astype(F32) + coeff * w1[...].astype(F32)
    second[...] = red[1].astype(F32) + coeff * w2[...].astype(F32)

    @pl.when(pl.program_id(0) == pl.num_programs(0) - 1)
    def _():
        load.wait()
        z_o[...] = sm[0:width, :] + coeff * wz[...].astype(F32)
        base = width + 2 * ndim * groups
        for j in range(groups):
            at = slice(j * LANES, (j + 1) * LANES)
            omega_o[:, at] = sm[base + j : base + j + 1, :]
            ffn_o[:, at] = sm[base + groups + j : base + groups + j + 1, :] + coeff * fgain[:, at]
            norm_o[:, at] = (
                sm[base + 3 * groups + j : base + 3 * groups + j + 1, :] + coeff * gain[:, at]
            )
        qk_o[...] = sm[base + 2 * groups : base + 2 * groups + 4, :] + coeff * qk[...]
        for j in range(ndim):
            sum_0 = sm[width + j * groups : width + (j + 1) * groups, :]
            sum_1 = sm[width + (ndim + j) * groups : width + (ndim + j + 1) * groups, :]
            alpha, damp = jax.nn.sigmoid(raw[0, j]), jax.nn.sigmoid(raw[1, j])
            inject = alpha * raw[2, j]
            inject_grad = raw[3, j] * sum_0
            decay_grad = raw[3, j] * inject * sum_1
            ema_o[0, j] = (inject_grad * raw[2, j] - decay_grad * damp) * alpha * (1.0 - alpha)
            ema_o[1, j] = -decay_grad * alpha * damp * (1.0 - damp)
            ema_o[2, j] = inject_grad * alpha
            ema_o[3, j] = inject * sum_0


def finish(coeff, seq, red, w1, w2, small, raw, gain, fgain, wz, qk, out, grad):
    block_rows, ff = red.shape[1:]
    any_spec = pl.BlockSpec(memory_space=pl.ANY)
    vmem = pl.BlockSpec(memory_space=pltpu.VMEM)
    tiles = block_rows // TILE_SMALL
    own = pl.BlockSpec((TILE_SMALL, ff), lambda j, s: (s[0] * tiles + j, 0))
    share = pl.BlockSpec((TILE_SMALL, ff), lambda j, s: (j, 0))
    rows = pl.BlockSpec((out.shape[0] // tiles, out.shape[1]), lambda j, s: (j, 0))

    def shape(dims):
        return jax.ShapeDtypeStruct(dims, F32)

    return pl.pallas_call(
        functools.partial(finish_kernel, coeff),
        grid_spec=pltpu.PrefetchScalarGridSpec(
            num_scalar_prefetch=1,
            grid=(tiles,),
            in_specs=[pl.BlockSpec((2, TILE_SMALL, ff), lambda j, s: (0, j, 0)), own, own]
            + [any_spec]
            + [vmem] * 5
            + [rows] * 2,
            out_specs=[share, share] + [vmem] * 6 + [rows] * 2,
            scratch_shapes=[
                pltpu.VMEM(small.shape, F32),
                pltpu.SemaphoreType.DMA,
            ],
        ),
        out_shape=[
            shape((block_rows, ff)),
            shape((block_rows, ff)),
            shape(wz.shape),
            shape(qk.shape),
            shape(raw.shape),
            shape(gain.shape),
            shape(gain.shape),
            shape(gain.shape),
            shape(out.shape),
            shape(grad.shape),
        ],
        compiler_params=pltpu.CompilerParams(vmem_limit_bytes=VMEM_LIMIT),
        name="finish",
    )(seq, red, w1, w2, small, raw, gain, fgain, wz, qk, out, grad)


def body(
    inputs, cotangent, norm_gain, first_pack, second_pack, w_z, qk_affine, ema_params, omega, ffn_gain
):
    n = lax.axis_size("seq")
    nd = lax.axis_size("dp")
    tok, width = inputs.shape[2:]
    groups = width // LANES
    ndim = ema_params.shape[2]

    raw = jnp.swapaxes(ema_params, 1, 2).reshape(4, ndim, groups, LANES)

    def line(v):
        return v.reshape(1, width)

    l, r, xs, gs, gxn, xx, cd, gp, h0, block_output, both, zg, misc = relay(
        n, inputs[0, 0], cotangent[0, 0], line(norm_gain), line(omega), line(ffn_gain),
        raw, qk_affine, w_z, first_pack[0], second_pack[0],
    )
    red, input_grad, small, late_output = reduce_grads(
        n, nd, l, r, both, first_pack[0], second_pack[0], xs, gs, gxn, xx, cd, gp, h0, zg, misc,
        raw, line(norm_gain),
    )

    if n == RECOMPUTE_OVER:
        block_output = late_output
    coeff = DECAY * 2 * nd * n * tok
    grads = finish(
        coeff, lax.axis_index("seq").reshape(1), red, first_pack[0], second_pack[0],
        small, raw, line(norm_gain), line(ffn_gain), w_z, qk_affine, block_output, input_grad,
    )
    first, second, z_grad, qk_grad, ema_grad, norm_grad, omega_grad, ffn_grad, output, in_grad = grads
    return (
        output[None, None],
        in_grad[None, None],
        norm_grad.reshape(width),
        first[None],
        second[None],
        z_grad,
        qk_grad,
        jnp.swapaxes(ema_grad.reshape(4, ndim, width), 1, 2),
        omega_grad.reshape(width),
        ffn_grad.reshape(width),
    )


def solution(mesh):
    rows = P("section", "dp", "seq", None)
    packs = P("section", None, None)
    shares = P("section", "seq", None)
    return jax.shard_map(
        body,
        mesh=mesh,
        in_specs=(rows, rows, P(), packs, packs, P(), P(), P(), P(), P()),
        out_specs=(rows, rows, P(), shares, shares, P(), P(), P(), P(), P()),
        check_vma=False,
    )
```

```python
import functools

import jax
import jax.numpy as jnp
from jax import lax
from jax.experimental import pallas as pl
from jax.experimental.pallas import tpu as pltpu
from jax.sharding import PartitionSpec as P

MESH = pl.DeviceIdType.MESH
F32 = jnp.float32
BF16 = jnp.bfloat16
VALUE_WIDTH = 2048
BLOCK = 128
EPSILON = 1e-05
DECAY = 0.01
CH = 512
WINDOW = 4
SUM_WINDOW = 3
CUTS = 2
HIDDEN = 1024
TILE = 128
TILE_SMALL = 64
LANES = 128
VMEM_LIMIT = 60 * 1024 * 1024
RECOMPUTE_OVER = 4


def dot(a, b):
    return lax.dot_general(a, b, (((1,), (0,)), ((), ())), preferred_element_type=F32)


def dot_nt(a, b):
    return lax.dot_general(a, b, (((1,), (1,)), ((), ())), preferred_element_type=F32)


def normed_rows(v):
    center = v - jnp.mean(v, axis=-1, keepdims=True)
    factor = lax.rsqrt(jnp.mean(center * center, axis=-1, keepdims=True) + EPSILON)
    return center * factor, factor


def norm_back(grad, gain, unit, factor):
    s = grad * gain
    return factor * (
        s
        - jnp.mean(s, axis=-1, keepdims=True)
        - unit * jnp.mean(s * unit, axis=-1, keepdims=True)
    )


def loop(count, body, unroll=1):
    lax.fori_loop(0, count, lambda i, c: (body(i), c)[1], 0, unroll=unroll)


def aligned(i, size):
    return pl.ds(pl.multiple_of(i * size, size), size)


def to_channel_rows(ref, row, tile):
    groups = tile.shape[1] // LANES
    for sub in range(tile.shape[0] // 8):
        for j in range(groups):
            ref[pl.ds((row + 8 * sub) * groups + j, 8, stride=groups), :] = tile[
                8 * sub : 8 * sub + 8, j * LANES : (j + 1) * LANES
            ]


def from_channel_rows(ref, row, rows, groups):
    tiles = []
    for sub in range(rows // 8):
        tiles.append(
            jnp.concatenate(
                [
                    ref[pl.ds((row + 8 * sub) * groups + j, 8, stride=groups), :]
                    for j in range(groups)
                ],
                axis=1,
            )
        )
    return jnp.concatenate(tiles, axis=0)


def bit_of(value, bit):
    return lax.rem(lax.div(value, 1 << bit), 2)


def flip(value, bit):
    return value + (1 - 2 * bit_of(value, bit)) * (1 << bit)


def rows_of(values):
    return [values[:, j * LANES : (j + 1) * LANES] for j in range(values.shape[1] // LANES)]


def add_all(terms):
    terms = list(terms)
    while len(terms) > 1:
        terms = [a + b for a, b in zip(terms[::2], terms[1::2])] + (
            [terms[-1]] if len(terms) % 2 else []
        )
    return terms[0]


def set_rates(raw, steps, q_r, w_r, qt_r):
    for j in range(q_r.shape[0]):
        alpha = jax.nn.sigmoid(raw[0, j])
        decay = 1.0 - alpha * jax.nn.sigmoid(raw[1, j])
        q_r[j] = decay
        w_r[j] = raw[3, j] * (alpha * raw[2, j])
        power, base, left = None, decay, steps
        while left:
            if left & 1:
                power = base if power is None else power * base
            base, left = base * base, left >> 1
        qt_r[j] = power


def relay_kernel(
    n,
    x_own, c_own, gain, omega, fgain, raw, qk, wz, w1h, w2h,
    l_h, r_h, xs_h, gs_h, gxn_h, xx_h, cd_h, gp_h, h0_h, out_h, all_h, zg_o, misc_o,
    w1, w2, xc, xn, xs, rv, lv, vl, vsl, rs, ra, mlow, msl, cu, cc, cd, ps, gp,
    gm, zp, zs, zq, zk, pr, prl, tl, tr, h0, fg, fgr, gz, qks, tmp, q_r, w_r, qt_r,
    w_sem, in_sem, o_sem, d2d_s, d2d_r, t_s, t_r, a_s, a_r,
):
    sec = lax.axis_index("section")
    seq = lax.axis_index("seq")
    rows, width = xc.shape
    tok = rows // 2
    groups = width // LANES
    ndim = q_r.shape[0]
    set_rates(raw, tok, q_r, w_r, qt_r)
    ff = w1.shape[1]
    vw = VALUE_WIDTH
    blocks = tok // BLOCK
    zw = qk.shape[1]
    scale = zw**-0.5
    gates, cand_at = 2 * vw, 3 * vw + width
    recompute = all_h.shape[1] > 1
    halves = [pl.ds(m * tok, tok) for m in range(2)]

    barrier = pltpu.get_barrier_semaphore()
    pl.semaphore_signal(barrier, inc=1, device_id={"section": 1 - sec}, device_id_type=MESH)
    for k in range(1, n):
        pl.semaphore_signal(
            barrier, inc=1, device_id={"seq": lax.rem(seq + k, n)}, device_id_type=MESH
        )

    def to_sibling(src, dst, k):
        return pltpu.make_async_remote_copy(
            src_ref=src, dst_ref=dst, send_sem=d2d_s.at[k], recv_sem=d2d_r.at[k],
            device_id={"section": 1 - sec}, device_id_type=MESH,
        )

    def half_to_sibling(ref, m, k):
        return to_sibling(ref.at[halves[m]], ref.at[halves[m]], k + m)

    outs = []

    def out_copy(src, dst):
        cp = pltpu.make_async_copy(src, dst, o_sem.at[len(outs)])
        cp.start()
        outs.append(cp)
        return len(outs) - 1

    def load_weights(parts):
        loads = []
        for k, (src, dst, start, size) in enumerate(parts):
            at = pl.ds(start, size)
            cp = pltpu.make_async_copy(src.at[:, at], dst.at[:, at], w_sem.at[k])
            cp.start()
            loads.append(cp)
        return loads

    def tail_copy(m, k):
        return pltpu.make_async_remote_copy(
            src_ref=tl.at[m], dst_ref=tr.at[m, k], send_sem=t_s.at[m, k], recv_sem=t_r.at[m, k],
            device_id={"seq": seq + k}, device_id_type=MESH,
        )

    def gather_copies(what, src, m, hop):
        copies = []
        half = tok // 2
        for way in range(2):
            at = pl.ds(m * tok + way * half, half)
            first, second = (0, 1) if way == 0 else (1, 0)
            if hop == 0:
                moves = [(src.at[at], 1 << first, first, 0)]
            else:
                moves = [
                    (src.at[at], 1 << second, second, 1),
                    (all_h.at[what, 1 << first, at], 3, second, 2),
                ]
            for source, slot, bit, k in moves:
                copies.append(
                    pltpu.make_async_remote_copy(
                        src_ref=source, dst_ref=all_h.at[what, slot, at],
                        send_sem=a_s.at[what, m, way * 3 + k],
                        recv_sem=a_r.at[what, m, way * 3 + k],
                        device_id={"seq": flip(seq, bit)}, device_id_type=MESH,
                    )
                )
        return copies

    def gather_start(what, src, m):
        if recompute:
            for cp in gather_copies(what, src, m, 0):
                cp.start()

    def gather_forward(what, src, m):
        if recompute:
            for cp in gather_copies(what, src, m, 0):
                cp.wait_recv()
            for cp in gather_copies(what, src, m, 1):
                cp.start()

    def gather_end(what, src, m):
        if recompute:
            for cp in gather_copies(what, src, m, 0):
                cp.wait_send()
            for cp in gather_copies(what, src, m, 1):
                cp.wait()

    def tiles(m, body):
        count = tok // TILE
        loop(count, lambda i: body(i + m * count))

    def transpose_into(slot, src, m):
        def one(j):
            lv[slot, aligned(j, LANES), halves[m]] = src[halves[m], aligned(j, LANES)].T

        loop(width // LANES, one)

    def normalise(m):
        g = gain[...]

        def norm_tile(i):
            unit, _ = normed_rows(xc[aligned(i, TILE), :].astype(F32))
            tile = unit * g
            xn[aligned(i, TILE), :] = tile
            mlow[aligned(i, TILE), :] = tile.astype(BF16)
            to_channel_rows(xs, i * TILE, tile)

        tiles(m, norm_tile)

    def channel_rows(t):
        return pl.ds(pl.multiple_of(t * groups, groups), groups)

    def local_states(m):
        q = [q_r[j] for j in range(ndim)]

        def step(i, h):
            for u in range(8):
                x = xs[channel_rows(m * tok + i * 8 + u), :]
                h = tuple(q[j] * h[j] + x for j in range(ndim))
            return h

        zeros = jnp.zeros((groups, LANES), F32)
        h = lax.fori_loop(0, tok // 8, step, tuple(zeros for _ in range(ndim)))
        for j in range(ndim):
            tl[m, j] = h[j]

    def send_states(m):
        for k in range(1, n):

            @pl.when(seq + k < n)
            def _():
                tail_copy(m, k).start()

            @pl.when(seq - k < 0)
            def _():
                tr[m, k] = jnp.zeros(tr.shape[2:], F32)

    def values(m):
        at_m = halves[m]
        transpose_into(0, mlow, m)

        def value_chunk(c):
            pre = dot(mlow[at_m, :], w1[:, aligned(c, CH)])
            sig = jax.nn.sigmoid(pre)
            vl[at_m, aligned(c, CH)] = (pre * sig).astype(BF16)
            vsl[at_m, aligned(c, CH)] = (sig * (1.0 + pre * (1.0 - sig))).astype(BF16)

        loop(vw // CH, value_chunk)

    def start_states(m):
        for k in range(1, n):

            @pl.when(seq - k >= 0)
            def _():
                tail_copy(m, k).wait_recv()

        for j in range(ndim):
            state = jnp.zeros((groups, LANES), F32)
            for k in range(n - 1, 0, -1):
                state = state * qt_r[j] + tr[m, k, j]
            h0[m, j] = state
        out_copy(h0.at[m], h0_h.at[m])

    def smooth(m):
        q = [q_r[j] for j in range(ndim)]
        w = [w_r[j] for j in range(ndim)]

        def step(i, h):
            for u in range(8):
                at = channel_rows(m * tok + i * 8 + u)
                x = xs[at, :]
                h = tuple(q[j] * h[j] + x for j in range(ndim))
                xs[at, :] = add_all(w[j] * h[j] for j in range(ndim))
            return h

        lax.fori_loop(0, tok // 8, step, tuple(h0[m, j] for j in range(ndim)))
        om = omega[...]

        def mixed_tile(i):
            pre = from_channel_rows(xs, i * TILE, TILE, groups) + om * xn[aligned(i, TILE), :]
            sig = jax.nn.sigmoid(pre)
            mlow[aligned(i, TILE), :] = (pre * sig).astype(BF16)
            msl[aligned(i, TILE), :] = (sig * (1.0 + pre * (1.0 - sig))).astype(BF16)

        tiles(m, mixed_tile)

    def attention(m):
        at_m = halves[m]
        tmz = dot(mlow[at_m, :], wz[...])
        sig = jax.nn.sigmoid(tmz)
        zpart = tmz * sig
        zp[at_m, :] = zpart
        zs[at_m, :] = sig * (1.0 + tmz * (1.0 - sig))
        zq[at_m, :] = (zpart * qk[0:1, :] + qk[1:2, :]).astype(BF16)
        zk[at_m, :] = (zpart * qk[2:3, :] + qk[3:4, :]).astype(BF16)
        row_ids = lax.broadcasted_iota(jnp.int32, (BLOCK, BLOCK), 0)
        col_ids = lax.broadcasted_iota(jnp.int32, (BLOCK, BLOCK), 1)
        for b in range(blocks):
            at = pl.ds(m * tok + b * BLOCK, BLOCK)
            scores = jnp.where(row_ids >= col_ids, dot_nt(zq[at, :], zk[at, :]) * scale, -1e30)
            expo = jnp.exp(scores - jnp.max(scores, axis=-1, keepdims=True))
            probs = expo / jnp.sum(expo, axis=-1, keepdims=True)
            pr[at, :] = probs
            prl[at, :] = probs.astype(BF16)

    def gate(m):
        at_m = halves[m]

        def reset_chunk(c):
            at = aligned(c, CH)
            pre = dot(mlow[at_m, :], w2[:, at])
            for b in range(blocks):
                part = pl.ds(m * tok + b * BLOCK, BLOCK)
                att = dot(prl[part, :], vl[part, at])
                p = pre[b * BLOCK : (b + 1) * BLOCK]
                sig = jax.nn.sigmoid(p)
                reset = p * sig
                rs[part, at] = reset.astype(BF16)
                ra[part, at] = (att * (sig * (1.0 + p * (1.0 - sig)))).astype(BF16)
                rv[part, aligned(c + vw // CH, CH)] = (reset * att).astype(BF16)

        loop(vw // CH, reset_chunk)

    def finish(m):
        at_m = halves[m]

        def cand_chunk(c):
            at = aligned(c, CH)
            update = jax.nn.sigmoid(dot(mlow[at_m, :], w2[:, aligned(c + vw // CH, CH)]))
            gm[at_m, at] = dot(mlow[at_m, :], w2[:, aligned(c + (vw + width) // CH, CH)])
            cand = gm[at_m, at] + dot_nt(rv[at_m, vw : 2 * vw], w1[at, vw : 2 * vw])
            x = xc[at_m, at].astype(F32)
            sig = jax.nn.sigmoid(cand)
            hidden = cand * sig
            keep = 1.0 - update
            ps[at_m, at] = (update * hidden + keep * x).astype(BF16)
            cu[at_m, at] = ((hidden - x) * update * keep).astype(BF16)
            cc[at_m, at] = (update * (sig * (1.0 + cand * (1.0 - sig)))).astype(BF16)
            cd[at_m, at] = keep.astype(BF16)

        loop(width // CH, cand_chunk)

    def backward(m):
        at_m = halves[m]
        first = m * blocks

        def direct_tile(i):
            at = aligned(i, TILE)
            grad = gp[at, :].astype(F32)
            rv[at, 3 * vw : cand_at] = (grad * cu[at, :].astype(F32)).astype(BF16)
            rv[at, cand_at:] = (grad * cc[at, :].astype(F32)).astype(BF16)

        tiles(m, direct_tile)

        def gated_chunk(c):
            at = aligned(c, CH)
            grad = dot(rv[at_m, cand_at:], w1[:, aligned(c + vw // CH, CH)])
            rv[at_m, aligned(c + gates // CH, CH)] = (grad * ra[at_m, at].astype(F32)).astype(BF16)
            rs[at_m, at] = (grad * rs[at_m, at].astype(F32)).astype(BF16)

        loop(vw // CH, gated_chunk)

        def attention_back(b):
            at = aligned(first + b, BLOCK)
            probs = pr[at, :]
            tmp[0] = dot_nt(rs[at, :], vl[at, :])
            grad_probs = tmp[0]
            grad_scores = probs * (
                grad_probs - jnp.sum(grad_probs * probs, axis=-1, keepdims=True)
            )
            tmp[1] = dot(grad_scores.astype(BF16), zk[at, :])
            tmp[2] = dot(grad_scores.T.astype(BF16), zq[at, :])
            grad_query, grad_keys = tmp[1] * scale, tmp[2] * scale
            zpart = zp[at, :]
            for k, term in enumerate((grad_query * zpart, grad_query, grad_keys * zpart, grad_keys)):
                qks[k : k + 1, :] += jnp.sum(term, axis=0, keepdims=True)
            gz[at, :] = (
                (grad_query * qk[0:1, :] + grad_keys * qk[2:3, :]) * zs[at, :]
            ).astype(BF16)
            prl[at, :] = probs.T.astype(BF16)

        loop(blocks, attention_back)

        def grad_value_chunk(c):
            at = aligned(c, CH)
            for b in range(blocks):
                part = pl.ds((first + b) * BLOCK, BLOCK)
                rv[part, at] = (
                    dot(prl[part, :], rs[part, at]) * vsl[part, at].astype(F32)
                ).astype(BF16)

        loop(vw // CH, grad_value_chunk)
        out_copy(rv.at[at_m], r_h.at[at_m])
        transpose_into(1, rv.at[:, pl.ds(cand_at, width)], m)
        out_copy(lv.at[1, :, at_m], l_h.at[1, :, at_m])

        def mixed_chunk(c):
            at = aligned(c, CH)
            gm[at_m, at] = dot_nt(gz[at_m, :], wz[at, :])
            grad = (gm[at_m, at] + dot_nt(rv[at_m, gates:], w2[at, :])) * msl[at_m, at].astype(F32)
            fgr[0:1, at] += jnp.sum(grad * xn[at_m, at], axis=0, keepdims=True)
            xn[at_m, at] = grad * omega[:, at] + dot_nt(rv[at_m, 0:vw], w1[at, 0:vw])
            gm[at_m, at] = grad

        loop(width // CH, mixed_chunk)
        out_copy(xn.at[at_m], gxn_h.at[at_m])
        tiles(m, lambda i: to_channel_rows(xs, i * TILE, gm[aligned(i, TILE), :]))
        of_m = pl.ds(m * tok * groups, tok * groups)
        out_copy(xs.at[of_m], gs_h.at[of_m])

    def own_rows(src, m):
        return pltpu.make_async_copy(src, xc.at[halves[m]], in_sem)

    @pl.when(sec == 0)
    def _():
        own_rows(x_own, 0).start()
        load_weights(((w1h, w1, 0, vw), (w2h, w2, 0, ff), (w1h, w1, vw, vw)))
        own_rows(x_own, 0).wait()
        normalise(0)
        local_states(0)

    @pl.when(sec == 1)
    def _():
        own_rows(c_own, 1).start()
        load_weights(((w2h, w2, 0, ff), (w1h, w1, 0, ff)))

    pl.semaphore_wait(barrier, n)

    def wait_weights(k, src, dst, start, size):
        at = pl.ds(start, size)
        pltpu.make_async_copy(src.at[:, at], dst.at[:, at], w_sem.at[k]).wait()

    @pl.when(sec == 0)
    def _():
        give = to_sibling(c_own, xc.at[halves[0]], 0)
        give.start()
        fgr[...] = jnp.zeros_like(fgr)
        qks[...] = jnp.zeros_like(qks)
        send_states(0)
        give.wait()
        out_copy(xc, xx_h)
        normalise(1)
        local_states(1)
        send_states(1)
        saved = out_copy(xs, xs_h)
        wait_weights(0, w1h, w1, 0, vw)
        for m in range(2):
            values(m)
            start_states(m)
            if m == 0:
                outs[saved].wait()
                outs[saved] = None
            smooth(m)
            if m == 0:
                wait_weights(1, w2h, w2, 0, ff)
            attention(m)
            gate(m)
            if m == 0:
                wait_weights(2, w1h, w1, vw, vw)
            finish(m)
            half_to_sibling(ps, m, 1).start()
            transpose_into(2, mlow, m)
            for slot in (0, 2):
                out_copy(lv.at[slot, :, halves[m]], l_h.at[slot, :, halves[m]])
        out_copy(cd, cd_h)
        for m in range(2):
            half_to_sibling(gp, m, 3).wait_recv()
            backward(m)
        out_copy(gp, gp_h)
        zg_o[...] = dot(lv[2], gz[...])
        for j, part in enumerate(rows_of(fgr[0:1, :])):
            misc_o[j : j + 1, :] = part
        to_sibling(fg, fg, 5).wait_recv()
        for j, part in enumerate(rows_of(fg[0:1, :])):
            misc_o[groups + j : groups + j + 1, :] = part
        misc_o[2 * groups : 3 * groups, :] = qks[...]
        misc_o[3 * groups :, :] = jnp.zeros((groups, LANES), F32)
        if not recompute:
            to_sibling(out_h, out_h, 6).wait_recv()
        for m in range(2):
            half_to_sibling(ps, m, 1).wait_send()
            for k in range(1, n):

                @pl.when(seq + k < n)
                def _():
                    tail_copy(m, k).wait_send()

        for cp in outs:
            if cp is not None:
                cp.wait()

    outs.clear()

    @pl.when(sec == 1)
    def _():
        give = to_sibling(x_own, xc.at[halves[1]], 0)
        give.start()
        own_rows(c_own, 1).wait()
        wait_weights(0, w2h, w2, 0, ff)

        def active_chunk(c, m):
            rv[halves[m], aligned(c, CH)] = dot(xc[halves[m], :], w2[:, aligned(c, CH)]).astype(BF16)

        loop(ff // CH, lambda c: active_chunk(c, 1))
        give.wait()
        if recompute:
            out_copy(xc, all_h.at[1, 0])
        loop(ff // CH, lambda c: active_chunk(c, 0))
        for m in range(2):
            gather_start(1, xc, m)
        if not recompute:
            for m in range(2):
                transpose_into(2, xc, m)
        wait_weights(1, w1h, w1, 0, ff)
        fg[...] = jnp.zeros_like(fg)
        g = fgain[...]
        for m in range(2):
            gather_forward(1, xc, m)
        for m in range(2):
            at_m = halves[m]
            half_to_sibling(ps, m, 1).wait_recv()

            def norm_tile(i):
                at = aligned(i, TILE)
                unit, _ = normed_rows(ps[at, :].astype(F32))
                mlow[at, :] = (unit * g).astype(BF16)

            tiles(m, norm_tile)
            gather_start(0, mlow, m)
            xn[at_m, :] = jnp.zeros((tok, width), F32)

            def hidden_chunk(c):
                at = aligned(c, HIDDEN)
                pre = dot(mlow[at_m, :], w1[:, at])
                sig = jax.nn.sigmoid(pre)
                rv[at_m, aligned(c + ff // HIDDEN, HIDDEN)] = (pre * sig).astype(BF16)
                grad = (
                    rv[at_m, at].astype(F32) * (sig * (1.0 + pre * (1.0 - sig)))
                ).astype(BF16)
                rv[at_m, at] = grad
                xn[at_m, :] += dot_nt(grad, w1[:, at])

            loop(ff // HIDDEN, hidden_chunk, unroll=2)

            def back_tile(i):
                at = aligned(i, TILE)
                unit, factor = normed_rows(ps[at, :].astype(F32))
                grad = xn[at, :]
                fg[0:1, :] += jnp.sum(grad * unit, axis=0, keepdims=True)
                gp[at, :] = (
                    xc[at, :].astype(F32) + norm_back(grad, g, unit, factor)
                ).astype(BF16)

            tiles(m, back_tile)
            half_to_sibling(gp, m, 3).start()
            gather_forward(0, mlow, m)
        gains = to_sibling(fg, fg, 5)
        gains.start()
        out_copy(rv, r_h)
        sent = [gains] + [half_to_sibling(gp, m, 3) for m in range(2)]
        if recompute:
            out_copy(mlow, all_h.at[0, 0])
            out_copy(ps, gp_h)
        else:
            for slot in range(2):
                for m in range(2):
                    transpose_into(slot, mlow, m)
            out_copy(lv, l_h)

            def out_chunk(c):
                at = aligned(c, CH)
                xn[:, at] = ps[:, at].astype(F32) + dot_nt(rv[:, ff : 2 * ff], w2[at, :])

            loop(width // CH, out_chunk)
            result = to_sibling(xn.at[halves[0]], out_h, 6)
            result.start()
            sent.append(result)
            out_copy(xn.at[halves[1]], out_h)
        for cp in sent:
            cp.wait_send()
        for what, src in enumerate((mlow, xc)):
            for m in range(2):
                gather_end(what, src, m)
        for cp in outs:
            cp.wait()


def relay(n, x, c, gain, omega, fgain, raw, qk, wz, w1, w2):
    rows, width = 2 * x.shape[0], x.shape[1]
    ff, vw, zw = w1.shape[1], VALUE_WIDTH, wz.shape[1]
    groups = width // LANES
    ndim = raw.shape[1]
    any_spec = pl.BlockSpec(memory_space=pl.ANY)
    vmem = pl.BlockSpec(memory_space=pltpu.VMEM)

    def shape(dims, kind):
        return jax.ShapeDtypeStruct(dims, kind)

    outs = [
        (shape((3, width, rows), BF16), any_spec),
        (shape((rows, 2 * ff), BF16), any_spec),
        (shape((rows * groups, LANES), F32), any_spec),
        (shape((rows * groups, LANES), F32), any_spec),
        (shape((rows, width), F32), any_spec),
        (shape((rows, width), BF16), any_spec),
        (shape((rows, width), BF16), any_spec),
        (shape((rows, width), BF16), any_spec),
        (shape((2, ndim, groups, LANES), F32), any_spec),
        (shape((rows // 2, width), F32), any_spec),
        (shape((2, n if n == RECOMPUTE_OVER else 1, rows, width), BF16), any_spec),
        (shape((width, zw), F32), vmem),
        (shape((4 * groups, LANES), F32), vmem),
    ]
    return pl.pallas_call(
        functools.partial(relay_kernel, n),
        out_shape=[o[0] for o in outs],
        in_specs=[any_spec, any_spec] + [vmem] * 6 + [any_spec, any_spec],
        out_specs=[o[1] for o in outs],
        scratch_shapes=[
            pltpu.VMEM((width, ff), BF16),
            pltpu.VMEM((width, ff), BF16),
            pltpu.VMEM((rows, width), BF16),
            pltpu.VMEM((rows, width), F32),
            pltpu.VMEM((rows * groups, LANES), F32),
            pltpu.VMEM((rows, 2 * ff), BF16),
            pltpu.VMEM((3, width, rows), BF16),
            pltpu.VMEM((rows, vw), BF16),
            pltpu.VMEM((rows, vw), BF16),
            pltpu.VMEM((rows, vw), BF16),
            pltpu.VMEM((rows, vw), BF16),
            pltpu.VMEM((rows, width), BF16),
            pltpu.VMEM((rows, width), BF16),
            pltpu.VMEM((rows, width), BF16),
            pltpu.VMEM((rows, width), BF16),
            pltpu.VMEM((rows, width), BF16),
            pltpu.VMEM((rows, width), BF16),
            pltpu.VMEM((rows, width), BF16),
            pltpu.VMEM((rows, width), F32),
            pltpu.VMEM((rows, zw), F32),
            pltpu.VMEM((rows, zw), F32),
            pltpu.VMEM((rows, zw), BF16),
            pltpu.VMEM((rows, zw), BF16),
            pltpu.VMEM((rows, BLOCK), F32),
            pltpu.VMEM((rows, BLOCK), BF16),
            pltpu.VMEM((2, ndim, groups, LANES), F32),
            pltpu.VMEM((2, n, ndim, groups, LANES), F32),
            pltpu.VMEM((2, ndim, groups, LANES), F32),
            pltpu.VMEM((8, width), F32),
            pltpu.VMEM((8, width), F32),
            pltpu.VMEM((rows, zw), BF16),
            pltpu.VMEM((8, zw), F32),
            pltpu.VMEM((3, BLOCK, BLOCK), F32),
            pltpu.VMEM((ndim, groups, LANES), F32),
            pltpu.VMEM((ndim, groups, LANES), F32),
            pltpu.VMEM((ndim, groups, LANES), F32),
            pltpu.SemaphoreType.DMA((3,)),
            pltpu.SemaphoreType.DMA,
            pltpu.SemaphoreType.DMA((20,)),
            pltpu.SemaphoreType.DMA((7,)),
            pltpu.SemaphoreType.DMA((7,)),
            pltpu.SemaphoreType.DMA((2, n)),
            pltpu.SemaphoreType.DMA((2, n)),
            pltpu.SemaphoreType.DMA((2, 2, 6)),
            pltpu.SemaphoreType.DMA((2, 2, 6)),
        ],
        compiler_params=pltpu.CompilerParams(
            collective_id=0, has_side_effects=True, vmem_limit_bytes=VMEM_LIMIT
        ),
        name="relay",
    )(x, c, gain, omega, fgain, raw, qk, wz, w1, w2)


def reduce_kernel(
    n, nd, schedule,
    l_h, r_h, all_h, w1h, w2h, xs_h, gs_h, gxn_h, xx_h, cd_h, gp_h,
    h0, zg, misc, raw, gain,
    red_h, ig_h, sm_h, out_h,
    recvs, lv, rv, part, acc, zr1, zr2, xs, gs, gxn, xx, cd, gp, tl, tr, carry, sm, smr, smz, wzp, wzr, wzz, q_r, w_r, qt_r,
    l_sem, r_sem, e_sem, x_s, x_r, z_s, z_r, o_sem, t_s, t_r, m_s, m_r, mo_sem, a_sem, w_sem, d_s, d_r, u_s, u_r, ready,
):
    sec = lax.axis_index("section")
    seq = lax.axis_index("seq")
    dp = lax.axis_index("dp")
    steps = n.bit_length() - 1
    rows, width = gxn.shape
    block_rows = width // n
    pairs = part.shape[0] // (2 * width)
    recompute = all_h.shape[1] > 1
    tok = rows // 2
    groups = width // LANES
    ndim = q_r.shape[0]
    set_rates(raw, rows // 2, q_r, w_r, qt_r)
    bit_orders = [
        [(s + color * (steps // 2)) % max(steps, 1) for s in range(steps)] for color in range(2)
    ]
    inner = (dp > 0) & (dp < nd - 1)
    outer_peer = jnp.where(dp < nd // 2, dp - 1, dp + 1)
    middle_peer = jnp.where(dp < nd // 2, dp + 1, dp - 1)

    def at_rows(ref, index, size):
        return ref.at[pl.ds(pl.multiple_of(index * size, size), size)]

    def part_at(t, color, p=0, count=1):
        start = ((t * 2 + color) * n + p) * block_rows
        return part.at[pl.ds(pl.multiple_of(start, block_rows), count * block_rows)]

    def part_rows(s):
        return (n >> (s + 1)) * block_rows // CUTS

    def sent_at(t, color, s, i):
        size = part_rows(s)
        start = (t * 2 + color) * n * block_rows + (2 * CUTS - 1 - i) * size
        return part.at[pl.ds(pl.multiple_of(start, size), size)]

    def kept_at(t, color, s, i):
        size = part_rows(s)
        start = (t * 2 + color) * n * block_rows + (CUTS - 1 - i) * size
        return part.at[pl.ds(pl.multiple_of(start, size), size)]

    def recv_at(t, color, s, i):
        if s == 0:
            rows_at = pl.ds(pl.multiple_of((t * CUTS + i) * part_rows(0), part_rows(0)), part_rows(0))
            return recvs[0].at[rows_at, pl.ds(color * CH, CH)]
        return at_rows(recvs[s], (t * 2 + color) * CUTS + i, part_rows(s))

    piece = block_rows // CUTS
    pieces = 2 * pairs * CUTS

    def own_at(v):
        unit, i = lax.div(v, CUTS), lax.rem(v, CUTS)
        start = unit * n * block_rows + (CUTS - 1 - i) * piece
        return part.at[pl.ds(pl.multiple_of(start, piece), piece)]

    def z_at(ref, v):
        return at_rows(ref, v, piece)

    def load_r(t, color):
        at = pl.ds(pl.multiple_of((t + color * pairs) * CH, CH), CH)
        return pltpu.make_async_copy(
            r_h.at[:, at], rv.at[lax.rem(t, 2), color], r_sem.at[lax.rem(t, 2), color]
        )

    for color in range(2):
        load_r(0, color).start()

    load_l = pltpu.make_async_copy(l_h, lv, l_sem)

    @pl.when((sec == 0) | (not recompute))
    def _():
        load_l.start()

    barrier = pltpu.get_barrier_semaphore()
    for k in range(1, n):
        pl.semaphore_signal(
            barrier, inc=1, device_id={"seq": lax.rem(seq + k, n)}, device_id_type=MESH
        )

    @pl.when(dp > 0)
    def _():
        pl.semaphore_signal(barrier, inc=1, device_id={"dp": dp - 1}, device_id_type=MESH)

    @pl.when(dp < nd - 1)
    def _():
        pl.semaphore_signal(barrier, inc=1, device_id={"dp": dp + 1}, device_id_type=MESH)

    @pl.when(sec == 1)
    def _():
        pl.semaphore_signal(barrier, inc=1, device_id={"section": 0}, device_id_type=MESH)

    def block_at(color, p):
        blk = seq
        for s in range(steps):
            if (p >> (steps - 1 - s)) & 1:
                blk = flip(blk, bit_orders[color][s])
        return blk

    def xy_copy(t, color, s, i):
        return pltpu.make_async_remote_copy(
            src_ref=sent_at(t, color, s, i),
            dst_ref=recv_at(t, color, s, i),
            send_sem=x_s.at[s, color, t * CUTS + i],
            recv_sem=x_r.at[s, color, t * CUTS + i],
            device_id={"seq": flip(seq, bit_orders[color][s])},
            device_id_type=MESH,
        )

    def z_copy(k, v):
        src, dst, peer = (
            (own_at(v), zr1, middle_peer),
            (own_at(v), zr2, middle_peer),
            (z_at(zr1, v), zr2, outer_peer),
        )[k]
        return pltpu.make_async_remote_copy(
            src_ref=src, dst_ref=z_at(dst, v),
            send_sem=z_s.at[0 if k < 2 else 1, v], recv_sem=z_r.at[min(k, 1), v],
            device_id={"dp": peer}, device_id_type=MESH,
        )

    def store(ref, v):
        unit, i = lax.div(v, CUTS), lax.rem(v, CUTS)
        t, color = lax.div(unit, 2), lax.rem(unit, 2)
        rows_at = pl.ds(pl.multiple_of((CUTS - 1 - i) * piece, piece), piece)
        columns_at = pl.ds(pl.multiple_of(t * CH, CH), CH)
        return pltpu.make_async_copy(z_at(ref, v), red_h.at[color, rows_at, columns_at], o_sem.at[v])

    def launch_xy(t, color, s, i):
        @pl.when(t >= SUM_WINDOW)
        def _():
            xy_copy(t - SUM_WINDOW, color, s, i).wait_send()

        xy_copy(t, color, s, i).start()

    def launch_z(k, v):
        @pl.when(v >= WINDOW)
        def _():
            z_copy(k, v - WINDOW).wait_send()

        z_copy(k, v).start()

    def launch_next(t, color, s, i):
        if s < steps and i < CUTS // 2:
            for k in range(2):
                launch_xy(t, color, s, 2 * i + k)

    def produce(t, color, i):
        if i == 0:

            @pl.when(t + 1 < pairs)
            def _():
                load_r(t + 1, color).start()

            load_r(t, color).wait()
        slot = 2 if color else lax.div(t, pairs // 2)
        share = n // CUTS
        for p in range(n - 1 - i * share, n - 1 - (i + 1) * share, -1):
            left = lv[slot, aligned(block_at(color, p), block_rows), :]
            part_at(t, color, p)[...] = dot(left, rv[lax.rem(t, 2), color]).astype(BF16)
        launch_next(t, color, 0, i)

    def add_into(total, term):
        total[...] = total[...] + term[...]

    def token_block(what, g):
        return recvs[0].at[pl.ds(pl.multiple_of((what * n + g) * rows, rows), rows)]

    def token_copy(what, g):
        return pltpu.make_async_copy(all_h.at[what, g], token_block(what, g), a_sem.at[what, g])

    def weight_at(t, which):
        return recvs[1].at[
            pl.ds(pl.multiple_of((lax.rem(t, 2) * 2 + which) * width, width), width)
        ]

    def weight_copy(t, which):
        return pltpu.make_async_copy(
            (w1h, w2h)[which].at[:, pl.ds(pl.multiple_of(t * CH, CH), CH)], weight_at(t, which),
            w_sem.at[lax.rem(t, 2), which],
        )

    def own_rows(what, g):
        return part_at(g, what, 1)

    def hidden_at(which):
        return part_at(0, which, 2, rows // block_rows)

    def recompute_start():
        for which in range(2):
            weight_copy(0, which).start()
        for g in range(n):
            for what in range(2):
                token_copy(what, g).start()
        pltpu.make_async_copy(gp_h, gp, e_sem.at[5]).start()

    def prepare_group(g):
        for what in range(2):
            token_copy(what, g).wait()
            own = token_block(what, g)[:, aligned(seq, block_rows)]
            own_rows(what, g)[...] = own.T

    def recompute_piece(t, g):
        @pl.when(t == 0)
        def _():
            prepare_group(g)

        if g == 0:

            @pl.when(t + 1 < pairs)
            def _():
                for which in range(2):
                    load_r(t + 1, which).start()
                    weight_copy(t + 1, which).start()

            for which in range(2):
                load_r(t, which).wait()
                weight_copy(t, which).wait()
                acc[which] = dot(own_rows(which, 0)[...], rv[lax.rem(t, 2), which])
        else:
            w1c, w2c = weight_at(t, 0), weight_at(t, 1)
            pre = dot(token_block(0, g)[...], w1c[...])
            sig = jax.nn.sigmoid(pre)
            hidden_at(1)[...] = (pre * sig).astype(BF16)
            slope = sig * (1.0 + pre * (1.0 - sig))
            grad = dot(token_block(1, g)[...], w2c[...])
            hidden_at(0)[...] = (grad * slope).astype(BF16)
            for which in range(2):
                acc[which] += dot(own_rows(which, g)[...], hidden_at(which)[...])
        if g == n - 1:
            for which in range(2):
                part_at(t, which)[...] = acc[which].astype(BF16)

    def output_load(c):
        if c == 0:
            pltpu.make_async_copy(gp_h, gp, e_sem.at[5]).wait()
            gxn[...] = gp[...].astype(F32)
        load_r(c, 1).start()
        weight_copy(c, 1).start()

    def output_chunk(c):
        load_r(c, 1).wait()
        weight_copy(c, 1).wait()
        gxn[...] += dot_nt(rv[c % 2, 1], weight_at(c, 1)[...])
        if c + 1 < pairs:
            output_load(c + 1)
        else:
            pl.semaphore_wait(ready, 1)
            own_output().start()
            give_output().start()

    def absorb(t, color, i, s):
        xy_copy(t, color, s, i).wait_recv()
        add_into(kept_at(t, color, s, i), recv_at(t, color, s, i))
        launch_next(t, color, s + 1, i)

    def z_first(v):
        @pl.when(jnp.logical_not(inner))
        def _():
            launch_z(0, v)

    def z_second(v):
        @pl.when(inner)
        def _():
            z_copy(0, v).wait_recv()
            add_into(own_at(v), z_at(zr1, v))
            launch_z(1, v)

    def z_third(v):
        @pl.when(inner)
        def _():
            z_copy(1, v).wait_recv()
            z_at(zr1, v)[...] = own_at(v)[...] + z_at(zr2, v)[...]
            launch_z(2, v)
            store(zr1, v).start()

    def z_last(v):
        @pl.when(jnp.logical_not(inner))
        def _():
            z_copy(2, v).wait_recv()
            store(zr2, v).start()

    z_stages = (z_first, z_second, z_third, z_last)

    def state_copy(k, way):
        return pltpu.make_async_remote_copy(
            src_ref=tl.at[way], dst_ref=tr.at[way, k],
            send_sem=t_s.at[way, k], recv_sem=t_r.at[way, k],
            device_id={"seq": seq + k if way == 0 else seq - k}, device_id_type=MESH,
        )

    def loads():
        return [
            pltpu.make_async_copy(src, dst, e_sem.at[k])
            for k, (src, dst) in enumerate(
                ((xs_h, xs), (gs_h, gs), (gxn_h, gxn), (xx_h, xx), (cd_h, cd), (gp_h, gp))
            )
        ]

    def channel_rows(t):
        return pl.ds(pl.multiple_of(t * groups, groups), groups)

    zeros = jnp.zeros((groups, LANES), F32)

    def ema_ends():
        for cp in loads()[:2]:
            cp.wait()
        q = [q_r[j] for j in range(ndim)]
        half = ndim // 2
        for m in range(2):
            for part_of in range(2):
                js = range(part_of * half, (part_of + 1) * half)

                def forth(i, state):
                    h, d = state
                    for u in range(8):
                        x = xs[channel_rows(m * tok + i * 8 + u), :]
                        d = tuple(q[j] * d[k] + h[k] for k, j in enumerate(js))
                        h = tuple(q[j] * h[k] + x for k, j in enumerate(js))
                    return h, d

                _, d = lax.fori_loop(
                    0, tok // 8, forth,
                    (tuple(h0[m, j] for j in js), tuple(zeros for _ in js)),
                )
                for k, j in enumerate(js):
                    tl[0, m, j] = d[k]

            def back(i, a):
                for u in range(8):
                    g = gs[channel_rows(m * tok + tok - 1 - (i * 8 + u)), :]
                    a = tuple(q[j] * a[j] + g for j in range(ndim))
                return a

            a = lax.fori_loop(0, tok // 8, back, tuple(zeros for _ in range(ndim)))
            for j in range(ndim):
                tl[1, m, j] = a[j]
        for way in range(2):
            for k in range(1, n):
                has = (seq + k < n) if way == 0 else (seq - k >= 0)
                gets = (seq - k >= 0) if way == 0 else (seq + k < n)

                @pl.when(has)
                def _():
                    state_copy(k, way).start()

                @pl.when(jnp.logical_not(gets))
                def _():
                    tr[way, k] = jnp.zeros(tr.shape[2:], F32)

    def ema_carries():
        for way in range(2):
            for k in range(1, n):
                gets = (seq - k >= 0) if way == 0 else (seq + k < n)

                @pl.when(gets)
                def _():
                    state_copy(k, way).wait_recv()

            for m in range(2):
                for j in range(ndim):
                    state = zeros
                    for k in range(n - 1, 0, -1):
                        state = state * qt_r[j] + tr[way, k, m, j]
                    carry[way, m, j] = state

    def ema_sums():
        half = ndim // 2
        for part_of in range(2):
            js = range(part_of * half, (part_of + 1) * half)
            q = [q_r[j] for j in js]
            total = tuple(zeros for _ in range(2 * half))
            for m in range(2):

                def forth(i, state):
                    h, d, s0, s1 = state
                    for u in range(4):
                        at = channel_rows(m * tok + i * 4 + u)
                        x, g = xs[at, :], gs[at, :]
                        d = tuple(q[k] * d[k] + h[k] for k in range(half))
                        h = tuple(q[k] * h[k] + x for k in range(half))
                        s0 = tuple(s0[k] + g * h[k] for k in range(half))
                        s1 = tuple(s1[k] + g * d[k] for k in range(half))
                    return h, d, s0, s1

                _, _, s0, s1 = lax.fori_loop(
                    0, tok // 4, forth,
                    (
                        tuple(h0[m, j] for j in js),
                        tuple(carry[0, m, j] for j in js),
                        total[:half],
                        total[half:],
                    ),
                )
                total = s0 + s1
            for k, j in enumerate(js):
                sm[pl.ds(width + j * groups, groups), :] = total[k]
                sm[pl.ds(width + (ndim + j) * groups, groups), :] = total[half + k]

    def ema_adjoint():
        q = [q_r[j] for j in range(ndim)]
        w = [w_r[j] for j in range(ndim)]
        for m in range(2):

            def back(i, a):
                for u in range(8):
                    at = channel_rows(m * tok + tok - 1 - (i * 8 + u))
                    g = gs[at, :]
                    a = tuple(q[j] * a[j] + g for j in range(ndim))
                    xs[at, :] = add_all(w[j] * a[j] for j in range(ndim))
                return a

            lax.fori_loop(0, tok // 8, back, tuple(carry[1, m, j] for j in range(ndim)))

    base = width + 2 * ndim * groups

    def own_grad():
        return pltpu.make_async_copy(gxn.at[pl.ds(0, tok)], ig_h, mo_sem.at[0])

    def to_sibling(src, dst, k):
        return pltpu.make_async_remote_copy(
            src_ref=src, dst_ref=dst, send_sem=d_s.at[k], recv_sem=d_r.at[k],
            device_id={"section": 1 - sec}, device_id_type=MESH,
        )

    def give_grad():
        return to_sibling(gxn.at[pl.ds(tok, tok)], ig_h, 0)

    def give_small():
        return to_sibling(sm, sm_h, 1)

    def give_output():
        return to_sibling(gxn.at[pl.ds(0, tok)], out_h, 2)

    def own_output():
        return pltpu.make_async_copy(gxn.at[pl.ds(tok, tok)], out_h, mo_sem.at[0])

    def input_grads():
        for cp in loads()[2:]:
            cp.wait()
        sm[pl.ds(base, 3 * groups), :] = misc[0 : 3 * groups, :]
        g = gain[...]

        def tile(i, total):
            at = aligned(i, TILE_SMALL)
            unit, factor = normed_rows(xx[at, :].astype(F32))
            grad = gxn[at, :] + from_channel_rows(xs, i * TILE_SMALL, TILE_SMALL, groups)
            gxn[at, :] = norm_back(grad, g, unit, factor) + gp[at, :].astype(F32) * cd[
                at, :
            ].astype(F32)
            return total + jnp.sum(grad * unit, axis=0, keepdims=True)

        total = lax.fori_loop(0, rows // TILE_SMALL, tile, jnp.zeros((1, width), F32))
        for j, piece in enumerate(rows_of(total)):
            sm[base + 3 * groups + j : base + 3 * groups + j + 1, :] = piece
        own_grad().start()
        give_grad().start()

    late = pl.ds(width, sm.shape[0] - width)

    def small_copy(k):
        return pltpu.make_async_remote_copy(
            src_ref=sm.at[late], dst_ref=smr.at[k], send_sem=m_s.at[k], recv_sem=m_r.at[k],
            device_id={"seq": flip(seq, k)}, device_id_type=MESH,
        )

    def small_z(k):
        dst, peer = ((0, middle_peer), (1, middle_peer), (1, outer_peer))[k]
        return pltpu.make_async_remote_copy(
            src_ref=sm.at[late], dst_ref=smz.at[dst],
            send_sem=m_s.at[steps + (0 if k < 2 else 1)],
            recv_sem=m_r.at[steps + min(k, 1)],
            device_id={"dp": peer}, device_id_type=MESH,
        )

    def small_add(k):
        small_copy(k).wait()
        sm[late, :] += smr[k]
        if k + 1 < steps:
            small_copy(k + 1).start()

    def small_z_first():
        @pl.when(jnp.logical_not(inner))
        def _():
            small_z(0).start()

    def small_z_second():
        @pl.when(inner)
        def _():
            small_z(0).wait_recv()
            sm[late, :] += smz[0]
            small_z(1).start()

    def small_z_third():
        @pl.when(inner)
        def _():
            small_z(1).wait()
            sm[late, :] += smz[1]
            small_z(2).start()

    def small_z_last():
        @pl.when(jnp.logical_not(inner))
        def _():
            small_z(0).wait_send()
            small_z(2).wait_recv()
            sm[late, :] = smz[1]

    def wz_rows(p, count=1):
        return pl.ds(p * block_rows, count * block_rows)

    def wz_start():
        for p in range(n):
            wzp[wz_rows(p), :] = zg[aligned(block_at(0, p), block_rows), :]
        if steps:
            wz_copy(0).start()

    def wz_copy(s):
        half = n >> (s + 1)
        return pltpu.make_async_remote_copy(
            src_ref=wzp.at[wz_rows(half, half)], dst_ref=wzr.at[wz_rows(half, half)],
            send_sem=u_s.at[s], recv_sem=u_r.at[s],
            device_id={"seq": flip(seq, bit_orders[0][s])}, device_id_type=MESH,
        )

    def wz_add(s):
        half = n >> (s + 1)
        wz_copy(s).wait()
        wzp[wz_rows(0, half), :] += wzr[wz_rows(half, half), :]
        if s + 1 < steps:
            wz_copy(s + 1).start()

    def wz_z(k):
        dst, peer = ((0, middle_peer), (1, middle_peer), (1, outer_peer))[k]
        return pltpu.make_async_remote_copy(
            src_ref=wzp.at[wz_rows(0)], dst_ref=wzz.at[dst],
            send_sem=u_s.at[2 * steps + (0 if k < 2 else 1)],
            recv_sem=u_r.at[2 * steps + min(k, 1)],
            device_id={"dp": peer}, device_id_type=MESH,
        )

    def wz_z_first():
        @pl.when(jnp.logical_not(inner))
        def _():
            wz_z(0).start()

    def wz_z_second():
        @pl.when(inner)
        def _():
            wz_z(0).wait_recv()
            wzp[wz_rows(0), :] += wzz[0]
            wz_z(1).start()

    def wz_z_third():
        @pl.when(inner)
        def _():
            wz_z(1).wait()
            wzp[wz_rows(0), :] += wzz[1]
            wz_z(2).start()

    def wz_z_last():
        @pl.when(jnp.logical_not(inner))
        def _():
            wz_z(0).wait_send()
            wz_z(2).wait_recv()
            wzp[wz_rows(0), :] = wzz[1]

        if steps:
            wz_back(steps - 1).start()

    def wz_back(s):
        half = n >> (s + 1)
        return pltpu.make_async_remote_copy(
            src_ref=wzp.at[wz_rows(0, half)], dst_ref=wzp.at[wz_rows(half, half)],
            send_sem=u_s.at[steps + s], recv_sem=u_r.at[steps + s],
            device_id={"seq": flip(seq, bit_orders[0][s])}, device_id_type=MESH,
        )

    def wz_spread(s):
        wz_back(s).wait()
        if s:
            wz_back(s - 1).start()

    def small_end():
        for p in range(n):
            sm[aligned(block_at(0, p), block_rows), :] = wzp[wz_rows(p), :]
        own_small().start()
        give_small().start()

    def own_small():
        return pltpu.make_async_copy(sm, sm_h, mo_sem.at[1])

    sum_lag, z_lag, z_lag_1, mega_at, wz_at, small_gap, wz_gap = schedule
    mega_work = [
        lambda: [cp.start() for cp in loads()], ema_ends, ema_carries, ema_sums, ema_adjoint, input_grads
    ]
    mega_ticks = list(mega_at)
    if steps:
        mega_work.append(lambda: small_copy(0).start())
        mega_ticks.append(mega_ticks[-1])
    for stage in [functools.partial(small_add, k) for k in range(steps)] + [
        small_z_first, small_z_second, small_z_third, small_z_last
    ]:
        mega_work.append(stage)
        mega_ticks.append(mega_ticks[-1] + small_gap * (stage != small_z_first))
    last = mega_ticks[-1]
    at = wz_at
    for stage in (
        [wz_start]
        + [functools.partial(wz_add, s) for s in range(steps)]
        + [wz_z_first, wz_z_second, wz_z_third, wz_z_last]
        + [functools.partial(wz_spread, s) for s in range(steps - 1, -1, -1)]
    ):
        mega_work.append(stage)
        mega_ticks.append(at)
        at += wz_gap * (stage not in (wz_z_first,))
    mega_work.append(small_end)
    mega_ticks.append(max(last, at))

    ticks = 2 * CUTS

    def z_work(pair, tick, lags):
        for lag, stage in zip(lags, z_stages):
            v = ticks * pair + tick - lag

            @pl.when((v >= 0) & (v < pieces))
            def _():
                stage(v)

    sum_stages = [(0, produce)]
    for s in range(steps):
        sum_stages.append(((s + 1) * sum_lag, functools.partial(absorb, s=s)))
    sum_z = [steps * sum_lag + lag for lag in z_lag]
    sum_pairs = pairs + -(-sum_z[-1] // ticks)

    def sum_tick(pair, tick):
        for lag, stage in sum_stages:
            unit, i = divmod(tick - lag, CUTS)
            t = pair + unit // 2

            @pl.when((t >= 0) & (t < pairs))
            def _():
                stage(t, unit % 2, i)

        z_work(pair, tick, sum_z)

    def sum_pair(pair):
        for tick in range(ticks):
            sum_tick(pair, tick)

    def mega_pair(pair):
        for tick in range(ticks):
            sum_tick(pair, tick)
            for when in sorted(set(mega_ticks)):
                if when % ticks == tick:
                    work = [f for f, m in zip(mega_work, mega_ticks) if m == when]

                    @pl.when(pair == when // ticks)
                    def _():
                        for f in work:
                            f()

    recompute_z = [ticks + lag for lag in z_lag_1]
    recompute_pairs = pairs + -(-recompute_z[-1] // ticks)

    def recompute_pair(pair):
        for g in range(n):

            @pl.when(pair < pairs)
            def _():
                recompute_piece(pair, g)

            for tick in range(g * ticks // n, (g + 1) * ticks // n):
                z_work(pair, tick, recompute_z)

            if g == n - 1:

                @pl.when(pair == pairs - 1)
                def _():
                    output_load(0)

            for c in range(pairs):
                if c % n == g:

                    @pl.when(pair == pairs + c // n)
                    def _():
                        output_chunk(c)

    def drain(summed):
        def sent(c):
            v = pieces - WINDOW + c

            @pl.when(inner)
            def _():
                z_copy(1, v).wait_send()
                z_copy(2, v).wait_send()

            @pl.when(jnp.logical_not(inner))
            def _():
                z_copy(0, v).wait_send()

        if summed:
            for color in range(2):
                for s in range(steps):
                    for i in range(CUTS):
                        for t in range(pairs - SUM_WINDOW, pairs):
                            xy_copy(t, color, s, i).wait_send()
        loop(WINDOW, sent)
        loop(pieces, lambda v: store(zr1, v).wait())

    if recompute:

        @pl.when(sec == 1)
        def _():
            recompute_start()

    pl.semaphore_wait(barrier, n - 1 + jnp.where(inner, 2, 1) + (1 - sec))

    @pl.when(sec == 0)
    def _():
        pl.semaphore_signal(ready, inc=1, device_id={"section": 1}, device_id_type=MESH)

    @pl.when(sec == 0)
    def _():
        load_l.wait()
        loop(max(sum_pairs, max(mega_ticks) // ticks + 1), mega_pair)
        drain(True)

    @pl.when(sec == 1)
    def _():
        if recompute:
            loop(max(recompute_pairs, pairs + (pairs + n - 1) // n), recompute_pair)
        else:
            load_l.wait()
            loop(sum_pairs, sum_pair)
        drain(not recompute)

    @pl.when(sec == 0)
    def _():
        for way in range(2):
            for k in range(1, n):
                has = (seq + k < n) if way == 0 else (seq - k >= 0)

                @pl.when(has)
                def _():
                    state_copy(k, way).wait_send()

        @pl.when(inner)
        def _():
            small_z(2).wait_send()
            wz_z(2).wait_send()

        own_small().wait()
        give_small().wait_send()
        if recompute:
            give_output().wait_recv()

        own_grad().wait()
        give_grad().wait_send()

    @pl.when(sec == 1)
    def _():
        if recompute:
            own_output().wait()
            give_output().wait_send()
        else:
            pl.semaphore_wait(ready, 1)
        give_grad().wait_recv()
        give_small().wait_recv()


SCHEDULE = (8, (0, 3, 6, 9), (0, 3, 6, 9), (8, 12, 16, 18, 20, 22), 2, 2, 4)


def reduce_grads(n, nd, l, r, both, w1, w2, xs, gs, gxn, xx, cd, gp, h0, zg, misc, raw, gain):
    rows, width = gxn.shape
    groups = width // LANES
    ndim = raw.shape[1]
    ff = r.shape[1] // 2
    pairs = ff // CH
    block_rows = width // n
    steps = n.bit_length() - 1
    small_rows = width + 2 * ndim * groups + 4 * groups
    any_spec = pl.BlockSpec(memory_space=pl.ANY)
    vmem = pl.BlockSpec(memory_space=pltpu.VMEM)

    def kernel(*refs):
        fixed = refs[: 16 + 4]
        rest = list(refs[16 + 4 :])
        recvs = rest[:steps]
        reduce_kernel(n, nd, SCHEDULE, *fixed, recvs, *rest[steps:])

    return pl.pallas_call(
        kernel,
        out_shape=[
            jax.ShapeDtypeStruct((2, block_rows, ff), BF16),
            jax.ShapeDtypeStruct((rows // 2, width), F32),
            jax.ShapeDtypeStruct((small_rows, LANES), F32),
            jax.ShapeDtypeStruct((rows // 2, width), F32),
        ],
        in_specs=[any_spec] * 11 + [vmem] * 5,
        out_specs=[any_spec] * 4,
        scratch_shapes=[
            pltpu.VMEM(
                (pairs * (n >> (s + 1)) * block_rows * (1 if s == 0 else 2), CH * (2 if s == 0 else 1)),
                BF16,
            )
            for s in range(steps)
        ]
        + [
            pltpu.VMEM((3, width, rows), BF16),
            pltpu.VMEM((2, 2, rows, CH), BF16),
            pltpu.VMEM((pairs * 2 * width, CH), BF16),
            pltpu.VMEM((2, block_rows, CH), F32),
            pltpu.VMEM((pairs * 2 * block_rows, CH), BF16),
            pltpu.VMEM((pairs * 2 * block_rows, CH), BF16),
            pltpu.VMEM((rows * groups, LANES), F32),
            pltpu.VMEM((rows * groups, LANES), F32),
            pltpu.VMEM((rows, width), F32),
            pltpu.VMEM((rows, width), BF16),
            pltpu.VMEM((rows, width), BF16),
            pltpu.VMEM((rows, width), BF16),
            pltpu.VMEM((2, 2, ndim, groups, LANES), F32),
            pltpu.VMEM((2, n, 2, ndim, groups, LANES), F32),
            pltpu.VMEM((2, 2, ndim, groups, LANES), F32),
            pltpu.VMEM((small_rows, LANES), F32),
            pltpu.VMEM((max(steps, 1), small_rows - width, LANES), F32),
            pltpu.VMEM((2, small_rows - width, LANES), F32),
            pltpu.VMEM((width, LANES), F32),
            pltpu.VMEM((width, LANES), F32),
            pltpu.VMEM((2, block_rows, LANES), F32),
            pltpu.VMEM((ndim, groups, LANES), F32),
            pltpu.VMEM((ndim, groups, LANES), F32),
            pltpu.VMEM((ndim, groups, LANES), F32),
            pltpu.SemaphoreType.DMA,
            pltpu.SemaphoreType.DMA((2, 2)),
            pltpu.SemaphoreType.DMA((6,)),
            pltpu.SemaphoreType.DMA((steps, 2, pairs * CUTS)),
            pltpu.SemaphoreType.DMA((steps, 2, pairs * CUTS)),
            pltpu.SemaphoreType.DMA((2, 2 * pairs * CUTS)),
            pltpu.SemaphoreType.DMA((2, 2 * pairs * CUTS)),
            pltpu.SemaphoreType.DMA((2 * pairs * CUTS,)),
            pltpu.SemaphoreType.DMA((2, n)),
            pltpu.SemaphoreType.DMA((2, n)),
            pltpu.SemaphoreType.DMA((steps + 2,)),
            pltpu.SemaphoreType.DMA((steps + 2,)),
            pltpu.SemaphoreType.DMA((2,)),
            pltpu.SemaphoreType.DMA((2, n)),
            pltpu.SemaphoreType.DMA((2, 2)),
            pltpu.SemaphoreType.DMA((3,)),
            pltpu.SemaphoreType.DMA((3,)),
            pltpu.SemaphoreType.DMA((2 * steps + 2,)),
            pltpu.SemaphoreType.DMA((2 * steps + 2,)),
            pltpu.SemaphoreType.REGULAR,
        ],
        compiler_params=pltpu.CompilerParams(
            collective_id=1, has_side_effects=True, vmem_limit_bytes=VMEM_LIMIT
        ),
        name="reduce_grads",
    )(l, r, both, w1, w2, xs, gs, gxn, xx, cd, gp, h0, zg, misc, raw, gain)


def finish_kernel(
    coeff, steps, seq_ref, red, w1, w2, sm_h, raw, gain, fgain, wz, qk, out_h, ig_h,
    first, second, z_o, qk_o, ema_o, norm_o, omega_o, ffn_o, out_o, ig_o,
    sm, sems,
):
    width, groups = wz.shape[0], gain.shape[1] // LANES
    ndim = raw.shape[1]
    load = pltpu.make_async_copy(sm_h, sm, sems)

    @pl.when(pl.program_id(0) == 0)
    def _():
        load.start()

    out_o[...] = out_h[...]
    ig_o[...] = ig_h[...]

    first[...] = red[0].astype(F32) + coeff * w1[...].astype(F32)
    second[...] = red[1].astype(F32) + coeff * w2[...].astype(F32)

    @pl.when(pl.program_id(0) == min(1, steps - 1))
    def _():
        load.wait()
        z_o[...] = sm[0:width, :] + coeff * wz[...].astype(F32)
        base = width + 2 * ndim * groups
        for j in range(groups):
            at = slice(j * LANES, (j + 1) * LANES)
            omega_o[:, at] = sm[base + j : base + j + 1, :]
            ffn_o[:, at] = sm[base + groups + j : base + groups + j + 1, :] + coeff * fgain[:, at]
            norm_o[:, at] = (
                sm[base + 3 * groups + j : base + 3 * groups + j + 1, :] + coeff * gain[:, at]
            )
        qk_o[...] = sm[base + 2 * groups : base + 2 * groups + 4, :] + coeff * qk[...]
        for j in range(ndim):
            sum_0 = sm[width + j * groups : width + (j + 1) * groups, :]
            sum_1 = sm[width + (ndim + j) * groups : width + (ndim + j + 1) * groups, :]
            alpha, damp = jax.nn.sigmoid(raw[0, j]), jax.nn.sigmoid(raw[1, j])
            inject = alpha * raw[2, j]
            inject_grad = raw[3, j] * sum_0
            decay_grad = raw[3, j] * inject * sum_1
            ema_o[0, j] = (inject_grad * raw[2, j] - decay_grad * damp) * alpha * (1.0 - alpha)
            ema_o[1, j] = -decay_grad * alpha * damp * (1.0 - damp)
            ema_o[2, j] = inject_grad * alpha
            ema_o[3, j] = inject * sum_0


def finish(coeff, seq, red, w1, w2, small, raw, gain, fgain, wz, qk, out, grad):
    block_rows, ff = red.shape[1:]
    any_spec = pl.BlockSpec(memory_space=pl.ANY)
    vmem = pl.BlockSpec(memory_space=pltpu.VMEM)
    tiles = block_rows // TILE_SMALL
    own = pl.BlockSpec((TILE_SMALL, ff), lambda j, s: (s[0] * tiles + j, 0))
    share = pl.BlockSpec((TILE_SMALL, ff), lambda j, s: (j, 0))
    rows = pl.BlockSpec((out.shape[0] // tiles, out.shape[1]), lambda j, s: (j, 0))

    def shape(dims):
        return jax.ShapeDtypeStruct(dims, F32)

    return pl.pallas_call(
        functools.partial(finish_kernel, coeff, tiles),
        grid_spec=pltpu.PrefetchScalarGridSpec(
            num_scalar_prefetch=1,
            grid=(tiles,),
            in_specs=[pl.BlockSpec((2, TILE_SMALL, ff), lambda j, s: (0, j, 0)), own, own]
            + [any_spec]
            + [vmem] * 5
            + [rows] * 2,
            out_specs=[share, share] + [vmem] * 6 + [rows] * 2,
            scratch_shapes=[
                pltpu.VMEM(small.shape, F32),
                pltpu.SemaphoreType.DMA,
            ],
        ),
        out_shape=[
            shape((block_rows, ff)),
            shape((block_rows, ff)),
            shape(wz.shape),
            shape(qk.shape),
            shape(raw.shape),
            shape(gain.shape),
            shape(gain.shape),
            shape(gain.shape),
            shape(out.shape),
            shape(grad.shape),
        ],
        compiler_params=pltpu.CompilerParams(vmem_limit_bytes=VMEM_LIMIT),
        name="finish",
    )(seq, red, w1, w2, small, raw, gain, fgain, wz, qk, out, grad)


def body(
    inputs, cotangent, norm_gain, first_pack, second_pack, w_z, qk_affine, ema_params, omega, ffn_gain
):
    n = lax.axis_size("seq")
    nd = lax.axis_size("dp")
    tok, width = inputs.shape[2:]
    groups = width // LANES
    ndim = ema_params.shape[2]

    raw = jnp.swapaxes(ema_params, 1, 2).reshape(4, ndim, groups, LANES)

    def line(v):
        return v.reshape(1, width)

    l, r, xs, gs, gxn, xx, cd, gp, h0, block_output, both, zg, misc = relay(
        n, inputs[0, 0], cotangent[0, 0], line(norm_gain), line(omega), line(ffn_gain),
        raw, qk_affine, w_z, first_pack[0], second_pack[0],
    )
    red, input_grad, small, late_output = reduce_grads(
        n, nd, l, r, both, first_pack[0], second_pack[0], xs, gs, gxn, xx, cd, gp, h0, zg, misc,
        raw, line(norm_gain),
    )

    if n == RECOMPUTE_OVER:
        block_output = late_output
    coeff = DECAY * 2 * nd * n * tok
    grads = finish(
        coeff, lax.axis_index("seq").reshape(1), red, first_pack[0], second_pack[0],
        small, raw, line(norm_gain), line(ffn_gain), w_z, qk_affine, block_output, input_grad,
    )
    first, second, z_grad, qk_grad, ema_grad, norm_grad, omega_grad, ffn_grad, output, in_grad = grads
    return (
        output[None, None],
        in_grad[None, None],
        norm_grad.reshape(width),
        first[None],
        second[None],
        z_grad,
        qk_grad,
        jnp.swapaxes(ema_grad.reshape(4, ndim, width), 1, 2),
        omega_grad.reshape(width),
        ffn_grad.reshape(width),
    )


def solution(mesh):
    rows = P("section", "dp", "seq", None)
    packs = P("section", None, None)
    shares = P("section", "seq", None)
    return jax.shard_map(
        body,
        mesh=mesh,
        in_specs=(rows, rows, P(), packs, packs, P(), P(), P(), P(), P()),
        out_specs=(rows, rows, P(), shares, shares, P(), P(), P(), P(), P()),
        check_vma=False,
    )
```
